512 devices in a mesh: row: 32 (over x_lo, y, core), col: 16 (over z, x_hi).
Axes of the slice: x: 4 (x_hi: 2, x_lo: 2; x = x_hi * 2 + x_lo), y: 8, z: 8, core: 2. Of those that a mesh axis runs over, the one named last changes fastest.
Arguments:
- biomass: bfloat16 [1024, 512, 256], P('row', 'col'), may hold values from 0 to 2
- block_stand: int32 [128, 64], P('row', 'col'), may hold values from 0 to 15
- stand_slot: int32 [32, 16, 16], P('row', 'col'), may hold values from 0 to 8
- tile_list: int32 [32, 16, 8], P('row', 'col'), may hold values from 0 to 63, as said below
- harvest_ops: bfloat16 [64, 256, 256], P('col')
- transition: bfloat16 [256, 256], replicated, may hold values from -0.5 to 0.5
- pattern: int32 [32, 32], replicated, may hold values 0 or 1
- fecundity: bfloat16 [256, 256], replicated, may hold values from -0.375 to 0.375
- radius: int32 [256], replicated, may hold values from 1 to 4, as said below
Outputs:
- final_biomass: bfloat16 [1024, 512, 256], P('row', 'col')
The draws below stay inside these ranges and needn't reach their ends.
Inputs may be any that keep to these rules, and one draw needn't show every extreme that they name: `tile_list`: each tile lists 8 different prescriptions, held by 8 different indices of col: prescription p is held by index p // 4. `stand_slot`: slot 8 marks a stand left unharvested; a slot k below 8 names entry k of the tile's list. Some cohort has radius 4.
All inputs are finite; a program needn't handle non-finite values.
Results may differ from the reference program's by a relative error of at most 0.0073.
Values may be sent and summed in bfloat16 or wider, within the bound.
No kernel may reach another device: no remote copies, remote signals or barrier semaphores. Data moves between devices by JAX's collectives and lax.ppermute only.
A program may use at most 128 MiB of HBM per device.

```python
import jax
import jax.numpy as jnp
from jax import lax

CX = 32
CY = 32
C = 256
TB = 8
RMAX = 4
BX = 8
BY = 8
S = 16
PD = 4
STEPS = 2
K = 8
NX = 1024
NY = 512
P_SIZE = 64
N_ROW = 32
N_COL = 16


def draw_tile_list(key, part):
    key = jax.random.fold_in(key, 11)
    keys = jax.random.split(key, N_ROW * N_COL)

    def holders(single):
        return jax.random.permutation(single, N_COL)[:K]
    owners = jax.vmap(holders)(keys)
    within = jax.random.randint(jax.random.fold_in(key, 1), (N_ROW * N_COL, K), 0, PD)
    return (owners * PD + within).reshape(N_ROW, N_COL, K).astype(jnp.int32)


def draw_radius(key, part):
    key = jax.random.fold_in(key, 12)
    values = jax.random.randint(key, (C,), 1, RMAX + 1)
    place = jax.random.randint(jax.random.fold_in(key, 1), (), 0, C)
    return jnp.where(jnp.arange(C) == place, RMAX, values).astype(jnp.int32)


def draw_harvest_ops(key, part):
    key = jax.random.fold_in(key, 13)
    first, second = jax.random.split(key)
    diagonal = jax.random.uniform(first, (P_SIZE, C), jnp.float32, 0.3, 0.9)
    spread = jax.random.normal(second, (P_SIZE, C, C), jnp.float32) * (0.5 / C ** 0.5)
    identity_mat = (jnp.arange(C)[:, None] == jnp.arange(C)[None, :]).astype(jnp.float32)
    return (spread * (1.0 - identity_mat) + diagonal[:, :, None] * identity_mat).astype(jnp.bfloat16)


def place_ends(values, key, low, high):
    longest = values.shape.index(max(values.shape))
    spots = []
    for shift in (0, 1):
        where = [jax.random.randint(jax.random.fold_in(key, axis), (), 0, length) for axis, length in enumerate(values.shape)]
        where[longest] = (where[longest] + shift) % values.shape[longest]
        spots.append(tuple(where))
    return values.at[spots[0]].set(low).at[spots[1]].set(high)


def steps_of(rng, shape, shards, low, high):
    level, own = 1.0, jax.random.fold_in(rng, 6)
    for axis_at, blocks in shards:
        steps = jnp.exp(jax.random.uniform(jax.random.fold_in(own, axis_at), (blocks,), jnp.float32, low / len(shards), high / len(shards)))
        level = level * jnp.repeat(steps, shape[axis_at] // blocks).reshape([-1 if axis == axis_at else 1 for axis in range(len(shape))])
    return level


def normal_values(rng, dims, scale, most, kind=jnp.bfloat16):
    entries = scale * jax.random.normal(rng, dims, jnp.float32)
    return jnp.clip(entries, min=-most, max=most).astype(kind)


def setup_inputs(seed: int = 0) -> dict:
    seeds = jax.random.split(jax.random.key(seed), 10)
    return {
        "biomass": jnp.clip(2.0 * jax.random.uniform(seeds[0], (NX, NY, C), jnp.float32) ** steps_of(seeds[0], (NX, NY, C), ((0, 32), (1, 16)), -0.2, 0.2), 0.0, 2.0).astype(jnp.bfloat16),
        "block_stand": place_ends(jax.random.randint(seeds[1], (NX // BX, NY // BY), 0, S), jax.random.fold_in(seeds[1], 1), 0, S - 1).astype(jnp.int32),
        "stand_slot": place_ends(jax.random.randint(seeds[2], (N_ROW, N_COL, S), 0, K + 1), jax.random.fold_in(seeds[2], 1), 0, K).astype(jnp.int32),
        "tile_list": draw_tile_list(jax.random.fold_in(seeds[9], 71), 0),
        "harvest_ops": draw_harvest_ops(jax.random.fold_in(seeds[9], 71), 0),
        "transition": normal_values(seeds[5], (C, C), (C // 2) ** -0.5, 0.5),
        "pattern": place_ends((jax.random.randint(seeds[6], (C // TB, C // TB), 0, 2) < 1).astype(jnp.int32), jax.random.fold_in(seeds[6], 1), 0, 1),
        "fecundity": normal_values(seeds[7], (C, C), C ** -0.5, 0.375),
        "radius": draw_radius(jax.random.fold_in(seeds[9], 71), 0),
    }


def kernel_weights(radius):
    offsets = jnp.arange(-RMAX, RMAX + 1).astype(jnp.float32)
    dist_sq = offsets[:, None] ** 2 + offsets[None, :] ** 2
    reach = (radius.astype(jnp.float32) ** 2)[:, None, None]
    values = jnp.exp(-dist_sq[None] / (2.0 * reach)) * (dist_sq[None] <= reach).astype(jnp.float32)
    return values / lax.optimization_barrier(jnp.sum(values, axis=(1, 2), keepdims=True))

def reference(biomass, block_stand, stand_slot, tile_list, harvest_ops, transition, pattern, fecundity, radius):
    kernel = kernel_weights(radius)
    block_mask = jnp.repeat(jnp.repeat(pattern, TB, 0), TB, 1).astype(jnp.float32)
    moves = (transition.astype(jnp.float32) * block_mask).astype(jnp.bfloat16)
    tile_rows = (jnp.arange(NX // BX) // (CX // BX)).astype(jnp.int32)
    tile_cols = (jnp.arange(NY // BY) // (CY // BY)).astype(jnp.int32)
    block_slot = stand_slot[tile_rows[:, None], tile_cols[None, :], block_stand]
    cell_slot = jnp.repeat(jnp.repeat(block_slot, BX, 0), BY, 1)
    operators = harvest_ops[tile_list]
    state = biomass
    width = 2 * RMAX + 1
    for period in range(STEPS):
        padded = jnp.pad(state, ((RMAX, RMAX), (RMAX, RMAX), (0, 0)))

        def strip_rows(index):
            rows = lax.dynamic_slice_in_dim(padded, index * CX, CX + 2 * RMAX, 0)
            seedfall = jnp.zeros((CX, NY, C), jnp.float32)
            for row_off in range(width):
                for col_off in range(width):
                    seedfall = seedfall + kernel[:, row_off, col_off] * rows[row_off:row_off + CX, col_off:col_off + NY].astype(jnp.float32)
            seed_bf = seedfall.astype(jnp.bfloat16)
            current = lax.dynamic_slice_in_dim(state, index * CX, CX, 0)
            middle = (current.astype(jnp.float32) + jnp.dot(seed_bf, fecundity, preferred_element_type=jnp.float32)).astype(jnp.bfloat16)
            shifted = jnp.dot(middle, moves, preferred_element_type=jnp.float32)
            grown = (shifted * lax.rsqrt(1.0 + lax.optimization_barrier(jnp.mean(shifted * shifted, axis=-1, keepdims=True)))).astype(jnp.bfloat16)
            slots = lax.dynamic_slice_in_dim(cell_slot, index * CX, CX, 0).reshape(CX, N_COL, CY, 1)
            tile_ops = operators[index].astype(jnp.float32)
            grown_tiles = grown.reshape(CX, N_COL, CY, C).astype(jnp.float32)
            result = jnp.where(slots == K, grown_tiles, 0.0)
            for slot in range(K):
                product = jnp.einsum('xjyc,jcd->xjyd', grown_tiles, tile_ops[:, slot])
                result = result + jnp.where(slots == slot, product, 0.0)
            return result.reshape(CX, NY, C).astype(jnp.bfloat16)
        state = lax.map(strip_rows, jnp.arange(N_ROW).astype(jnp.int32)).reshape(NX, NY, C)
    return state
```

```python
import math

import jax
import jax.numpy as jnp
from jax import lax
from jax.sharding import PartitionSpec as P

TB = 8
RMAX = 4
BX = 8
BY = 8
STEPS = 2


def padded_2(cells, sides, width):
    for axis, dim in sides:
        count = math.prod(lax.axis_size(name) for name in axis)
        ends = count - 1
        head = lax.slice_in_dim(cells, 0, width, axis=dim)
        tail = lax.slice_in_dim(cells, cells.shape[dim] - width, cells.shape[dim], axis=dim)
        cells = jnp.concatenate(
            [
                lax.ppermute(tail, axis, [(i, (i + 1) % count) for i in range(ends)]),
                cells,
                lax.ppermute(head, axis, [((i + 1) % count, i) for i in range(ends)]),
            ],
            axis=dim,
        )
    return cells


def kernel_weights(radius):
    offsets = jnp.arange(-RMAX, RMAX + 1).astype(jnp.float32)
    dist_sq = offsets[:, None] ** 2 + offsets[None, :] ** 2
    reach = (radius.astype(jnp.float32) ** 2)[:, None, None]
    values = jnp.exp(-dist_sq[None] / (2.0 * reach)) * (dist_sq[None] <= reach).astype(jnp.float32)
    return values / jnp.sum(values, axis=(1, 2), keepdims=True)


SPLIT = (("xl", 2), ("yh", 4), ("yl", 2), ("co", 2), ("zh", 4), ("zl", 2), ("xh", 2))
ROW = ("xl", "yh", "yl", "co")
COL = ("zh", "zl", "xh")
NEAR = ("xl", "yl", "co", "zl", "xh")


def fetch_operators(tile_list, harvest_ops):
    listed = tile_list[0, 0]
    count = listed.shape[0]
    held, cohorts, _ = harvest_ops.shape
    lists = lax.all_to_all(
        jnp.broadcast_to(listed[None, :, None], (32, count, 128)), NEAR, 0, 0, tiled=True
    )[:, :, 0]
    mine = (lax.axis_index("xl") * 2 + lax.axis_index("yl")) * 2 + lax.axis_index("co")
    strip = lax.dynamic_slice_in_dim(harvest_ops, mine * 32, 32, axis=1)
    strip = strip.reshape(held, 2, 16, 2, 128).transpose(1, 3, 0, 2, 4)
    spread = jnp.broadcast_to(strip[None], (4, 2, 2, held, 16, 128)).reshape(16, held, 16, 128)
    pieces = lax.all_to_all(spread, COL, 0, 0, tiled=True).reshape(16 * held, 16, 128)
    wanted = pieces[lists.reshape(-1)].reshape(32, count, 16, 128)
    parts = lax.all_to_all(wanted, NEAR, 0, 0, tiled=True)
    parts = parts.reshape(8, 2, 2, count, 16, 128).transpose(3, 0, 1, 4, 2, 5)
    return parts.reshape(count, cohorts, cohorts)


def local(
    biomass, block_stand, stand_slot, tile_list, harvest_ops, transition, pattern, fecundity, radius
):
    rows_here, cols_here, cohorts = biomass.shape
    count = tile_list.shape[-1]
    stands = stand_slot.shape[-1]
    kernel = kernel_weights(radius)
    block_mask = jnp.repeat(jnp.repeat(pattern, TB, 0), TB, 1).astype(jnp.float32)
    moves = (transition.astype(jnp.float32) * block_mask).astype(jnp.bfloat16)
    stand_hit = block_stand[:, :, None] == jnp.arange(stands)[None, None, :]
    block_slot = jnp.sum(jnp.where(stand_hit, stand_slot[0, 0][None, None, :], 0), axis=-1)
    cell_slot = jnp.repeat(jnp.repeat(block_slot, BX, 0), BY, 1)[:, :, None]
    operators = fetch_operators(tile_list, harvest_ops)
    width = 2 * RMAX + 1
    cohort_state = biomass
    for period in range(STEPS):
        padded = padded_2(cohort_state, ((ROW, 0), (COL, 1)), RMAX)
        seedfall = jnp.zeros((rows_here, cols_here, cohorts), jnp.float32)
        for row_off in range(width):
            for col_off in range(width):
                seedfall = seedfall + kernel[:, row_off, col_off] * padded[
                    row_off : row_off + rows_here, col_off : col_off + cols_here
                ].astype(jnp.float32)
        seed_bf = seedfall.astype(jnp.bfloat16)
        middle = (
            cohort_state.astype(jnp.float32)
            + jnp.dot(seed_bf, fecundity, preferred_element_type=jnp.float32)
        ).astype(jnp.bfloat16)
        shifted = jnp.dot(middle, moves, preferred_element_type=jnp.float32)
        grown_rows = (
            shifted * lax.rsqrt(1.0 + jnp.mean(shifted * shifted, axis=-1, keepdims=True))
        ).astype(jnp.bfloat16)
        result = jnp.where(cell_slot == count, grown_rows.astype(jnp.float32), 0.0)
        for slot in range(count):
            product = jnp.dot(grown_rows, operators[slot], preferred_element_type=jnp.float32)
            result = result + jnp.where(cell_slot == slot, product, 0.0)
        cohort_state = result.astype(jnp.bfloat16)
    return cohort_state


def solution(mesh):
    names = tuple(name for name, _ in SPLIT)
    sizes = tuple(size for _, size in SPLIT)
    fine = jax.sharding.Mesh(mesh.devices.reshape(sizes), names)
    placed = (
        P(ROW, COL, None),
        P(ROW, COL),
        P(ROW, COL, None),
        P(ROW, COL, None),
        P(COL, None, None),
        P(),
        P(),
        P(),
        P(),
    )
    return jax.shard_map(
        local, mesh=fine, in_specs=placed, out_specs=P(ROW, COL, None), check_vma=False
    )
```

```python
import functools
import math

import jax
import jax.numpy as jnp
from jax import lax
from jax.experimental import pallas as pl
from jax.experimental.pallas import tpu as pltpu
from jax.sharding import PartitionSpec as P

TB = 8
RMAX = 4
BX = 8
BY = 8
STEPS = 2

SPLIT = (("xl", 2), ("yh", 4), ("yl", 2), ("co", 2), ("zh", 4), ("zl", 2), ("xh", 2))
ROW = ("xl", "yh", "yl", "co")
COL = ("zh", "zl", "xh")
NEAR = ("xl", "yl", "co", "zl", "xh")

DIST_SQ = (0, 1, 2, 4, 5, 8, 9, 10, 13, 16)
OFFSETS = (1, 4, 4, 4, 8, 4, 4, 8, 8, 4)

LEAD = 8


def shift_pairs(count):
    return [(i, i + 1) for i in range(count - 1)], [(i + 1, i) for i in range(count - 1)]


def halos(cells):
    count = math.prod(lax.axis_size(name) for name in ROW)
    down, up = shift_pairs(count)
    top = lax.ppermute(cells[-RMAX:], ROW, down)
    bottom = lax.ppermute(cells[:RMAX], ROW, up)
    count = math.prod(lax.axis_size(name) for name in COL)
    right, left = shift_pairs(count)
    tail = jnp.concatenate([top[:, -RMAX:], cells[:, -RMAX:], bottom[:, -RMAX:]], axis=0)
    head = jnp.concatenate([top[:, :RMAX], cells[:, :RMAX], bottom[:, :RMAX]], axis=0)
    return top, bottom, lax.ppermute(tail, COL, right), lax.ppermute(head, COL, left)


def class_weights(radius):
    dist = jnp.array(DIST_SQ, jnp.float32)[:, None]
    reach = (radius.astype(jnp.float32) ** 2)[None, :]
    values = jnp.exp(-dist / (2.0 * reach)) * (dist <= reach).astype(jnp.float32)
    total = jnp.sum(values * jnp.array(OFFSETS, jnp.float32)[:, None], axis=0, keepdims=True)
    return values / total


def fetch_operators(tile_list, harvest_ops):
    listed = tile_list[0, 0]
    count = listed.shape[0]
    held = harvest_ops.shape[0]
    lists = lax.all_to_all(
        jnp.broadcast_to(listed[None, :, None], (32, count, 128)), NEAR, 0, 0, tiled=True
    )[:, :, 0]
    mine = (lax.axis_index("xl") * 2 + lax.axis_index("yl")) * 2 + lax.axis_index("co")
    strip = lax.dynamic_slice_in_dim(harvest_ops, mine * 32, 32, axis=1)
    strip = strip.reshape(held, 2, 16, 2, 128).transpose(1, 3, 0, 2, 4)
    spread = jnp.broadcast_to(strip[None], (4, 2, 2, held, 16, 128)).reshape(16, held, 16, 128)
    pieces = lax.all_to_all(spread, COL, 0, 0, tiled=True).reshape(16 * held, 16, 128)
    wanted = pieces[lists.reshape(-1)].reshape(32, count, 16, 128)
    return lax.all_to_all(wanted, NEAR, 0, 0, tiled=True)


def grow(cells, top, bottom, left, right, weights, fecundity, moves, grown, padded, pairs, seeds):
    rows, cols, cohorts = cells.shape
    high = rows + 2 * RMAX
    f32 = jnp.float32

    for part, start in ((top, 0), (bottom, RMAX + rows)):
        for i in range(RMAX):
            padded[start + i, pl.ds(LEAD, cols), :] = part[i].astype(f32)

    def fill(x, carry):
        padded[RMAX + x, pl.ds(LEAD, cols), :] = cells[x].astype(f32)
        return carry

    lax.fori_loop(0, rows, fill, 0, unroll=4)

    def add_pairs(x, carry):
        padded[x, pl.ds(LEAD - RMAX, RMAX), :] = left[x].astype(f32)
        padded[x, pl.ds(LEAD + cols, RMAX), :] = right[x].astype(f32)
        for b in range(1, RMAX + 1):
            pairs[b - 1, x] = (
                padded[x, pl.ds(LEAD - b, cols), :] + padded[x, pl.ds(LEAD + b, cols), :]
            )
        return carry

    lax.fori_loop(0, high, add_pairs, 0, unroll=2)

    def row_sum(x, b):
        return padded[x, pl.ds(LEAD, cols), :] if b == 0 else pairs[b - 1, x]

    def both(x, a, b):
        return row_sum(x + a, b) + row_sum(x - a, b)

    def disperse(x):
        at = x + RMAX
        sums = (
            row_sum(at, 0),
            row_sum(at, 1) + both(at, 1, 0),
            both(at, 1, 1),
            row_sum(at, 2) + both(at, 2, 0),
            both(at, 2, 1) + both(at, 1, 2),
            both(at, 2, 2),
            row_sum(at, 3) + both(at, 3, 0),
            both(at, 1, 3) + both(at, 3, 1),
            both(at, 2, 3) + both(at, 3, 2),
            row_sum(at, 4) + both(at, 4, 0),
        )
        total = sums[0] * weights[0:1, :]
        for k in range(1, len(sums)):
            total = total + sums[k] * weights[k : k + 1, :]
        seeds[x] = total.astype(jnp.bfloat16)

    def chunk(i, carry):
        def one(j, inner):
            disperse(i * BX + j)
            return inner

        lax.fori_loop(0, BX, one, 0, unroll=2)
        span = pl.ds(pl.multiple_of(i * BX, BX), BX)
        arrived = jnp.dot(
            seeds[span].reshape(BX * cols, cohorts), fecundity[...], preferred_element_type=f32
        )
        here = cells[span].reshape(BX * cols, cohorts).astype(f32)
        middle = (here + arrived).astype(jnp.bfloat16)
        shifted = jnp.dot(middle, moves[...], preferred_element_type=f32)
        norm = lax.rsqrt(1.0 + jnp.mean(shifted * shifted, axis=-1, keepdims=True))
        grown[span] = (shifted * norm).astype(jnp.bfloat16).reshape(BX, cols, cohorts)
        return carry

    lax.fori_loop(0, rows // BX, chunk, 0)


def harvest(slots, grown, ops, out):
    rows, cols, cohorts = grown.shape
    count = ops.shape[0]
    wide = 2 * BY
    for i in range(rows // BX):
        for j in range(cols // wide):
            block = grown[i * BX : (i + 1) * BX, j * wide : (j + 1) * wide, :]
            flat = block.reshape(BX * wide, cohorts)
            halves = []
            for h in range(2):
                slot = slots[i, 2 * j + h]
                product = jnp.dot(
                    flat, ops[jnp.minimum(slot, count - 1)], preferred_element_type=jnp.float32
                )
                product = jnp.where(slot == count, flat.astype(jnp.float32), product)
                halves.append(product.reshape(BX, wide, cohorts)[:, h * BY : (h + 1) * BY])
            out[i * BX : (i + 1) * BX, j * wide : (j + 1) * wide, :] = jnp.concatenate(
                halves, axis=1
            ).astype(jnp.bfloat16)


def assemble(parts, ops):
    count = ops.shape[0]

    def one(k, carry):
        for piece in range(parts.shape[0]):
            r, h = divmod(piece, 2)
            ops[k, r * 16 : (r + 1) * 16, h * 128 : (h + 1) * 128] = parts[piece, k]
        return carry

    lax.fori_loop(0, count, one, 0)


def first_kernel(cells, top, bottom, left, right, weights, fecundity, moves, grown, padded, pairs, seeds):
    grow(cells, top, bottom, left, right, weights, fecundity, moves, grown, padded, pairs, seeds)


def harvest_kernel(slots, grown, parts, out, ops):
    assemble(parts, ops)
    harvest(slots, grown, ops, out)


def last_kernel(
    slots, cells, top, bottom, left, right, weights, fecundity, moves, ops,
    out, grown, padded, pairs, seeds,
):
    grow(cells, top, bottom, left, right, weights, fecundity, moves, grown, padded, pairs, seeds)
    harvest(slots, grown, ops, out)


VMEM = pl.BlockSpec(memory_space=pltpu.VMEM)
SMEM = pl.BlockSpec(memory_space=pltpu.SMEM)
PARAMS = pltpu.CompilerParams(vmem_limit_bytes=32 * 1024 * 1024)


def scratch(rows, cols, cohorts):
    high = rows + 2 * RMAX
    return [
        pltpu.VMEM((high, cols + 2 * LEAD, cohorts), jnp.float32),
        pltpu.VMEM((RMAX, high, cols, cohorts), jnp.float32),
        pltpu.VMEM((rows, cols, cohorts), jnp.bfloat16),
    ]


def local(
    biomass, block_stand, stand_slot, tile_list, harvest_ops, transition, pattern, fecundity, radius
):
    shape = biomass.shape
    rows, cols, cohorts = shape
    count = tile_list.shape[-1]
    stands = stand_slot.shape[-1]
    state = jax.ShapeDtypeStruct(shape, jnp.bfloat16)
    operators = jax.ShapeDtypeStruct((count, cohorts, cohorts), jnp.bfloat16)

    weights = class_weights(radius)
    block_mask = jnp.repeat(jnp.repeat(pattern, TB, 0), TB, 1).astype(jnp.float32)
    moves = (transition.astype(jnp.float32) * block_mask).astype(jnp.bfloat16)
    stand_hit = block_stand[:, :, None] == jnp.arange(stands)[None, None, :]
    slots = jnp.sum(jnp.where(stand_hit, stand_slot[0, 0][None, None, :], 0), axis=-1)

    parts = fetch_operators(tile_list, harvest_ops)
    grown = pl.pallas_call(
        first_kernel,
        out_shape=state,
        in_specs=[VMEM] * 8,
        out_specs=VMEM,
        scratch_shapes=scratch(*shape),
        compiler_params=PARAMS,
        cost_estimate=pl.CostEstimate(flops=2**28, bytes_accessed=2**24, transcendentals=0),
    )(biomass, *halos(biomass), weights, fecundity, moves)
    cells, ops = pl.pallas_call(
        harvest_kernel,
        out_shape=(state, operators),
        in_specs=[SMEM, VMEM, VMEM],
        out_specs=(VMEM, VMEM),
        compiler_params=PARAMS,
        cost_estimate=pl.CostEstimate(flops=2**28, bytes_accessed=2**22, transcendentals=0),
    )(slots, grown, parts)
    return pl.pallas_call(
        last_kernel,
        out_shape=state,
        in_specs=[SMEM] + [VMEM] * 9,
        out_specs=VMEM,
        scratch_shapes=[pltpu.VMEM(shape, jnp.bfloat16)] + scratch(*shape),
        compiler_params=PARAMS,
        cost_estimate=pl.CostEstimate(flops=2**29, bytes_accessed=2**24, transcendentals=0),
    )(slots, cells, *halos(cells), weights, fecundity, moves, ops)


def solution(mesh):
    names = tuple(name for name, _ in SPLIT)
    sizes = tuple(size for _, size in SPLIT)
    fine = jax.sharding.Mesh(mesh.devices.reshape(sizes), names)
    placed = (
        P(ROW, COL, None),
        P(ROW, COL),
        P(ROW, COL, None),
        P(ROW, COL, None),
        P(COL, None, None),
        P(),
        P(),
        P(),
        P(),
    )
    return jax.shard_map(
        local, mesh=fine, in_specs=placed, out_specs=P(ROW, COL, None), check_vma=False
    )
```

```python
import functools
import math

import jax
import jax.numpy as jnp
from jax import lax
from jax.experimental import pallas as pl
from jax.experimental.pallas import tpu as pltpu
from jax.sharding import PartitionSpec as P

TB = 8
RMAX = 4
BX = 8
BY = 8
STEPS = 2

SPLIT = (("xl", 2), ("yh", 4), ("yl", 2), ("co", 2), ("zh", 4), ("zl", 2), ("xh", 2))
ROW = ("xl", "yh", "yl", "co")
COL = ("zh", "zl", "xh")
NEAR = ("xl", "yl", "co", "zl", "xh")

DIST_SQ = (0, 1, 2, 4, 5, 8, 9, 10, 13, 16)
OFFSETS = (1, 4, 4, 4, 8, 4, 4, 8, 8, 4)

VMEM = pl.BlockSpec(memory_space=pltpu.VMEM)
SMEM = pl.BlockSpec(memory_space=pltpu.SMEM)
ANY = pl.BlockSpec(memory_space=pl.ANY)
PARAMS = pltpu.CompilerParams(vmem_limit_bytes=32 * 1024 * 1024)

LEAD = 8


def shift_pairs(count):
    return [(i, i + 1) for i in range(count - 1)], [(i + 1, i) for i in range(count - 1)]


def swap_rows(first, last):
    down, up = shift_pairs(math.prod(lax.axis_size(name) for name in ROW))
    return lax.ppermute(last, ROW, down), lax.ppermute(first, ROW, up)


def swap_columns(head, tail):
    right, left = shift_pairs(math.prod(lax.axis_size(name) for name in COL))
    return lax.ppermute(tail, COL, right), lax.ppermute(head, COL, left)


def class_weights(radius):
    dist = jnp.array(DIST_SQ, jnp.float32)[:, None]
    reach = (radius.astype(jnp.float32) ** 2)[None, :]
    values = jnp.exp(-dist / (2.0 * reach)) * (dist <= reach).astype(jnp.float32)
    total = jnp.sum(values * jnp.array(OFFSETS, jnp.float32)[:, None], axis=0, keepdims=True)
    return values / total


def edges_kernel(cells, lists, first, last, head, tail):
    del lists
    rows, cols, _ = cells.shape
    first[...] = cells[pl.ds(0, RMAX)]
    last[...] = cells[pl.ds(rows - RMAX, RMAX)]

    def one(x, carry):
        row = cells[x].astype(jnp.float32)
        head[x] = row[:RMAX].astype(jnp.bfloat16)
        tail[x] = row[cols - RMAX :].astype(jnp.bfloat16)
        return carry

    lax.fori_loop(0, rows, one, 0, unroll=4)


def gather_kernel(lists, pieces, top, bottom, own_head, own_tail, wanted, head, tail):
    members, count = wanted.shape[:2]
    rows, cols = own_head.shape[0], top.shape[1]

    def one(m, carry):
        found = [pieces[lists[m, 0, k]] for k in range(count)]
        for k in range(count):
            wanted[m, k] = found[k]
        return carry

    lax.fori_loop(0, members, one, 0, unroll=4)
    head[pl.ds(RMAX, rows)] = own_head[...]
    tail[pl.ds(RMAX, rows)] = own_tail[...]
    for part, start in ((top, 0), (bottom, RMAX + rows)):
        for i in range(RMAX):
            row = part[i].astype(jnp.float32)
            head[start + i] = row[:RMAX].astype(jnp.bfloat16)
            tail[start + i] = row[cols - RMAX :].astype(jnp.bfloat16)


def fetch(tile_list, harvest_ops, cells):
    rows, cols, cohorts = cells.shape
    count = tile_list.shape[-1]
    held = harvest_ops.shape[0]
    row_part = jax.ShapeDtypeStruct((RMAX, cols, cohorts), jnp.bfloat16)
    col_part = jax.ShapeDtypeStruct((rows, RMAX, cohorts), jnp.bfloat16)
    col_whole = jax.ShapeDtypeStruct((rows + 2 * RMAX, RMAX, cohorts), jnp.bfloat16)
    lists = lax.all_to_all(
        jnp.broadcast_to(jnp.pad(tile_list, ((0, 0), (0, 0), (0, 128 - count))), (32, 1, 128)),
        NEAR, 0, 0, tiled=True,
    )
    first, last, own_head, own_tail = pl.pallas_call(
        edges_kernel,
        out_shape=(row_part, row_part, col_part, col_part),
        in_specs=[VMEM, ANY],
        out_specs=(VMEM,) * 4,
        compiler_params=PARAMS,
        cost_estimate=pl.CostEstimate(flops=0, bytes_accessed=2**20, transcendentals=0),
    )(cells, lists)
    top, bottom = swap_rows(first, last)
    mine = (lax.axis_index("xl") * 2 + lax.axis_index("yl")) * 2 + lax.axis_index("co")
    strip = lax.dynamic_slice_in_dim(harvest_ops, mine * 32, 32, axis=1)
    strip = strip.reshape(held, 2, 16, 2, 128).transpose(1, 3, 0, 2, 4)
    spread = jnp.broadcast_to(strip[None], (4, 2, 2, held, 16, 128)).reshape(16, held, 16, 128)
    pieces = lax.all_to_all(spread, COL, 0, 0, tiled=True).reshape(16 * held, 16, 128)
    wanted, head, tail = pl.pallas_call(
        gather_kernel,
        out_shape=(
            jax.ShapeDtypeStruct((32, count, 16, 128), jnp.bfloat16), col_whole, col_whole
        ),
        in_specs=[SMEM] + [VMEM] * 5,
        out_specs=(VMEM,) * 3,
        compiler_params=PARAMS,
        cost_estimate=pl.CostEstimate(flops=0, bytes_accessed=2**21, transcendentals=0),
    )(lists, pieces, top, bottom, own_head, own_tail)
    parts = lax.all_to_all(wanted, NEAR, 0, 0, tiled=True)
    return parts, (top, bottom) + swap_columns(head, tail)


def fill_rows(cells, top, bottom, padded):
    rows, cols, _ = cells.shape
    for part, start in ((top, 0), (bottom, RMAX + rows)):
        for i in range(RMAX):
            padded[start + i, pl.ds(LEAD, cols), :] = part[i].astype(jnp.float32)

    def fill(x, carry):
        padded[RMAX + x, pl.ds(LEAD, cols), :] = cells[x].astype(jnp.float32)
        return carry

    lax.fori_loop(0, rows, fill, 0, unroll=4)


def fill_sides(left, right, padded, pairs):
    high, cols, cohorts = pairs.shape[1:]

    def one(x, carry):
        if left is None:
            before = after = jnp.zeros((RMAX, cohorts), jnp.float32)
        else:
            before, after = left[x].astype(jnp.float32), right[x].astype(jnp.float32)
        padded[x, pl.ds(LEAD - RMAX, RMAX), :] = before
        padded[x, pl.ds(LEAD + cols, RMAX), :] = after
        for b in range(1, RMAX + 1):
            pairs[b - 1, x] = (
                padded[x, pl.ds(LEAD - b, cols), :] + padded[x, pl.ds(LEAD + b, cols), :]
            )
        return carry

    lax.fori_loop(0, high, one, 0, unroll=2)


def weigh(x, row_sum, weights):
    at = x + RMAX

    def both(a, b):
        low, high = row_sum(at - a, b), row_sum(at + a, b)
        return None if low is None else low + high

    sums = (
        (row_sum(at, 0),),
        (row_sum(at, 1), both(1, 0)),
        (both(1, 1),),
        (row_sum(at, 2), both(2, 0)),
        (both(2, 1), both(1, 2)),
        (both(2, 2),),
        (row_sum(at, 3), both(3, 0)),
        (both(1, 3), both(3, 1)),
        (both(2, 3), both(3, 2)),
        (row_sum(at, 4), both(4, 0)),
    )
    total = None
    for k, terms in enumerate(sums):
        terms = [term for term in terms if term is not None]
        if terms:
            value = functools.reduce(lambda p, q: p + q, terms) * weights[k : k + 1, :]
            total = value if total is None else total + value
    return total


def establish(seeds, here, fecundity, moves):
    arrived = jnp.dot(seeds, fecundity[...], preferred_element_type=jnp.float32)
    middle = (here + arrived).astype(jnp.bfloat16)
    shifted = jnp.dot(middle, moves[...], preferred_element_type=jnp.float32)
    norm = lax.rsqrt(1.0 + jnp.mean(shifted * shifted, axis=-1, keepdims=True))
    return (shifted * norm).astype(jnp.bfloat16)


def remove(flat, slot, ops):
    count = ops.shape[0]
    product = jnp.dot(flat, ops[jnp.minimum(slot, count - 1)], preferred_element_type=jnp.float32)
    return jnp.where(slot == count, flat.astype(jnp.float32), product)


def remove_pair(flat, slots, ops):
    halves = []
    for h, slot in enumerate(slots):
        product = remove(flat, slot, ops).reshape(BX, 2 * BY, flat.shape[-1])
        halves.append(product[:, h * BY : (h + 1) * BY])
    return jnp.concatenate(halves, axis=1)


def assemble(parts, ops):
    count = ops.shape[0]

    def one(k, carry):
        for piece in range(parts.shape[0]):
            r, h = divmod(piece, 2)
            ops[k, r * 16 : (r + 1) * 16, h * 128 : (h + 1) * 128] = parts[piece, k]
        return carry

    lax.fori_loop(0, count, one, 0)


def first_kernel(cells, top, bottom, left, right, weights, fecundity, moves, grown, padded, pairs, seeds):
    rows, cols, cohorts = cells.shape
    fill_rows(cells, top, bottom, padded)
    fill_sides(left, right, padded, pairs)

    def row_sum(x, b):
        return padded[x, pl.ds(LEAD, cols), :] if b == 0 else pairs[b - 1, x]

    def one(x, carry):
        seeds[x] = weigh(x, row_sum, weights).astype(jnp.bfloat16)
        return carry

    lax.fori_loop(0, rows, one, 0, unroll=2)
    for i in range(rows // BX):
        span = pl.ds(i * BX, BX)
        here = cells[span].reshape(BX * cols, cohorts).astype(jnp.float32)
        result = establish(seeds[span].reshape(BX * cols, cohorts), here, fecundity, moves)
        grown[span] = result.reshape(BX, cols, cohorts)


def harvest_kernel(slots, grown, parts, out, ops, first, last, head, tail):
    assemble(parts, ops)
    rows, cols, cohorts = grown.shape
    wide = 2 * BY
    for i in range(rows // BX):
        span = pl.ds(i * BX, BX)
        done = []
        for j in range(cols // wide):
            flat = grown[span, pl.ds(j * wide, wide), :].reshape(BX * wide, cohorts)
            done.append(remove_pair(flat, (slots[i, 2 * j], slots[i, 2 * j + 1]), ops))
        whole = jnp.concatenate(done, axis=1)
        out[span] = whole.astype(jnp.bfloat16)
        head[span] = whole[:, :RMAX].astype(jnp.bfloat16)
        tail[span] = whole[:, cols - RMAX :].astype(jnp.bfloat16)
        if i == 0:
            first[...] = whole[:RMAX].astype(jnp.bfloat16)
        if i == rows // BX - 1:
            last[...] = whole[BX - RMAX :].astype(jnp.bfloat16)


def middle_kernel(
    slots, cells, top, bottom, weights, fecundity, moves, ops, inner, partial, padded, pairs, seeds
):
    rows, cols, cohorts = cells.shape
    fill_rows(cells, top, bottom, padded)
    fill_sides(None, None, padded, pairs)

    def row_sum(x, b):
        return padded[x, pl.ds(LEAD, cols), :] if b == 0 else pairs[b - 1, x]

    def one(x, carry):
        total = weigh(x, row_sum, weights)
        partial[x] = jnp.concatenate([total[:BY], total[cols - BY :]], axis=0)
        seeds[x] = total[BY : cols - BY].astype(jnp.bfloat16)
        return carry

    lax.fori_loop(0, rows, one, 0, unroll=2)
    for i in range(0, rows // BX, 2):
        span = pl.ds(i * BX, 2 * BX)
        here = cells[span].astype(jnp.float32)[:, BY : cols - BY].reshape(-1, cohorts)
        grown = establish(seeds[span].reshape(-1, cohorts), here, fecundity, moves)
        half = grown.shape[0] // 2
        for k in range(2):
            done = remove_pair(
                grown[k * half : (k + 1) * half], (slots[i + k, 1], slots[i + k, 2]), ops
            )
            inner[pl.ds((i + k) * BX, BX)] = done.astype(jnp.bfloat16)


def last_kernel(
    slots, cells, left, right, weights, fecundity, moves, ops, inner, partial,
    out, sides, pairs, seeds,
):
    rows, cols, cohorts = cells.shape
    near = lax.broadcasted_iota(jnp.int32, (BY, cohorts), 0) < RMAX
    gap = jnp.zeros((RMAX, cohorts), jnp.float32)

    def place(x, carry):
        sides[x, pl.ds(BY - RMAX, RMAX), :] = left[x].astype(jnp.float32)
        sides[x, pl.ds(BY, RMAX), :] = gap
        sides[x, pl.ds(BY + RMAX, RMAX), :] = right[x].astype(jnp.float32)
        for b in range(1, RMAX + 1):
            pairs[b - 1, x] = jnp.where(
                near, sides[x, pl.ds(BY - b, BY), :], sides[x, pl.ds(RMAX + b, BY), :]
            )
        return carry

    lax.fori_loop(0, rows + 2 * RMAX, place, 0, unroll=4)

    def row_sum(x, b):
        return None if b == 0 else pairs[b - 1, x]

    def one(x, carry):
        extra = weigh(x, row_sum, weights)
        both = jnp.concatenate([jnp.where(near, extra, 0.0), jnp.where(near, 0.0, extra)], axis=0)
        seeds[x] = (partial[x] + both).astype(jnp.bfloat16)
        return carry

    lax.fori_loop(0, rows, one, 0, unroll=4)
    for i in range(0, rows // BX, 2):
        span = pl.ds(i * BX, 2 * BX)
        here = cells[span].astype(jnp.float32)
        here = jnp.concatenate([here[:, :BY], here[:, cols - BY :]], axis=1).reshape(-1, cohorts)
        grown = establish(seeds[span].reshape(-1, cohorts), here, fecundity, moves)
        half = grown.shape[0] // 2
        for k in range(2):
            done = remove_pair(
                grown[k * half : (k + 1) * half], (slots[i + k, 0], slots[i + k, 3]), ops
            )
            at = pl.ds((i + k) * BX, BX)
            whole = jnp.concatenate(
                [done[:, :BY], inner[at].astype(jnp.float32), done[:, BY:]], axis=1
            )
            out[at] = whole.astype(jnp.bfloat16)


def scratch(rows, cols, cohorts, seeded=None):
    high = rows + 2 * RMAX
    return [
        pltpu.VMEM((high, cols + 2 * LEAD, cohorts), jnp.float32),
        pltpu.VMEM((RMAX, high, cols, cohorts), jnp.float32),
        pltpu.VMEM((rows, seeded or cols, cohorts), jnp.bfloat16),
    ]


def local(
    biomass, block_stand, stand_slot, tile_list, harvest_ops, transition, pattern, fecundity, radius
):
    shape = biomass.shape
    rows, cols, cohorts = shape
    count = tile_list.shape[-1]
    stands = stand_slot.shape[-1]
    state = jax.ShapeDtypeStruct(shape, jnp.bfloat16)
    operators = jax.ShapeDtypeStruct((count, cohorts, cohorts), jnp.bfloat16)

    weights = class_weights(radius)
    block_mask = jnp.repeat(jnp.repeat(pattern, TB, 0), TB, 1).astype(jnp.float32)
    moves = (transition.astype(jnp.float32) * block_mask).astype(jnp.bfloat16)
    stand_hit = block_stand[:, :, None] == jnp.arange(stands)[None, None, :]
    slots = jnp.sum(jnp.where(stand_hit, stand_slot[0, 0][None, None, :], 0), axis=-1)

    parts, around = fetch(tile_list, harvest_ops, biomass)
    grown = pl.pallas_call(
        first_kernel,
        out_shape=state,
        in_specs=[VMEM] * 8,
        out_specs=VMEM,
        scratch_shapes=scratch(*shape),
        compiler_params=PARAMS,
        cost_estimate=pl.CostEstimate(flops=2**28, bytes_accessed=2**24, transcendentals=0),
    )(biomass, *around, weights, fecundity, moves)
    row_part = jax.ShapeDtypeStruct((RMAX, cols, cohorts), jnp.bfloat16)
    col_part = jax.ShapeDtypeStruct((rows, RMAX, cohorts), jnp.bfloat16)
    cells, ops, first, last, head, tail = pl.pallas_call(
        harvest_kernel,
        out_shape=(state, operators, row_part, row_part, col_part, col_part),
        in_specs=[SMEM, VMEM, VMEM],
        out_specs=(VMEM,) * 6,
        compiler_params=PARAMS,
        cost_estimate=pl.CostEstimate(flops=2**28, bytes_accessed=2**22, transcendentals=0),
    )(slots, grown, parts)
    top, bottom = swap_rows(first, last)
    head = jnp.concatenate([top[:, :RMAX], head, bottom[:, :RMAX]], axis=0)
    tail = jnp.concatenate([top[:, -RMAX:], tail, bottom[:, -RMAX:]], axis=0)
    left, right = swap_columns(head, tail)
    high = rows + 2 * RMAX
    outer = 2 * BY
    inner, partial = pl.pallas_call(
        middle_kernel,
        out_shape=(
            jax.ShapeDtypeStruct((rows, cols - outer, cohorts), jnp.bfloat16),
            jax.ShapeDtypeStruct((rows, outer, cohorts), jnp.float32),
        ),
        in_specs=[SMEM] + [VMEM] * 7,
        out_specs=(VMEM, VMEM),
        scratch_shapes=scratch(rows, cols, cohorts, cols - outer),
        compiler_params=PARAMS,
        cost_estimate=pl.CostEstimate(flops=2**28, bytes_accessed=2**24, transcendentals=0),
    )(slots, cells, top, bottom, weights, fecundity, moves, ops)
    return pl.pallas_call(
        last_kernel,
        out_shape=state,
        in_specs=[SMEM] + [VMEM] * 9,
        out_specs=VMEM,
        scratch_shapes=[
            pltpu.VMEM((high, outer, cohorts), jnp.float32),
            pltpu.VMEM((RMAX, high, BY, cohorts), jnp.float32),
            pltpu.VMEM((rows, outer, cohorts), jnp.bfloat16),
        ],
        compiler_params=PARAMS,
        cost_estimate=pl.CostEstimate(flops=2**28, bytes_accessed=2**22, transcendentals=0),
    )(slots, cells, left, right, weights, fecundity, moves, ops, inner, partial)


def solution(mesh):
    names = tuple(name for name, _ in SPLIT)
    sizes = tuple(size for _, size in SPLIT)
    fine = jax.sharding.Mesh(mesh.devices.reshape(sizes), names)
    placed = (
        P(ROW, COL, None),
        P(ROW, COL),
        P(ROW, COL, None),
        P(ROW, COL, None),
        P(COL, None, None),
        P(),
        P(),
        P(),
        P(),
    )
    return jax.shard_map(
        local, mesh=fine, in_specs=placed, out_specs=P(ROW, COL, None), check_vma=False
    )
```

```python
import functools
import math

import jax
import jax.numpy as jnp
from jax import lax
from jax.experimental import pallas as pl
from jax.experimental.pallas import tpu as pltpu
from jax.sharding import PartitionSpec as P

TB = 8
RMAX = 4
BX = 8
BY = 8
STEPS = 2

SPLIT = (("xl", 2), ("yh", 4), ("yl", 2), ("co", 2), ("zh", 4), ("zl", 2), ("xh", 2))
ROW = ("xl", "yh", "yl", "co")
COL = ("zh", "zl", "xh")
NEAR = ("xl", "yl", "co", "zl", "xh")

DIST_SQ = (0, 1, 2, 4, 5, 8, 9, 10, 13, 16)
OFFSETS = (1, 4, 4, 4, 8, 4, 4, 8, 8, 4)

VMEM = pl.BlockSpec(memory_space=pltpu.VMEM)
SMEM = pl.BlockSpec(memory_space=pltpu.SMEM)
ANY = pl.BlockSpec(memory_space=pl.ANY)
PARAMS = pltpu.CompilerParams(vmem_limit_bytes=32 * 1024 * 1024)

LEAD = 8


def shift_pairs(count):
    return [(i, i + 1) for i in range(count - 1)], [(i + 1, i) for i in range(count - 1)]


def surround(first, last, head, tail):
    down, up = shift_pairs(math.prod(lax.axis_size(name) for name in ROW))
    top, bottom = lax.ppermute(last, ROW, down), lax.ppermute(first, ROW, up)
    head = jnp.concatenate([top[:, :RMAX], head, bottom[:, :RMAX]], axis=0)
    tail = jnp.concatenate([top[:, -RMAX:], tail, bottom[:, -RMAX:]], axis=0)
    right, left = shift_pairs(math.prod(lax.axis_size(name) for name in COL))
    return top, bottom, lax.ppermute(tail, COL, right), lax.ppermute(head, COL, left)


def class_weights(radius):
    dist = jnp.array(DIST_SQ, jnp.float32)[:, None]
    reach = (radius.astype(jnp.float32) ** 2)[None, :]
    values = jnp.exp(-dist / (2.0 * reach)) * (dist <= reach).astype(jnp.float32)
    total = jnp.sum(values * jnp.array(OFFSETS, jnp.float32)[:, None], axis=0, keepdims=True)
    return values / total


def edges_kernel(cells, first, last, head, tail):
    rows, cols, _ = cells.shape
    first[...] = cells[pl.ds(0, RMAX)]
    last[...] = cells[pl.ds(rows - RMAX, RMAX)]

    def one(x, carry):
        row = cells[x].astype(jnp.float32)
        head[x] = row[:RMAX].astype(jnp.bfloat16)
        tail[x] = row[cols - RMAX :].astype(jnp.bfloat16)
        return carry

    lax.fori_loop(0, rows, one, 0, unroll=4)


def spread_kernel(held, weights, moves, spread):
    del weights, moves
    mine = (lax.axis_index("xl") * 2 + lax.axis_index("yl")) * 2 + lax.axis_index("co")
    for k in range(held.shape[0]):
        for near in range(4):
            low, half = divmod(near, 2)
            at = pl.multiple_of(mine * 32 + low * 16, 16)
            piece = held[k, pl.ds(at, 16), pl.ds(half * 128, 128)]
            for far in range(4):
                spread[far * 4 + near, k] = piece


def gather_kernel(lists, pieces, left, wanted):
    del left
    members, count = wanted.shape[:2]

    def one(m, carry):
        found = [pieces[lists[m, 0, k]] for k in range(count)]
        for k in range(count):
            wanted[m, k] = found[k]
        return carry

    lax.fori_loop(0, members, one, 0, unroll=4)


def fetch(tile_list, harvest_ops, cells, weights, moves):
    rows, cols, cohorts = cells.shape
    count = tile_list.shape[-1]
    held = harvest_ops.shape[0]
    row_part = jax.ShapeDtypeStruct((RMAX, cols, cohorts), jnp.bfloat16)
    col_part = jax.ShapeDtypeStruct((rows, RMAX, cohorts), jnp.bfloat16)
    lists = lax.all_to_all(
        jnp.broadcast_to(jnp.pad(tile_list, ((0, 0), (0, 0), (0, 128 - count))), (32, 1, 128)),
        NEAR, 0, 0, tiled=True,
    )
    first, last, head, tail = pl.pallas_call(
        edges_kernel,
        out_shape=(row_part, row_part, col_part, col_part),
        in_specs=[VMEM],
        out_specs=(VMEM,) * 4,
        compiler_params=PARAMS,
        cost_estimate=pl.CostEstimate(flops=0, bytes_accessed=2**20, transcendentals=0),
    )(cells)
    top, bottom, left, right = surround(first, last, head, tail)
    spread = pl.pallas_call(
        spread_kernel,
        out_shape=jax.ShapeDtypeStruct((16, held, 16, 128), jnp.bfloat16),
        in_specs=[VMEM, ANY, ANY],
        out_specs=VMEM,
        compiler_params=PARAMS,
        cost_estimate=pl.CostEstimate(flops=0, bytes_accessed=2**20, transcendentals=0),
    )(harvest_ops, weights, moves)
    pieces = lax.all_to_all(spread, COL, 0, 0, tiled=True).reshape(16 * held, 16, 128)
    wanted = pl.pallas_call(
        gather_kernel,
        out_shape=jax.ShapeDtypeStruct((32, count, 16, 128), jnp.bfloat16),
        in_specs=[SMEM, VMEM, ANY],
        out_specs=VMEM,
        compiler_params=PARAMS,
        cost_estimate=pl.CostEstimate(flops=0, bytes_accessed=2**21, transcendentals=0),
    )(lists, pieces, left)
    parts = lax.all_to_all(wanted, NEAR, 0, 0, tiled=True)
    return parts, (top, bottom, left, right)


def fill_rows(cells, top, bottom, padded):
    rows, cols, _ = cells.shape
    for part, start in ((top, 0), (bottom, RMAX + rows)):
        for i in range(RMAX):
            padded[start + i, pl.ds(LEAD, cols), :] = part[i].astype(jnp.float32)

    def fill(x, carry):
        padded[RMAX + x, pl.ds(LEAD, cols), :] = cells[x].astype(jnp.float32)
        return carry

    lax.fori_loop(0, rows, fill, 0, unroll=4)


def fill_sides(left, right, padded, pairs):
    high, cols, cohorts = pairs.shape[1:]

    def one(x, carry):
        if left is None:
            before = after = jnp.zeros((RMAX, cohorts), jnp.float32)
        else:
            before, after = left[x].astype(jnp.float32), right[x].astype(jnp.float32)
        padded[x, pl.ds(LEAD - RMAX, RMAX), :] = before
        padded[x, pl.ds(LEAD + cols, RMAX), :] = after
        for b in range(1, RMAX + 1):
            pairs[b - 1, x] = (
                padded[x, pl.ds(LEAD - b, cols), :] + padded[x, pl.ds(LEAD + b, cols), :]
            )
        return carry

    lax.fori_loop(0, high, one, 0, unroll=2)


def weigh(x, row_sum, weights):
    at = x + RMAX

    def both(a, b):
        low, high = row_sum(at - a, b), row_sum(at + a, b)
        return None if low is None else low + high

    sums = (
        (row_sum(at, 0),),
        (row_sum(at, 1), both(1, 0)),
        (both(1, 1),),
        (row_sum(at, 2), both(2, 0)),
        (both(2, 1), both(1, 2)),
        (both(2, 2),),
        (row_sum(at, 3), both(3, 0)),
        (both(1, 3), both(3, 1)),
        (both(2, 3), both(3, 2)),
        (row_sum(at, 4), both(4, 0)),
    )
    total = None
    for k, terms in enumerate(sums):
        terms = [term for term in terms if term is not None]
        if terms:
            value = functools.reduce(lambda p, q: p + q, terms) * weights[k : k + 1, :]
            total = value if total is None else total + value
    return total


def establish(seeds, here, fecundity, moves):
    arrived = jnp.dot(seeds, fecundity[...], preferred_element_type=jnp.float32)
    middle = (here + arrived).astype(jnp.bfloat16)
    shifted = jnp.dot(middle, moves[...], preferred_element_type=jnp.float32)
    norm = lax.rsqrt(1.0 + jnp.mean(shifted * shifted, axis=-1, keepdims=True))
    return (shifted * norm).astype(jnp.bfloat16)


def remove(flat, slot, ops):
    count = ops.shape[0]
    product = jnp.dot(flat, ops[jnp.minimum(slot, count - 1)], preferred_element_type=jnp.float32)
    return jnp.where(slot == count, flat.astype(jnp.float32), product)


def remove_pair(flat, slots, ops):
    halves = []
    for h, slot in enumerate(slots):
        product = remove(flat, slot, ops).reshape(BX, 2 * BY, flat.shape[-1])
        halves.append(product[:, h * BY : (h + 1) * BY])
    return jnp.concatenate(halves, axis=1)


def assemble(parts, ops):
    count = ops.shape[0]

    def one(k, carry):
        for piece in range(parts.shape[0]):
            r, h = divmod(piece, 2)
            ops[k, r * 16 : (r + 1) * 16, h * 128 : (h + 1) * 128] = parts[piece, k]
        return carry

    lax.fori_loop(0, count, one, 0)


def first_kernel(cells, top, bottom, left, right, weights, fecundity, moves, grown, padded, pairs, seeds):
    rows, cols, cohorts = cells.shape
    fill_rows(cells, top, bottom, padded)
    fill_sides(left, right, padded, pairs)

    def row_sum(x, b):
        return padded[x, pl.ds(LEAD, cols), :] if b == 0 else pairs[b - 1, x]

    def one(x, carry):
        seeds[x] = weigh(x, row_sum, weights).astype(jnp.bfloat16)
        return carry

    lax.fori_loop(0, rows, one, 0, unroll=2)
    for i in range(rows // BX):
        span = pl.ds(i * BX, BX)
        here = cells[span].reshape(BX * cols, cohorts).astype(jnp.float32)
        result = establish(seeds[span].reshape(BX * cols, cohorts), here, fecundity, moves)
        grown[span] = result.reshape(BX, cols, cohorts)


def harvest_kernel(slots, grown, parts, out, ops, first, last, head, tail):
    assemble(parts, ops)
    rows, cols, cohorts = grown.shape
    wide = 2 * BY
    for i in range(rows // BX):
        span = pl.ds(i * BX, BX)
        done = []
        for j in range(cols // wide):
            flat = grown[span, pl.ds(j * wide, wide), :].reshape(BX * wide, cohorts)
            done.append(remove_pair(flat, (slots[i, 2 * j], slots[i, 2 * j + 1]), ops))
        whole = jnp.concatenate(done, axis=1)
        out[span] = whole.astype(jnp.bfloat16)
        head[span] = whole[:, :RMAX].astype(jnp.bfloat16)
        tail[span] = whole[:, cols - RMAX :].astype(jnp.bfloat16)
        if i == 0:
            first[...] = whole[:RMAX].astype(jnp.bfloat16)
        if i == rows // BX - 1:
            last[...] = whole[BX - RMAX :].astype(jnp.bfloat16)


def middle_kernel(
    slots, cells, top, bottom, weights, fecundity, moves, ops, inner, partial, padded, pairs, seeds
):
    rows, cols, cohorts = cells.shape
    fill_rows(cells, top, bottom, padded)
    fill_sides(None, None, padded, pairs)

    def row_sum(x, b):
        return padded[x, pl.ds(LEAD, cols), :] if b == 0 else pairs[b - 1, x]

    def one(x, carry):
        total = weigh(x, row_sum, weights)
        partial[x] = jnp.concatenate([total[:BY], total[cols - BY :]], axis=0)
        seeds[x] = total[BY : cols - BY].astype(jnp.bfloat16)
        return carry

    lax.fori_loop(0, rows, one, 0, unroll=2)
    for i in range(0, rows // BX, 2):
        span = pl.ds(i * BX, 2 * BX)
        here = cells[span].astype(jnp.float32)[:, BY : cols - BY].reshape(-1, cohorts)
        grown = establish(seeds[span].reshape(-1, cohorts), here, fecundity, moves)
        half = grown.shape[0] // 2
        for k in range(2):
            done = remove_pair(
                grown[k * half : (k + 1) * half], (slots[i + k, 1], slots[i + k, 2]), ops
            )
            inner[pl.ds((i + k) * BX, BX)] = done.astype(jnp.bfloat16)


def last_kernel(
    slots, cells, left, right, weights, fecundity, moves, ops, inner, partial,
    out, sides, pairs, seeds,
):
    rows, cols, cohorts = cells.shape
    near = lax.broadcasted_iota(jnp.int32, (BY, cohorts), 0) < RMAX
    gap = jnp.zeros((RMAX, cohorts), jnp.float32)

    def place(x, carry):
        sides[x, pl.ds(BY - RMAX, RMAX), :] = left[x].astype(jnp.float32)
        sides[x, pl.ds(BY, RMAX), :] = gap
        sides[x, pl.ds(BY + RMAX, RMAX), :] = right[x].astype(jnp.float32)
        for b in range(1, RMAX + 1):
            pairs[b - 1, x] = jnp.where(
                near, sides[x, pl.ds(BY - b, BY), :], sides[x, pl.ds(RMAX + b, BY), :]
            )
        return carry

    lax.fori_loop(0, rows + 2 * RMAX, place, 0, unroll=4)

    def row_sum(x, b):
        return None if b == 0 else pairs[b - 1, x]

    def one(x, carry):
        extra = weigh(x, row_sum, weights)
        both = jnp.concatenate([jnp.where(near, extra, 0.0), jnp.where(near, 0.0, extra)], axis=0)
        seeds[x] = (partial[x] + both).astype(jnp.bfloat16)
        return carry

    lax.fori_loop(0, rows, one, 0, unroll=4)
    for i in range(0, rows // BX, 2):
        span = pl.ds(i * BX, 2 * BX)
        here = cells[span].astype(jnp.float32)
        here = jnp.concatenate([here[:, :BY], here[:, cols - BY :]], axis=1).reshape(-1, cohorts)
        grown = establish(seeds[span].reshape(-1, cohorts), here, fecundity, moves)
        half = grown.shape[0] // 2
        for k in range(2):
            done = remove_pair(
                grown[k * half : (k + 1) * half], (slots[i + k, 0], slots[i + k, 3]), ops
            )
            at = pl.ds((i + k) * BX, BX)
            whole = jnp.concatenate(
                [done[:, :BY], inner[at].astype(jnp.float32), done[:, BY:]], axis=1
            )
            out[at] = whole.astype(jnp.bfloat16)


def scratch(rows, cols, cohorts, seeded=None):
    high = rows + 2 * RMAX
    return [
        pltpu.VMEM((high, cols + 2 * LEAD, cohorts), jnp.float32),
        pltpu.VMEM((RMAX, high, cols, cohorts), jnp.float32),
        pltpu.VMEM((rows, seeded or cols, cohorts), jnp.bfloat16),
    ]


def local(
    biomass, block_stand, stand_slot, tile_list, harvest_ops, transition, pattern, fecundity, radius
):
    shape = biomass.shape
    rows, cols, cohorts = shape
    count = tile_list.shape[-1]
    stands = stand_slot.shape[-1]
    state = jax.ShapeDtypeStruct(shape, jnp.bfloat16)
    operators = jax.ShapeDtypeStruct((count, cohorts, cohorts), jnp.bfloat16)

    weights = class_weights(radius)
    block_mask = jnp.repeat(jnp.repeat(pattern, TB, 0), TB, 1).astype(jnp.float32)
    moves = (transition.astype(jnp.float32) * block_mask).astype(jnp.bfloat16)
    stand_hit = block_stand[:, :, None] == jnp.arange(stands)[None, None, :]
    slots = jnp.sum(jnp.where(stand_hit, stand_slot[0, 0][None, None, :], 0), axis=-1)

    parts, around = fetch(tile_list, harvest_ops, biomass, weights, moves)
    grown = pl.pallas_call(
        first_kernel,
        out_shape=state,
        in_specs=[VMEM] * 8,
        out_specs=VMEM,
        scratch_shapes=scratch(*shape),
        compiler_params=PARAMS,
        cost_estimate=pl.CostEstimate(flops=2**28, bytes_accessed=2**24, transcendentals=0),
    )(biomass, *around, weights, fecundity, moves)
    row_part = jax.ShapeDtypeStruct((RMAX, cols, cohorts), jnp.bfloat16)
    col_part = jax.ShapeDtypeStruct((rows, RMAX, cohorts), jnp.bfloat16)
    cells, ops, first, last, head, tail = pl.pallas_call(
        harvest_kernel,
        out_shape=(state, operators, row_part, row_part, col_part, col_part),
        in_specs=[SMEM, VMEM, VMEM],
        out_specs=(VMEM,) * 6,
        compiler_params=PARAMS,
        cost_estimate=pl.CostEstimate(flops=2**28, bytes_accessed=2**22, transcendentals=0),
    )(slots, grown, parts)
    top, bottom, left, right = surround(first, last, head, tail)
    high = rows + 2 * RMAX
    outer = 2 * BY
    inner, partial = pl.pallas_call(
        middle_kernel,
        out_shape=(
            jax.ShapeDtypeStruct((rows, cols - outer, cohorts), jnp.bfloat16),
            jax.ShapeDtypeStruct((rows, outer, cohorts), jnp.float32),
        ),
        in_specs=[SMEM] + [VMEM] * 7,
        out_specs=(VMEM, VMEM),
        scratch_shapes=scratch(rows, cols, cohorts, cols - outer),
        compiler_params=PARAMS,
        cost_estimate=pl.CostEstimate(flops=2**28, bytes_accessed=2**24, transcendentals=0),
    )(slots, cells, top, bottom, weights, fecundity, moves, ops)
    return pl.pallas_call(
        last_kernel,
        out_shape=state,
        in_specs=[SMEM] + [VMEM] * 9,
        out_specs=VMEM,
        scratch_shapes=[
            pltpu.VMEM((high, outer, cohorts), jnp.float32),
            pltpu.VMEM((RMAX, high, BY, cohorts), jnp.float32),
            pltpu.VMEM((rows, outer, cohorts), jnp.bfloat16),
        ],
        compiler_params=PARAMS,
        cost_estimate=pl.CostEstimate(flops=2**28, bytes_accessed=2**22, transcendentals=0),
    )(slots, cells, left, right, weights, fecundity, moves, ops, inner, partial)


def solution(mesh):
    names = tuple(name for name, _ in SPLIT)
    sizes = tuple(size for _, size in SPLIT)
    fine = jax.sharding.Mesh(mesh.devices.reshape(sizes), names)
    placed = (
        P(ROW, COL, None),
        P(ROW, COL),
        P(ROW, COL, None),
        P(ROW, COL, None),
        P(COL, None, None),
        P(),
        P(),
        P(),
        P(),
    )
    return jax.shard_map(
        local, mesh=fine, in_specs=placed, out_specs=P(ROW, COL, None), check_vma=False
    )
```

```python
import functools
import math

import jax
import jax.numpy as jnp
from jax import lax
from jax.experimental import pallas as pl
from jax.experimental.pallas import tpu as pltpu
from jax.sharding import PartitionSpec as P

TB = 8
RMAX = 4
BX = 8
BY = 8
STEPS = 2

SPLIT = (("xl", 2), ("yh", 4), ("yl", 2), ("co", 2), ("zh", 4), ("zl", 2), ("xh", 2))
ROW = ("xl", "yh", "yl", "co")
COL = ("zh", "zl", "xh")
NEAR = ("xl", "yl", "co", "zl", "xh")
WIDE = ("xl", "yl", "co", "zh", "zl", "xh")

DIST_SQ = (0, 1, 2, 4, 5, 8, 9, 10, 13, 16)
OFFSETS = (1, 4, 4, 4, 8, 4, 4, 8, 8, 4)

VMEM = pl.BlockSpec(memory_space=pltpu.VMEM)
SMEM = pl.BlockSpec(memory_space=pltpu.SMEM)
ANY = pl.BlockSpec(memory_space=pl.ANY)
PARAMS = pltpu.CompilerParams(vmem_limit_bytes=32 * 1024 * 1024)

LEAD = 8


def shift_pairs(count):
    return [(i, i + 1) for i in range(count - 1)], [(i + 1, i) for i in range(count - 1)]


def surround(first, last, head, tail):
    down, up = shift_pairs(math.prod(lax.axis_size(name) for name in ROW))
    top, bottom = lax.ppermute(last, ROW, down), lax.ppermute(first, ROW, up)
    head = jnp.concatenate([top[:, :RMAX], head, bottom[:, :RMAX]], axis=0)
    tail = jnp.concatenate([top[:, -RMAX:], tail, bottom[:, -RMAX:]], axis=0)
    right, left = shift_pairs(math.prod(lax.axis_size(name) for name in COL))
    return top, bottom, lax.ppermute(tail, COL, right), lax.ppermute(head, COL, left)


def class_weights(radius):
    dist = jnp.array(DIST_SQ, jnp.float32)[:, None]
    reach = (radius.astype(jnp.float32) ** 2)[None, :]
    values = jnp.exp(-dist / (2.0 * reach)) * (dist <= reach).astype(jnp.float32)
    total = jnp.sum(values * jnp.array(OFFSETS, jnp.float32)[:, None], axis=0, keepdims=True)
    return values / total


def edges_kernel(cells, first, last, head, tail):
    rows, cols, _ = cells.shape
    first[...] = cells[pl.ds(0, RMAX)]
    last[...] = cells[pl.ds(rows - RMAX, RMAX)]

    def one(x, carry):
        row = cells[x].astype(jnp.float32)
        head[x] = row[:RMAX].astype(jnp.bfloat16)
        tail[x] = row[cols - RMAX :].astype(jnp.bfloat16)
        return carry

    lax.fori_loop(0, rows, one, 0, unroll=4)


def spread_kernel(listed, held, spread):
    mine = (lax.axis_index("xl") * 2 + lax.axis_index("yl")) * 2 + lax.axis_index("co")
    lane = lax.broadcasted_iota(jnp.int32, (8, 128), 1)
    names = jnp.zeros((8, 128), jnp.float32)
    for k in range(listed.shape[-1]):
        names = jnp.where(lane == k, listed[0, 0, k].astype(jnp.float32), names)
    held_at, upper = mine // 2, lax.rem(mine, 2) == 1
    for group in range(8):
        for near in range(4):
            low, half = divmod(near, 2)
            piece = held[
                held_at, pl.ds(group * 32 + low * 16, 16), pl.ds(half * 128, 128)
            ].astype(jnp.float32)
            part = jnp.where(upper, piece[8:], piece[:8])
            message = jnp.concatenate([part, names], axis=0).astype(jnp.bfloat16)
            for far in range(4):
                spread[(group * 4 + far) * 4 + near] = message


def gather_kernel(lists, arrived, left, right, weights, moves, wanted):
    del left, right, weights, moves
    members, count = wanted.shape[:2]

    def one(m, carry):
        found = []
        for k in range(count):
            name = lists[m, k]
            at = lax.rem(name, 4) * 32 + name // 4
            parts = [arrived[at + 16 * h].astype(jnp.float32)[:8] for h in range(2)]
            found.append(jnp.concatenate(parts, axis=0).astype(jnp.bfloat16))
        for k in range(count):
            wanted[m, k] = found[k]
        return carry

    lax.fori_loop(0, members, one, 0, unroll=2)


def fetch(tile_list, harvest_ops, cells, weights, moves):
    rows, cols, cohorts = cells.shape
    count = tile_list.shape[-1]
    row_part = jax.ShapeDtypeStruct((RMAX, cols, cohorts), jnp.bfloat16)
    col_part = jax.ShapeDtypeStruct((rows, RMAX, cohorts), jnp.bfloat16)
    spread = pl.pallas_call(
        spread_kernel,
        out_shape=jax.ShapeDtypeStruct((128, 16, 128), jnp.bfloat16),
        in_specs=[SMEM, VMEM],
        out_specs=VMEM,
        compiler_params=PARAMS,
        cost_estimate=pl.CostEstimate(flops=0, bytes_accessed=2**20, transcendentals=0),
    )(tile_list, harvest_ops)
    arrived = lax.all_to_all(spread, WIDE, 0, 0, tiled=True)
    first, last, head, tail = pl.pallas_call(
        edges_kernel,
        out_shape=(row_part, row_part, col_part, col_part),
        in_specs=[VMEM],
        out_specs=(VMEM,) * 4,
        compiler_params=PARAMS,
        cost_estimate=pl.CostEstimate(flops=0, bytes_accessed=2**20, transcendentals=0),
    )(cells)
    top, bottom, left, right = surround(first, last, head, tail)
    lists = lax.dynamic_index_in_dim(
        arrived.reshape(8, 4, 4, 16, 128), lax.axis_index("zh"), axis=1, keepdims=False
    )[:, :, 8, :count].astype(jnp.int32).reshape(32, count)
    wanted = pl.pallas_call(
        gather_kernel,
        out_shape=jax.ShapeDtypeStruct((32, count, 16, 128), jnp.bfloat16),
        in_specs=[SMEM, VMEM] + [ANY] * 4,
        out_specs=VMEM,
        compiler_params=PARAMS,
        cost_estimate=pl.CostEstimate(flops=0, bytes_accessed=2**21, transcendentals=0),
    )(lists, arrived, left, right, weights, moves)
    parts = lax.all_to_all(wanted, NEAR, 0, 0, tiled=True)
    return parts, (top, bottom, left, right)


def fill_rows(cells, top, bottom, padded):
    rows, cols, _ = cells.shape
    for part, start in ((top, 0), (bottom, RMAX + rows)):
        for i in range(RMAX):
            padded[start + i, pl.ds(LEAD, cols), :] = part[i].astype(jnp.float32)

    def fill(x, carry):
        padded[RMAX + x, pl.ds(LEAD, cols), :] = cells[x].astype(jnp.float32)
        return carry

    lax.fori_loop(0, rows, fill, 0, unroll=4)


def fill_sides(left, right, padded, pairs):
    high, cols, cohorts = pairs.shape[1:]

    def one(x, carry):
        if left is None:
            before = after = jnp.zeros((RMAX, cohorts), jnp.float32)
        else:
            before, after = left[x].astype(jnp.float32), right[x].astype(jnp.float32)
        padded[x, pl.ds(LEAD - RMAX, RMAX), :] = before
        padded[x, pl.ds(LEAD + cols, RMAX), :] = after
        for b in range(1, RMAX + 1):
            pairs[b - 1, x] = (
                padded[x, pl.ds(LEAD - b, cols), :] + padded[x, pl.ds(LEAD + b, cols), :]
            )
        return carry

    lax.fori_loop(0, high, one, 0, unroll=2)


def weigh(x, row_sum, weights):
    at = x + RMAX

    def both(a, b):
        low, high = row_sum(at - a, b), row_sum(at + a, b)
        return None if low is None else low + high

    sums = (
        (row_sum(at, 0),),
        (row_sum(at, 1), both(1, 0)),
        (both(1, 1),),
        (row_sum(at, 2), both(2, 0)),
        (both(2, 1), both(1, 2)),
        (both(2, 2),),
        (row_sum(at, 3), both(3, 0)),
        (both(1, 3), both(3, 1)),
        (both(2, 3), both(3, 2)),
        (row_sum(at, 4), both(4, 0)),
    )
    total = None
    for k, terms in enumerate(sums):
        terms = [term for term in terms if term is not None]
        if terms:
            value = functools.reduce(lambda p, q: p + q, terms) * weights[k : k + 1, :]
            total = value if total is None else total + value
    return total


def establish(seeds, here, fecundity, moves):
    arrived = jnp.dot(seeds, fecundity[...], preferred_element_type=jnp.float32)
    middle = (here + arrived).astype(jnp.bfloat16)
    shifted = jnp.dot(middle, moves[...], preferred_element_type=jnp.float32)
    norm = lax.rsqrt(1.0 + jnp.mean(shifted * shifted, axis=-1, keepdims=True))
    return (shifted * norm).astype(jnp.bfloat16)


def remove(flat, slot, ops):
    count = ops.shape[0]
    product = jnp.dot(flat, ops[jnp.minimum(slot, count - 1)], preferred_element_type=jnp.float32)
    return jnp.where(slot == count, flat.astype(jnp.float32), product)


def remove_pair(flat, slots, ops):
    halves = []
    for h, slot in enumerate(slots):
        product = remove(flat, slot, ops).reshape(BX, 2 * BY, flat.shape[-1])
        halves.append(product[:, h * BY : (h + 1) * BY])
    return jnp.concatenate(halves, axis=1)


def assemble(parts, ops):
    count = ops.shape[0]

    def one(k, carry):
        for piece in range(parts.shape[0]):
            r, h = divmod(piece, 2)
            ops[k, r * 16 : (r + 1) * 16, h * 128 : (h + 1) * 128] = parts[piece, k]
        return carry

    lax.fori_loop(0, count, one, 0)


def first_kernel(cells, top, bottom, left, right, weights, fecundity, moves, grown, padded, pairs, seeds):
    rows, cols, cohorts = cells.shape
    fill_rows(cells, top, bottom, padded)
    fill_sides(left, right, padded, pairs)

    def row_sum(x, b):
        return padded[x, pl.ds(LEAD, cols), :] if b == 0 else pairs[b - 1, x]

    def one(x, carry):
        seeds[x] = weigh(x, row_sum, weights).astype(jnp.bfloat16)
        return carry

    lax.fori_loop(0, rows, one, 0, unroll=2)
    for i in range(rows // BX):
        span = pl.ds(i * BX, BX)
        here = cells[span].reshape(BX * cols, cohorts).astype(jnp.float32)
        result = establish(seeds[span].reshape(BX * cols, cohorts), here, fecundity, moves)
        grown[span] = result.reshape(BX, cols, cohorts)


def harvest_kernel(slots, grown, parts, out, ops, first, last, head, tail):
    assemble(parts, ops)
    rows, cols, cohorts = grown.shape
    wide = 2 * BY
    for i in range(rows // BX):
        span = pl.ds(i * BX, BX)
        done = []
        for j in range(cols // wide):
            flat = grown[span, pl.ds(j * wide, wide), :].reshape(BX * wide, cohorts)
            done.append(remove_pair(flat, (slots[i, 2 * j], slots[i, 2 * j + 1]), ops))
        whole = jnp.concatenate(done, axis=1)
        out[span] = whole.astype(jnp.bfloat16)
        head[span] = whole[:, :RMAX].astype(jnp.bfloat16)
        tail[span] = whole[:, cols - RMAX :].astype(jnp.bfloat16)
        if i == 0:
            first[...] = whole[:RMAX].astype(jnp.bfloat16)
        if i == rows // BX - 1:
            last[...] = whole[BX - RMAX :].astype(jnp.bfloat16)


def middle_kernel(
    slots, cells, top, bottom, weights, fecundity, moves, ops, inner, partial, padded, pairs, seeds
):
    rows, cols, cohorts = cells.shape
    fill_rows(cells, top, bottom, padded)
    fill_sides(None, None, padded, pairs)

    def row_sum(x, b):
        return padded[x, pl.ds(LEAD, cols), :] if b == 0 else pairs[b - 1, x]

    def one(x, carry):
        total = weigh(x, row_sum, weights)
        partial[x] = jnp.concatenate([total[:BY], total[cols - BY :]], axis=0)
        seeds[x] = total[BY : cols - BY].astype(jnp.bfloat16)
        return carry

    lax.fori_loop(0, rows, one, 0, unroll=2)
    for i in range(0, rows // BX, 2):
        span = pl.ds(i * BX, 2 * BX)
        here = cells[span].astype(jnp.float32)[:, BY : cols - BY].reshape(-1, cohorts)
        grown = establish(seeds[span].reshape(-1, cohorts), here, fecundity, moves)
        half = grown.shape[0] // 2
        for k in range(2):
            done = remove_pair(
                grown[k * half : (k + 1) * half], (slots[i + k, 1], slots[i + k, 2]), ops
            )
            inner[pl.ds((i + k) * BX, BX)] = done.astype(jnp.bfloat16)


def last_kernel(
    slots, cells, left, right, weights, fecundity, moves, ops, inner, partial,
    out, sides, pairs, seeds,
):
    rows, cols, cohorts = cells.shape
    near = lax.broadcasted_iota(jnp.int32, (BY, cohorts), 0) < RMAX
    gap = jnp.zeros((RMAX, cohorts), jnp.float32)

    def place(x, carry):
        sides[x, pl.ds(BY - RMAX, RMAX), :] = left[x].astype(jnp.float32)
        sides[x, pl.ds(BY, RMAX), :] = gap
        sides[x, pl.ds(BY + RMAX, RMAX), :] = right[x].astype(jnp.float32)
        for b in range(1, RMAX + 1):
            pairs[b - 1, x] = jnp.where(
                near, sides[x, pl.ds(BY - b, BY), :], sides[x, pl.ds(RMAX + b, BY), :]
            )
        return carry

    lax.fori_loop(0, rows + 2 * RMAX, place, 0, unroll=4)

    def row_sum(x, b):
        return None if b == 0 else pairs[b - 1, x]

    def one(x, carry):
        extra = weigh(x, row_sum, weights)
        both = jnp.concatenate([jnp.where(near, extra, 0.0), jnp.where(near, 0.0, extra)], axis=0)
        seeds[x] = (partial[x] + both).astype(jnp.bfloat16)
        return carry

    lax.fori_loop(0, rows, one, 0, unroll=4)
    for i in range(0, rows // BX, 2):
        span = pl.ds(i * BX, 2 * BX)
        here = cells[span].astype(jnp.float32)
        here = jnp.concatenate([here[:, :BY], here[:, cols - BY :]], axis=1).reshape(-1, cohorts)
        grown = establish(seeds[span].reshape(-1, cohorts), here, fecundity, moves)
        half = grown.shape[0] // 2
        for k in range(2):
            done = remove_pair(
                grown[k * half : (k + 1) * half], (slots[i + k, 0], slots[i + k, 3]), ops
            )
            at = pl.ds((i + k) * BX, BX)
            whole = jnp.concatenate(
                [done[:, :BY], inner[at].astype(jnp.float32), done[:, BY:]], axis=1
            )
            out[at] = whole.astype(jnp.bfloat16)


def scratch(rows, cols, cohorts, seeded=None):
    high = rows + 2 * RMAX
    return [
        pltpu.VMEM((high, cols + 2 * LEAD, cohorts), jnp.float32),
        pltpu.VMEM((RMAX, high, cols, cohorts), jnp.float32),
        pltpu.VMEM((rows, seeded or cols, cohorts), jnp.bfloat16),
    ]


def local(
    biomass, block_stand, stand_slot, tile_list, harvest_ops, transition, pattern, fecundity, radius
):
    shape = biomass.shape
    rows, cols, cohorts = shape
    count = tile_list.shape[-1]
    stands = stand_slot.shape[-1]
    state = jax.ShapeDtypeStruct(shape, jnp.bfloat16)
    operators = jax.ShapeDtypeStruct((count, cohorts, cohorts), jnp.bfloat16)

    weights = class_weights(radius)
    block_mask = jnp.repeat(jnp.repeat(pattern, TB, 0), TB, 1).astype(jnp.float32)
    moves = (transition.astype(jnp.float32) * block_mask).astype(jnp.bfloat16)
    stand_hit = block_stand[:, :, None] == jnp.arange(stands)[None, None, :]
    slots = jnp.sum(jnp.where(stand_hit, stand_slot[0, 0][None, None, :], 0), axis=-1)

    parts, around = fetch(tile_list, harvest_ops, biomass, weights, moves)
    grown = pl.pallas_call(
        first_kernel,
        out_shape=state,
        in_specs=[VMEM] * 8,
        out_specs=VMEM,
        scratch_shapes=scratch(*shape),
        compiler_params=PARAMS,
        cost_estimate=pl.CostEstimate(flops=2**28, bytes_accessed=2**24, transcendentals=0),
    )(biomass, *around, weights, fecundity, moves)
    row_part = jax.ShapeDtypeStruct((RMAX, cols, cohorts), jnp.bfloat16)
    col_part = jax.ShapeDtypeStruct((rows, RMAX, cohorts), jnp.bfloat16)
    cells, ops, first, last, head, tail = pl.pallas_call(
        harvest_kernel,
        out_shape=(state, operators, row_part, row_part, col_part, col_part),
        in_specs=[SMEM, VMEM, VMEM],
        out_specs=(VMEM,) * 6,
        compiler_params=PARAMS,
        cost_estimate=pl.CostEstimate(flops=2**28, bytes_accessed=2**22, transcendentals=0),
    )(slots, grown, parts)
    top, bottom, left, right = surround(first, last, head, tail)
    high = rows + 2 * RMAX
    outer = 2 * BY
    inner, partial = pl.pallas_call(
        middle_kernel,
        out_shape=(
            jax.ShapeDtypeStruct((rows, cols - outer, cohorts), jnp.bfloat16),
            jax.ShapeDtypeStruct((rows, outer, cohorts), jnp.float32),
        ),
        in_specs=[SMEM] + [VMEM] * 7,
        out_specs=(VMEM, VMEM),
        scratch_shapes=scratch(rows, cols, cohorts, cols - outer),
        compiler_params=PARAMS,
        cost_estimate=pl.CostEstimate(flops=2**28, bytes_accessed=2**24, transcendentals=0),
    )(slots, cells, top, bottom, weights, fecundity, moves, ops)
    return pl.pallas_call(
        last_kernel,
        out_shape=state,
        in_specs=[SMEM] + [VMEM] * 9,
        out_specs=VMEM,
        scratch_shapes=[
            pltpu.VMEM((high, outer, cohorts), jnp.float32),
            pltpu.VMEM((RMAX, high, BY, cohorts), jnp.float32),
            pltpu.VMEM((rows, outer, cohorts), jnp.bfloat16),
        ],
        compiler_params=PARAMS,
        cost_estimate=pl.CostEstimate(flops=2**28, bytes_accessed=2**22, transcendentals=0),
    )(slots, cells, left, right, weights, fecundity, moves, ops, inner, partial)


def solution(mesh):
    names = tuple(name for name, _ in SPLIT)
    sizes = tuple(size for _, size in SPLIT)
    fine = jax.sharding.Mesh(mesh.devices.reshape(sizes), names)
    placed = (
        P(ROW, COL, None),
        P(ROW, COL),
        P(ROW, COL, None),
        P(ROW, COL, None),
        P(COL, None, None),
        P(),
        P(),
        P(),
        P(),
    )
    return jax.shard_map(
        local, mesh=fine, in_specs=placed, out_specs=P(ROW, COL, None), check_vma=False
    )
```

```python
import functools
import math

import jax
import jax.numpy as jnp
from jax import lax
from jax.experimental import pallas as pl
from jax.experimental.pallas import tpu as pltpu
from jax.sharding import PartitionSpec as P

TB = 8
RMAX = 4
BX = 8
BY = 8
STEPS = 2

SPLIT = (("xl", 2), ("yh", 4), ("yl", 2), ("co", 2), ("zh", 4), ("zl", 2), ("xh", 2))
ROW = ("xl", "yh", "yl", "co")
COL = ("zh", "zl", "xh")
NEAR = ("xl", "yl", "co", "zl", "xh")
WIDE = ("xl", "yl", "co", "zh", "zl", "xh")

DIST_SQ = (0, 1, 2, 4, 5, 8, 9, 10, 13, 16)
OFFSETS = (1, 4, 4, 4, 8, 4, 4, 8, 8, 4)

VMEM = pl.BlockSpec(memory_space=pltpu.VMEM)
SMEM = pl.BlockSpec(memory_space=pltpu.SMEM)
ANY = pl.BlockSpec(memory_space=pl.ANY)
PARAMS = pltpu.CompilerParams(vmem_limit_bytes=32 * 1024 * 1024)

LEAD = 8


def shift_pairs(count):
    return [(i, i + 1) for i in range(count - 1)], [(i + 1, i) for i in range(count - 1)]


def swap(head, tail, axis):
    after, before = shift_pairs(math.prod(lax.axis_size(name) for name in axis))
    return lax.ppermute(tail, axis, after), lax.ppermute(head, axis, before)


def surround(first, last, head, tail):
    top, bottom = swap(first, last, ROW)
    head = jnp.concatenate([top[:, :RMAX], head, bottom[:, :RMAX]], axis=0)
    tail = jnp.concatenate([top[:, -RMAX:], tail, bottom[:, -RMAX:]], axis=0)
    return (top, bottom) + swap(head, tail, COL)


def class_weights(radius):
    dist = jnp.array(DIST_SQ, jnp.float32)[:, None]
    reach = (radius.astype(jnp.float32) ** 2)[None, :]
    values = jnp.exp(-dist / (2.0 * reach)) * (dist <= reach).astype(jnp.float32)
    total = jnp.sum(values * jnp.array(OFFSETS, jnp.float32)[:, None], axis=0, keepdims=True)
    return values / total


def sides_kernel(cells, spread, head, tail):
    del spread
    rows, cols, _ = cells.shape

    def one(x, carry):
        row = cells[x].astype(jnp.float32)
        head[x] = row[:RMAX].astype(jnp.bfloat16)
        tail[x] = row[cols - RMAX :].astype(jnp.bfloat16)
        return carry

    lax.fori_loop(0, rows, one, 0, unroll=4)


def rows_kernel(cells, left, right, first, last):
    rows = cells.shape[0]
    for out, start in ((first, 0), (last, rows - RMAX)):
        for i in range(RMAX):
            parts = [left[start + i], cells[start + i], right[start + i]]
            whole = jnp.concatenate([part.astype(jnp.float32) for part in parts], axis=0)
            out[i] = whole.astype(jnp.bfloat16)


def spread_kernel(listed, held, spread):
    mine = (lax.axis_index("xl") * 2 + lax.axis_index("yl")) * 2 + lax.axis_index("co")
    lane = lax.broadcasted_iota(jnp.int32, (16, 128), 1)
    names = jnp.zeros((16, 128), jnp.float32)
    for k in range(listed.shape[-1]):
        names = jnp.where(lax.rem(lane, 64) == k, listed[0, 0, k].astype(jnp.float32), names)
    held_at, upper = mine // 2, lax.rem(mine, 2)
    sent = lane // 64 == upper
    for group in range(8):
        for near in range(4):
            low, half = divmod(near, 2)
            piece = held[held_at, pl.ds(group * 32 + low * 16, 16), pl.ds(half * 128, 128)]
            message = jnp.where(sent, piece.astype(jnp.float32), names).astype(jnp.bfloat16)
            for far in range(4):
                spread[(group * 4 + far) * 4 + near] = message


def gather_kernel(lists, arrived, left, right, weights, moves, wanted):
    del left, right, weights, moves
    members, count = wanted.shape[:2]
    lower = lax.broadcasted_iota(jnp.int32, (16, 128), 1) < 64

    def one(m, carry):
        found = []
        for k in range(count):
            name = lists[m, k]
            at = lax.rem(name, 4) * 32 + name // 4
            found.append(jnp.where(lower, arrived[at], arrived[at + 16]))
        for k in range(count):
            wanted[m, k] = found[k]
        return carry

    lax.fori_loop(0, members, one, 0, unroll=2)


def fetch(tile_list, harvest_ops, cells, weights, moves):
    rows, cols, cohorts = cells.shape
    count = tile_list.shape[-1]
    col_part = jax.ShapeDtypeStruct((rows, RMAX, cohorts), jnp.bfloat16)
    row_part = jax.ShapeDtypeStruct((RMAX, cols + 2 * RMAX, cohorts), jnp.bfloat16)
    small = pl.CostEstimate(flops=0, bytes_accessed=2**20, transcendentals=0)
    spread = pl.pallas_call(
        spread_kernel,
        out_shape=jax.ShapeDtypeStruct((128, 16, 128), jnp.bfloat16),
        in_specs=[SMEM, VMEM],
        out_specs=VMEM,
        compiler_params=PARAMS,
        cost_estimate=small,
    )(tile_list, harvest_ops)
    arrived = lax.all_to_all(spread, WIDE, 0, 0, tiled=True)
    head, tail = pl.pallas_call(
        sides_kernel,
        out_shape=(col_part, col_part),
        in_specs=[VMEM, ANY],
        out_specs=(VMEM,) * 2,
        compiler_params=PARAMS,
        cost_estimate=small,
    )(cells, spread)
    left, right = swap(head, tail, COL)
    first, last = pl.pallas_call(
        rows_kernel,
        out_shape=(row_part, row_part),
        in_specs=[VMEM] * 3,
        out_specs=(VMEM,) * 2,
        compiler_params=PARAMS,
        cost_estimate=small,
    )(cells, left, right)
    top, bottom = swap(first, last, ROW)
    own = lax.dynamic_index_in_dim(
        arrived.reshape(8, 4, 4, 16, 128), lax.axis_index("zh"), axis=1, keepdims=False
    )[:, :, 0].astype(jnp.int32)
    even = jnp.arange(8)[:, None, None] % 2 == 0
    lists = jnp.where(even, own[:, :, 64 : 64 + count], own[:, :, :count]).reshape(32, count)
    wanted = pl.pallas_call(
        gather_kernel,
        out_shape=jax.ShapeDtypeStruct((32, count, 16, 128), jnp.bfloat16),
        in_specs=[SMEM, VMEM] + [ANY] * 4,
        out_specs=VMEM,
        compiler_params=PARAMS,
        cost_estimate=small,
    )(lists, arrived, left, right, weights, moves)
    parts = lax.all_to_all(wanted, NEAR, 0, 0, tiled=True)
    return parts, (top, bottom, left, right)


def fill_rows(cells, top, bottom, padded):
    rows, cols, _ = cells.shape
    wide = top.shape[1]
    for part, start in ((top, 0), (bottom, RMAX + rows)):
        for i in range(RMAX):
            at = pl.ds(LEAD - (wide - cols) // 2, wide)
            padded[start + i, at, :] = part[i].astype(jnp.float32)

    def fill(x, carry):
        padded[RMAX + x, pl.ds(LEAD, cols), :] = cells[x].astype(jnp.float32)
        return carry

    lax.fori_loop(0, rows, fill, 0, unroll=4)


def fill_sides(left, right, padded):
    def one(x, carry):
        at = RMAX + x
        cols = padded.shape[1] - 2 * LEAD
        padded[at, pl.ds(LEAD - RMAX, RMAX), :] = left[x].astype(jnp.float32)
        padded[at, pl.ds(LEAD + cols, RMAX), :] = right[x].astype(jnp.float32)
        return carry

    lax.fori_loop(0, left.shape[0], one, 0, unroll=4)


def clear_sides(padded):
    gap = jnp.zeros((RMAX, padded.shape[2]), jnp.float32)

    def one(x, carry):
        padded[x, pl.ds(LEAD - RMAX, RMAX), :] = gap
        padded[x, pl.ds(padded.shape[1] - LEAD, RMAX), :] = gap
        return carry

    lax.fori_loop(0, padded.shape[0], one, 0, unroll=4)


def add_pairs(padded, pairs):
    high, cols, _ = pairs.shape[1:]

    def one(x, carry):
        for b in range(1, RMAX + 1):
            pairs[b - 1, x] = (
                padded[x, pl.ds(LEAD - b, cols), :] + padded[x, pl.ds(LEAD + b, cols), :]
            )
        return carry

    lax.fori_loop(0, high, one, 0, unroll=2)


def weigh(x, row_sum, weights):
    at = x + RMAX

    def both(a, b):
        low, high = row_sum(at - a, b), row_sum(at + a, b)
        return None if low is None else low + high

    sums = (
        (row_sum(at, 0),),
        (row_sum(at, 1), both(1, 0)),
        (both(1, 1),),
        (row_sum(at, 2), both(2, 0)),
        (both(2, 1), both(1, 2)),
        (both(2, 2),),
        (row_sum(at, 3), both(3, 0)),
        (both(1, 3), both(3, 1)),
        (both(2, 3), both(3, 2)),
        (row_sum(at, 4), both(4, 0)),
    )
    total = None
    for k, terms in enumerate(sums):
        terms = [term for term in terms if term is not None]
        if terms:
            value = functools.reduce(lambda p, q: p + q, terms) * weights[k : k + 1, :]
            total = value if total is None else total + value
    return total


def establish(seeds, here, fecundity, moves):
    arrived = jnp.dot(seeds, fecundity[...], preferred_element_type=jnp.float32)
    middle = (here + arrived).astype(jnp.bfloat16)
    shifted = jnp.dot(middle, moves[...], preferred_element_type=jnp.float32)
    norm = lax.rsqrt(1.0 + jnp.mean(shifted * shifted, axis=-1, keepdims=True))
    return (shifted * norm).astype(jnp.bfloat16)


def remove(flat, slot, ops):
    count = ops.shape[0]
    product = jnp.dot(flat, ops[jnp.minimum(slot, count - 1)], preferred_element_type=jnp.float32)
    return jnp.where(slot == count, flat.astype(jnp.float32), product)


def remove_pair(flat, slots, ops):
    halves = []
    for h, slot in enumerate(slots):
        product = remove(flat, slot, ops).reshape(BX, 2 * BY, flat.shape[-1])
        halves.append(product[:, h * BY : (h + 1) * BY])
    return jnp.concatenate(halves, axis=1)


def assemble(parts, ops):
    count = ops.shape[0]

    def one(k, carry):
        for piece in range(parts.shape[0]):
            r, h = divmod(piece, 2)
            ops[k, r * 16 : (r + 1) * 16, h * 128 : (h + 1) * 128] = parts[piece, k]
        return carry

    lax.fori_loop(0, count, one, 0)


def first_kernel(cells, top, bottom, left, right, weights, fecundity, moves, grown, padded, pairs, seeds):
    rows, cols, cohorts = cells.shape
    fill_rows(cells, top, bottom, padded)
    fill_sides(left, right, padded)
    add_pairs(padded, pairs)

    def row_sum(x, b):
        return padded[x, pl.ds(LEAD, cols), :] if b == 0 else pairs[b - 1, x]

    def one(x, carry):
        seeds[x] = weigh(x, row_sum, weights).astype(jnp.bfloat16)
        return carry

    lax.fori_loop(0, rows, one, 0, unroll=2)
    for i in range(rows // BX):
        span = pl.ds(i * BX, BX)
        here = cells[span].reshape(BX * cols, cohorts).astype(jnp.float32)
        result = establish(seeds[span].reshape(BX * cols, cohorts), here, fecundity, moves)
        grown[span] = result.reshape(BX, cols, cohorts)


def harvest_kernel(slots, grown, parts, out, ops, first, last, head, tail):
    assemble(parts, ops)
    rows, cols, cohorts = grown.shape
    wide = 2 * BY
    for i in range(rows // BX):
        span = pl.ds(i * BX, BX)
        done = []
        for j in range(cols // wide):
            flat = grown[span, pl.ds(j * wide, wide), :].reshape(BX * wide, cohorts)
            done.append(remove_pair(flat, (slots[i, 2 * j], slots[i, 2 * j + 1]), ops))
        whole = jnp.concatenate(done, axis=1)
        out[span] = whole.astype(jnp.bfloat16)
        head[span] = whole[:, :RMAX].astype(jnp.bfloat16)
        tail[span] = whole[:, cols - RMAX :].astype(jnp.bfloat16)
        if i == 0:
            first[...] = whole[:RMAX].astype(jnp.bfloat16)
        if i == rows // BX - 1:
            last[...] = whole[BX - RMAX :].astype(jnp.bfloat16)


def middle_kernel(
    slots, cells, top, bottom, weights, fecundity, moves, ops, inner, partial, padded, pairs, seeds
):
    rows, cols, cohorts = cells.shape
    fill_rows(cells, top, bottom, padded)
    clear_sides(padded)
    add_pairs(padded, pairs)

    def row_sum(x, b):
        return padded[x, pl.ds(LEAD, cols), :] if b == 0 else pairs[b - 1, x]

    def one(x, carry):
        total = weigh(x, row_sum, weights)
        partial[x] = jnp.concatenate([total[:BY], total[cols - BY :]], axis=0)
        seeds[x] = total[BY : cols - BY].astype(jnp.bfloat16)
        return carry

    lax.fori_loop(0, rows, one, 0, unroll=2)
    for i in range(0, rows // BX, 2):
        span = pl.ds(i * BX, 2 * BX)
        here = cells[span].astype(jnp.float32)[:, BY : cols - BY].reshape(-1, cohorts)
        grown = establish(seeds[span].reshape(-1, cohorts), here, fecundity, moves)
        half = grown.shape[0] // 2
        for k in range(2):
            done = remove_pair(
                grown[k * half : (k + 1) * half], (slots[i + k, 1], slots[i + k, 2]), ops
            )
            inner[pl.ds((i + k) * BX, BX)] = done.astype(jnp.bfloat16)


def last_kernel(
    slots, cells, left, right, weights, fecundity, moves, ops, inner, partial,
    out, sides, pairs, seeds,
):
    rows, cols, cohorts = cells.shape
    near = lax.broadcasted_iota(jnp.int32, (BY, cohorts), 0) < RMAX
    gap = jnp.zeros((RMAX, cohorts), jnp.float32)

    def place(x, carry):
        sides[x, pl.ds(BY - RMAX, RMAX), :] = left[x].astype(jnp.float32)
        sides[x, pl.ds(BY, RMAX), :] = gap
        sides[x, pl.ds(BY + RMAX, RMAX), :] = right[x].astype(jnp.float32)
        for b in range(1, RMAX + 1):
            pairs[b - 1, x] = jnp.where(
                near, sides[x, pl.ds(BY - b, BY), :], sides[x, pl.ds(RMAX + b, BY), :]
            )
        return carry

    lax.fori_loop(0, rows + 2 * RMAX, place, 0, unroll=4)

    def row_sum(x, b):
        return None if b == 0 else pairs[b - 1, x]

    def one(x, carry):
        extra = weigh(x, row_sum, weights)
        both = jnp.concatenate([jnp.where(near, extra, 0.0), jnp.where(near, 0.0, extra)], axis=0)
        seeds[x] = (partial[x] + both).astype(jnp.bfloat16)
        return carry

    lax.fori_loop(0, rows, one, 0, unroll=4)
    for i in range(0, rows // BX, 2):
        span = pl.ds(i * BX, 2 * BX)
        here = cells[span].astype(jnp.float32)
        here = jnp.concatenate([here[:, :BY], here[:, cols - BY :]], axis=1).reshape(-1, cohorts)
        grown = establish(seeds[span].reshape(-1, cohorts), here, fecundity, moves)
        half = grown.shape[0] // 2
        for k in range(2):
            done = remove_pair(
                grown[k * half : (k + 1) * half], (slots[i + k, 0], slots[i + k, 3]), ops
            )
            at = pl.ds((i + k) * BX, BX)
            whole = jnp.concatenate(
                [done[:, :BY], inner[at].astype(jnp.float32), done[:, BY:]], axis=1
            )
            out[at] = whole.astype(jnp.bfloat16)


def scratch(rows, cols, cohorts, seeded=None):
    high = rows + 2 * RMAX
    return [
        pltpu.VMEM((high, cols + 2 * LEAD, cohorts), jnp.float32),
        pltpu.VMEM((RMAX, high, cols, cohorts), jnp.float32),
        pltpu.VMEM((rows, seeded or cols, cohorts), jnp.bfloat16),
    ]


def local(
    biomass, block_stand, stand_slot, tile_list, harvest_ops, transition, pattern, fecundity, radius
):
    shape = biomass.shape
    rows, cols, cohorts = shape
    count = tile_list.shape[-1]
    stands = stand_slot.shape[-1]
    state = jax.ShapeDtypeStruct(shape, jnp.bfloat16)
    operators = jax.ShapeDtypeStruct((count, cohorts, cohorts), jnp.bfloat16)

    weights = class_weights(radius)
    block_mask = jnp.repeat(jnp.repeat(pattern, TB, 0), TB, 1).astype(jnp.float32)
    moves = (transition.astype(jnp.float32) * block_mask).astype(jnp.bfloat16)
    stand_hit = block_stand[:, :, None] == jnp.arange(stands)[None, None, :]
    slots = jnp.sum(jnp.where(stand_hit, stand_slot[0, 0][None, None, :], 0), axis=-1)

    parts, around = fetch(tile_list, harvest_ops, biomass, weights, moves)
    grown = pl.pallas_call(
        first_kernel,
        out_shape=state,
        in_specs=[VMEM] * 8,
        out_specs=VMEM,
        scratch_shapes=scratch(*shape),
        compiler_params=PARAMS,
        cost_estimate=pl.CostEstimate(flops=2**28, bytes_accessed=2**24, transcendentals=0),
    )(biomass, *around, weights, fecundity, moves)
    row_part = jax.ShapeDtypeStruct((RMAX, cols, cohorts), jnp.bfloat16)
    col_part = jax.ShapeDtypeStruct((rows, RMAX, cohorts), jnp.bfloat16)
    cells, ops, first, last, head, tail = pl.pallas_call(
        harvest_kernel,
        out_shape=(state, operators, row_part, row_part, col_part, col_part),
        in_specs=[SMEM, VMEM, VMEM],
        out_specs=(VMEM,) * 6,
        compiler_params=PARAMS,
        cost_estimate=pl.CostEstimate(flops=2**28, bytes_accessed=2**22, transcendentals=0),
    )(slots, grown, parts)
    top, bottom, left, right = surround(first, last, head, tail)
    high = rows + 2 * RMAX
    outer = 2 * BY
    inner, partial = pl.pallas_call(
        middle_kernel,
        out_shape=(
            jax.ShapeDtypeStruct((rows, cols - outer, cohorts), jnp.bfloat16),
            jax.ShapeDtypeStruct((rows, outer, cohorts), jnp.float32),
        ),
        in_specs=[SMEM] + [VMEM] * 7,
        out_specs=(VMEM, VMEM),
        scratch_shapes=scratch(rows, cols, cohorts, cols - outer),
        compiler_params=PARAMS,
        cost_estimate=pl.CostEstimate(flops=2**28, bytes_accessed=2**24, transcendentals=0),
    )(slots, cells, top, bottom, weights, fecundity, moves, ops)
    return pl.pallas_call(
        last_kernel,
        out_shape=state,
        in_specs=[SMEM] + [VMEM] * 9,
        out_specs=VMEM,
        scratch_shapes=[
            pltpu.VMEM((high, outer, cohorts), jnp.float32),
            pltpu.VMEM((RMAX, high, BY, cohorts), jnp.float32),
            pltpu.VMEM((rows, outer, cohorts), jnp.bfloat16),
        ],
        compiler_params=PARAMS,
        cost_estimate=pl.CostEstimate(flops=2**28, bytes_accessed=2**22, transcendentals=0),
    )(slots, cells, left, right, weights, fecundity, moves, ops, inner, partial)


def solution(mesh):
    names = tuple(name for name, _ in SPLIT)
    sizes = tuple(size for _, size in SPLIT)
    fine = jax.sharding.Mesh(mesh.devices.reshape(sizes), names)
    placed = (
        P(ROW, COL, None),
        P(ROW, COL),
        P(ROW, COL, None),
        P(ROW, COL, None),
        P(COL, None, None),
        P(),
        P(),
        P(),
        P(),
    )
    return jax.shard_map(
        local, mesh=fine, in_specs=placed, out_specs=P(ROW, COL, None), check_vma=False
    )
```

```python
import functools
import math

import jax
import jax.numpy as jnp
from jax import lax
from jax.experimental import pallas as pl
from jax.experimental.pallas import tpu as pltpu
from jax.sharding import PartitionSpec as P

TB = 8
RMAX = 4
BX = 8
BY = 8
STEPS = 2

SPLIT = (("xl", 2), ("yh", 4), ("yl", 2), ("co", 2), ("zh", 4), ("zl", 2), ("xh", 2))
ROW = ("xl", "yh", "yl", "co")
COL = ("zh", "zl", "xh")
NEAR = ("xl", "yl", "co", "zl", "xh")
WIDE = ("xl", "yl", "co", "zh", "zl", "xh")

DIST_SQ = (0, 1, 2, 4, 5, 8, 9, 10, 13, 16)
OFFSETS = (1, 4, 4, 4, 8, 4, 4, 8, 8, 4)

VMEM = pl.BlockSpec(memory_space=pltpu.VMEM)
SMEM = pl.BlockSpec(memory_space=pltpu.SMEM)
ANY = pl.BlockSpec(memory_space=pl.ANY)
HBM = pl.BlockSpec(memory_space=pltpu.HBM)
PARAMS = pltpu.CompilerParams(vmem_limit_bytes=32 * 1024 * 1024)

LEAD = 8


def shift_pairs(count):
    return [(i, i + 1) for i in range(count - 1)], [(i + 1, i) for i in range(count - 1)]


def swap(head, tail, axis):
    after, before = shift_pairs(math.prod(lax.axis_size(name) for name in axis))
    return lax.ppermute(tail, axis, after), lax.ppermute(head, axis, before)


def class_weights(radius):
    dist = jnp.array(DIST_SQ, jnp.float32)[:, None]
    reach = (radius.astype(jnp.float32) ** 2)[None, :]
    values = jnp.exp(-dist / (2.0 * reach)) * (dist <= reach).astype(jnp.float32)
    total = jnp.sum(values * jnp.array(OFFSETS, jnp.float32)[:, None], axis=0, keepdims=True)
    return values / total


def sides_kernel(cells, spread, head, tail):
    del spread
    rows, cols, _ = cells.shape

    def one(x, carry):
        row = cells[x].astype(jnp.float32)
        head[x] = row[:RMAX].astype(jnp.bfloat16)
        tail[x] = row[cols - RMAX :].astype(jnp.bfloat16)
        return carry

    lax.fori_loop(0, rows, one, 0, unroll=4)


def rows_kernel(cells, left, right, first, last):
    rows = cells.shape[0]
    for out, start in ((first, 0), (last, rows - RMAX)):
        for i in range(RMAX):
            parts = [left[start + i], cells[start + i], right[start + i]]
            whole = jnp.concatenate([part.astype(jnp.float32) for part in parts], axis=0)
            out[i] = whole.astype(jnp.bfloat16)


def spread_kernel(tile_list, harvest_ops, spread, listed, held, sems):
    mine = (lax.axis_index("xl") * 2 + lax.axis_index("yl")) * 2 + lax.axis_index("co")
    list_copy = pltpu.make_async_copy(tile_list, listed, sems.at[0])
    held_copy = pltpu.make_async_copy(harvest_ops.at[mine // 2], held, sems.at[1])
    list_copy.start()
    held_copy.start()
    list_copy.wait()
    lane = lax.broadcasted_iota(jnp.int32, (16, 128), 1)
    names = jnp.zeros((16, 128), jnp.float32)
    for k in range(listed.shape[-1]):
        names = jnp.where(lax.rem(lane, 64) == k, listed[0, 0, k].astype(jnp.float32), names)
    sent = lane // 64 == lax.rem(mine, 2)
    held_copy.wait()
    for group in range(8):
        for near in range(4):
            low, half = divmod(near, 2)
            piece = held[pl.ds(group * 32 + low * 16, 16), pl.ds(half * 128, 128)]
            message = jnp.where(sent, piece.astype(jnp.float32), names).astype(jnp.bfloat16)
            for far in range(4):
                spread[(group * 4 + far) * 4 + near] = message


def gather_kernel(places, arrived, left, right, weights, moves, wanted):
    del left, right, weights, moves
    members, count = wanted.shape[:2]
    lower = lax.broadcasted_iota(jnp.int32, (16, 128), 1) < 64

    def one(m, carry):
        found = []
        for k in range(count):
            at = places[m, k]
            found.append(jnp.where(lower, arrived[at], arrived[at + 16]))
        for k in range(count):
            wanted[m, k] = found[k]
        return carry

    lax.fori_loop(0, members, one, 0, unroll=2)


def fetch(tile_list, harvest_ops, cells, weights, moves):
    rows, cols, cohorts = cells.shape
    count = tile_list.shape[-1]
    col_part = jax.ShapeDtypeStruct((rows, RMAX, cohorts), jnp.bfloat16)
    row_part = jax.ShapeDtypeStruct((RMAX, cols + 2 * RMAX, cohorts), jnp.bfloat16)
    small = pl.CostEstimate(flops=0, bytes_accessed=2**20, transcendentals=0)
    spread = pl.pallas_call(
        spread_kernel,
        out_shape=jax.ShapeDtypeStruct((128, 16, 128), jnp.bfloat16),
        in_specs=[HBM, HBM],
        out_specs=VMEM,
        scratch_shapes=[
            pltpu.SMEM(tile_list.shape, jnp.int32),
            pltpu.VMEM((cohorts, cohorts), jnp.bfloat16),
            pltpu.SemaphoreType.DMA((2,)),
        ],
        compiler_params=PARAMS,
        cost_estimate=small,
    )(tile_list, harvest_ops)
    arrived = lax.all_to_all(spread, WIDE, 0, 0, tiled=True)
    head, tail = pl.pallas_call(
        sides_kernel,
        out_shape=(col_part, col_part),
        in_specs=[VMEM, ANY],
        out_specs=(VMEM,) * 2,
        compiler_params=PARAMS,
        cost_estimate=small,
    )(cells, spread)
    left, right = swap(head, tail, COL)
    first, last = pl.pallas_call(
        rows_kernel,
        out_shape=(row_part, row_part),
        in_specs=[VMEM] * 3,
        out_specs=(VMEM,) * 2,
        compiler_params=PARAMS,
        cost_estimate=small,
    )(cells, left, right)
    top, bottom = swap(first, last, ROW)
    own = lax.dynamic_index_in_dim(
        arrived.reshape(8, 4, 4, 16, 128), lax.axis_index("zh"), axis=1, keepdims=False
    )[:, :, 0].astype(jnp.int32)
    even = jnp.arange(8)[:, None, None] % 2 == 0
    lists = jnp.where(even, own[:, :, 64 : 64 + count], own[:, :, :count])
    places = (lists % 4 * 32 + lists // 4).reshape(32, count)
    wanted = pl.pallas_call(
        gather_kernel,
        out_shape=jax.ShapeDtypeStruct((32, count, 16, 128), jnp.bfloat16),
        in_specs=[SMEM, VMEM] + [ANY] * 4,
        out_specs=VMEM,
        compiler_params=PARAMS,
        cost_estimate=small,
    )(places, arrived, left, right, weights, moves)
    parts = lax.all_to_all(wanted, NEAR, 0, 0, tiled=True)
    return parts, (top, bottom, left, right)


def fill_rows(cells, top, bottom, padded):
    rows, cols, _ = cells.shape
    wide = top.shape[1]
    for part, start in ((top, 0), (bottom, RMAX + rows)):
        for i in range(RMAX):
            at = pl.ds(LEAD - (wide - cols) // 2, wide)
            padded[start + i, at, :] = part[i].astype(jnp.float32)

    def fill(x, carry):
        padded[RMAX + x, pl.ds(LEAD, cols), :] = cells[x].astype(jnp.float32)
        return carry

    lax.fori_loop(0, rows, fill, 0, unroll=4)


def fill_sides(left, right, padded):
    def one(x, carry):
        at = RMAX + x
        cols = padded.shape[1] - 2 * LEAD
        padded[at, pl.ds(LEAD - RMAX, RMAX), :] = left[x].astype(jnp.float32)
        padded[at, pl.ds(LEAD + cols, RMAX), :] = right[x].astype(jnp.float32)
        return carry

    lax.fori_loop(0, left.shape[0], one, 0, unroll=4)


def clear_sides(padded):
    gap = jnp.zeros((RMAX, padded.shape[2]), jnp.float32)

    def one(x, carry):
        padded[x, pl.ds(LEAD - RMAX, RMAX), :] = gap
        padded[x, pl.ds(padded.shape[1] - LEAD, RMAX), :] = gap
        return carry

    lax.fori_loop(0, padded.shape[0], one, 0, unroll=4)


def add_pairs(padded, pairs):
    high, cols, _ = pairs.shape[1:]

    def one(x, carry):
        for b in range(1, RMAX + 1):
            pairs[b - 1, x] = (
                padded[x, pl.ds(LEAD - b, cols), :] + padded[x, pl.ds(LEAD + b, cols), :]
            )
        return carry

    lax.fori_loop(0, high, one, 0, unroll=2)


def weigh(x, row_sum, weights):
    at = x + RMAX

    def both(a, b):
        low, high = row_sum(at - a, b), row_sum(at + a, b)
        return None if low is None else low + high

    sums = (
        (row_sum(at, 0),),
        (row_sum(at, 1), both(1, 0)),
        (both(1, 1),),
        (row_sum(at, 2), both(2, 0)),
        (both(2, 1), both(1, 2)),
        (both(2, 2),),
        (row_sum(at, 3), both(3, 0)),
        (both(1, 3), both(3, 1)),
        (both(2, 3), both(3, 2)),
        (row_sum(at, 4), both(4, 0)),
    )
    total = None
    for k, terms in enumerate(sums):
        terms = [term for term in terms if term is not None]
        if terms:
            value = functools.reduce(lambda p, q: p + q, terms) * weights[k : k + 1, :]
            total = value if total is None else total + value
    return total


def establish(seeds, here, fecundity, moves):
    arrived = jnp.dot(seeds, fecundity[...], preferred_element_type=jnp.float32)
    middle = (here + arrived).astype(jnp.bfloat16)
    shifted = jnp.dot(middle, moves[...], preferred_element_type=jnp.float32)
    norm = lax.rsqrt(1.0 + jnp.mean(shifted * shifted, axis=-1, keepdims=True))
    return (shifted * norm).astype(jnp.bfloat16)


def remove(flat, slot, ops):
    count = ops.shape[0]
    product = jnp.dot(flat, ops[jnp.minimum(slot, count - 1)], preferred_element_type=jnp.float32)
    return jnp.where(slot == count, flat.astype(jnp.float32), product)


def remove_pair(flat, slots, ops):
    halves = []
    for h, slot in enumerate(slots):
        product = remove(flat, slot, ops).reshape(BX, 2 * BY, flat.shape[-1])
        halves.append(product[:, h * BY : (h + 1) * BY])
    return jnp.concatenate(halves, axis=1)


def assemble(parts, ops):
    count = ops.shape[0]

    def one(k, carry):
        for piece in range(parts.shape[0]):
            r, h = divmod(piece, 2)
            ops[k, r * 16 : (r + 1) * 16, h * 128 : (h + 1) * 128] = parts[piece, k]
        return carry

    lax.fori_loop(0, count, one, 0)


def first_kernel(cells, top, bottom, left, right, weights, fecundity, moves, grown, padded, pairs, seeds):
    rows, cols, cohorts = cells.shape
    fill_rows(cells, top, bottom, padded)
    fill_sides(left, right, padded)
    add_pairs(padded, pairs)

    def row_sum(x, b):
        return padded[x, pl.ds(LEAD, cols), :] if b == 0 else pairs[b - 1, x]

    def one(x, carry):
        seeds[x] = weigh(x, row_sum, weights).astype(jnp.bfloat16)
        return carry

    lax.fori_loop(0, rows, one, 0, unroll=2)
    for i in range(rows // BX):
        span = pl.ds(i * BX, BX)
        here = cells[span].reshape(BX * cols, cohorts).astype(jnp.float32)
        result = establish(seeds[span].reshape(BX * cols, cohorts), here, fecundity, moves)
        grown[span] = result.reshape(BX, cols, cohorts)


def harvest_kernel(slots, grown, parts, out, ops, last, head, tail):
    assemble(parts, ops)
    rows, cols, cohorts = grown.shape
    wide = 2 * BY
    for i in range(rows // BX):
        span = pl.ds(i * BX, BX)
        done = []
        for j in range(cols // wide):
            flat = grown[span, pl.ds(j * wide, wide), :].reshape(BX * wide, cohorts)
            done.append(remove_pair(flat, (slots[i, 2 * j], slots[i, 2 * j + 1]), ops))
        whole = jnp.concatenate(done, axis=1)
        out[span] = whole.astype(jnp.bfloat16)
        head[span] = whole[:, :RMAX].astype(jnp.bfloat16)
        tail[span] = whole[:, cols - RMAX :].astype(jnp.bfloat16)
        if i == rows // BX - 1:
            last[...] = whole[BX - RMAX :].astype(jnp.bfloat16)


def clear_and_pair(padded, pairs):
    clear_sides(padded)
    add_pairs(padded, pairs)


def split_row(total):
    cols = total.shape[0]
    outer = jnp.concatenate([total[:BY], total[cols - BY :]], axis=0)
    return outer, total[BY : cols - BY].astype(jnp.bfloat16)


def inner_rows_kernel(cells, weights, first, partial, seeds, padded, pairs):
    rows, cols, _ = cells.shape
    first[...] = cells[pl.ds(0, RMAX)]

    def fill(x, carry):
        padded[x, pl.ds(LEAD, cols), :] = cells[x].astype(jnp.float32)
        return carry

    lax.fori_loop(0, rows, fill, 0, unroll=4)
    clear_and_pair(padded, pairs)

    def row_sum(x, b):
        return padded[x - RMAX, pl.ds(LEAD, cols), :] if b == 0 else pairs[b - 1, x - RMAX]

    def one(i, carry):
        partial[i], seeds[i] = split_row(weigh(i + RMAX, row_sum, weights))
        return carry

    lax.fori_loop(0, rows - 2 * RMAX, one, 0, unroll=2)


def outer_rows_kernel(cells, top, bottom, own_head, weights, head, partial, seeds, padded, pairs):
    rows, cols, _ = cells.shape
    head[pl.ds(RMAX, rows)] = own_head[...]
    for part, start in ((top, 0), (bottom, RMAX + rows)):
        for i in range(RMAX):
            head[start + i] = part[i].astype(jnp.float32)[:RMAX].astype(jnp.bfloat16)
    for i in range(RMAX):
        padded[i, pl.ds(LEAD, cols), :] = top[i].astype(jnp.float32)
        padded[5 * RMAX + i, pl.ds(LEAD, cols), :] = bottom[i].astype(jnp.float32)
    for i in range(2 * RMAX):
        padded[RMAX + i, pl.ds(LEAD, cols), :] = cells[i].astype(jnp.float32)
        padded[3 * RMAX + i, pl.ds(LEAD, cols), :] = cells[rows - 2 * RMAX + i].astype(jnp.float32)
    clear_and_pair(padded, pairs)

    def row_sum(x, b):
        return padded[x, pl.ds(LEAD, cols), :] if b == 0 else pairs[b - 1, x]

    def one(i, carry):
        for h in range(2):
            total = weigh(i + 3 * RMAX * h, row_sum, weights)
            partial[i + RMAX * h], seeds[i + RMAX * h] = split_row(total)
        return carry

    lax.fori_loop(0, RMAX, one, 0)


def inner_blocks_kernel(slots, cells, seeds_in, seeds_out, fecundity, moves, ops, inner):
    rows, cols, cohorts = cells.shape
    half = rows // 2
    for h in range(2):
        span = pl.ds(h * half, half)
        middle = seeds_in[pl.ds(h * (half - RMAX), half - RMAX)]
        edge = seeds_out[pl.ds(h * RMAX, RMAX)]
        seeds = jnp.concatenate([middle, edge] if h else [edge, middle], axis=0)
        here = cells[span].astype(jnp.float32)[:, BY : cols - BY].reshape(-1, cohorts)
        grown = establish(seeds.reshape(-1, cohorts), here, fecundity, moves)
        size = 2 * BY * BX
        for k in range(half // BX):
            i = h * (half // BX) + k
            done = remove_pair(grown[k * size : (k + 1) * size], (slots[i, 1], slots[i, 2]), ops)
            inner[pl.ds(i * BX, BX)] = done.astype(jnp.bfloat16)


def last_kernel(
    slots, cells, left, right, weights, fecundity, moves, ops, inner, partial_in, partial_out,
    out, sides, pairs, seeds,
):
    rows, cols, cohorts = cells.shape
    near = lax.broadcasted_iota(jnp.int32, (BY, cohorts), 0) < RMAX
    gap = jnp.zeros((RMAX, cohorts), jnp.float32)

    def place(x, carry):
        sides[x, pl.ds(BY - RMAX, RMAX), :] = left[x].astype(jnp.float32)
        sides[x, pl.ds(BY, RMAX), :] = gap
        sides[x, pl.ds(BY + RMAX, RMAX), :] = right[x].astype(jnp.float32)
        for b in range(1, RMAX + 1):
            pairs[b - 1, x] = jnp.where(
                near, sides[x, pl.ds(BY - b, BY), :], sides[x, pl.ds(RMAX + b, BY), :]
            )
        return carry

    lax.fori_loop(0, rows + 2 * RMAX, place, 0, unroll=4)

    def row_sum(x, b):
        return None if b == 0 else pairs[b - 1, x]

    def add(x, partial):
        extra = weigh(x, row_sum, weights)
        both = jnp.concatenate([jnp.where(near, extra, 0.0), jnp.where(near, 0.0, extra)], axis=0)
        seeds[x] = (partial + both).astype(jnp.bfloat16)

    def one(i, carry):
        add(i + RMAX, partial_in[i])
        return carry

    lax.fori_loop(0, rows - 2 * RMAX, one, 0, unroll=4)
    for i in range(RMAX):
        add(i, partial_out[i])
        add(rows - RMAX + i, partial_out[RMAX + i])
    for i in range(0, rows // BX, 2):
        span = pl.ds(i * BX, 2 * BX)
        here = cells[span].astype(jnp.float32)
        here = jnp.concatenate([here[:, :BY], here[:, cols - BY :]], axis=1).reshape(-1, cohorts)
        grown = establish(seeds[span].reshape(-1, cohorts), here, fecundity, moves)
        half = grown.shape[0] // 2
        for k in range(2):
            done = remove_pair(
                grown[k * half : (k + 1) * half], (slots[i + k, 0], slots[i + k, 3]), ops
            )
            at = pl.ds((i + k) * BX, BX)
            whole = jnp.concatenate(
                [done[:, :BY], inner[at].astype(jnp.float32), done[:, BY:]], axis=1
            )
            out[at] = whole.astype(jnp.bfloat16)


def scratch(rows, cols, cohorts):
    high = rows + 2 * RMAX
    return [
        pltpu.VMEM((high, cols + 2 * LEAD, cohorts), jnp.float32),
        pltpu.VMEM((RMAX, high, cols, cohorts), jnp.float32),
        pltpu.VMEM((rows, cols, cohorts), jnp.bfloat16),
    ]


def local(
    biomass, block_stand, stand_slot, tile_list, harvest_ops, transition, pattern, fecundity, radius
):
    shape = biomass.shape
    rows, cols, cohorts = shape
    count = tile_list.shape[-1]
    stands = stand_slot.shape[-1]
    state = jax.ShapeDtypeStruct(shape, jnp.bfloat16)
    operators = jax.ShapeDtypeStruct((count, cohorts, cohorts), jnp.bfloat16)

    weights = class_weights(radius)
    block_mask = jnp.repeat(jnp.repeat(pattern, TB, 0), TB, 1).astype(jnp.float32)
    moves = (transition.astype(jnp.float32) * block_mask).astype(jnp.bfloat16)
    stand_hit = block_stand[:, :, None] == jnp.arange(stands)[None, None, :]
    slots = jnp.sum(jnp.where(stand_hit, stand_slot[0, 0][None, None, :], 0), axis=-1)

    parts, around = fetch(tile_list, harvest_ops, biomass, weights, moves)
    grown = pl.pallas_call(
        first_kernel,
        out_shape=state,
        in_specs=[VMEM] * 8,
        out_specs=VMEM,
        scratch_shapes=scratch(*shape),
        compiler_params=PARAMS,
        cost_estimate=pl.CostEstimate(flops=2**28, bytes_accessed=2**24, transcendentals=0),
    )(biomass, *around, weights, fecundity, moves)
    row_part = jax.ShapeDtypeStruct((RMAX, cols, cohorts), jnp.bfloat16)
    col_part = jax.ShapeDtypeStruct((rows, RMAX, cohorts), jnp.bfloat16)
    cells, ops, last, own_head, tail = pl.pallas_call(
        harvest_kernel,
        out_shape=(state, operators, row_part, col_part, col_part),
        in_specs=[SMEM, VMEM, VMEM],
        out_specs=(VMEM,) * 5,
        compiler_params=PARAMS,
        cost_estimate=pl.CostEstimate(flops=2**28, bytes_accessed=2**22, transcendentals=0),
    )(slots, grown, parts)
    high = rows + 2 * RMAX
    outer = 2 * BY
    few = 2 * RMAX

    def halves(count):
        return (
            jax.ShapeDtypeStruct((count, outer, cohorts), jnp.float32),
            jax.ShapeDtypeStruct((count, cols - outer, cohorts), jnp.bfloat16),
        )

    def room(count):
        return [
            pltpu.VMEM((count, cols + 2 * LEAD, cohorts), jnp.float32),
            pltpu.VMEM((RMAX, count, cols, cohorts), jnp.float32),
        ]

    work = pl.CostEstimate(flops=2**28, bytes_accessed=2**23, transcendentals=0)
    first, partial_in, seeds_in = pl.pallas_call(
        inner_rows_kernel,
        out_shape=(row_part,) + halves(rows - few),
        in_specs=[VMEM] * 2,
        out_specs=(VMEM,) * 3,
        scratch_shapes=room(rows),
        compiler_params=PARAMS,
        cost_estimate=work,
    )(cells, weights)
    top, bottom = swap(first, last, ROW)
    tail = jnp.concatenate([top[:, -RMAX:], tail, bottom[:, -RMAX:]], axis=0)
    head, partial_out, seeds_out = pl.pallas_call(
        outer_rows_kernel,
        out_shape=(jax.ShapeDtypeStruct((high, RMAX, cohorts), jnp.bfloat16),) + halves(few),
        in_specs=[VMEM] * 5,
        out_specs=(VMEM,) * 3,
        scratch_shapes=room(3 * few),
        compiler_params=PARAMS,
        cost_estimate=work,
    )(cells, top, bottom, own_head, weights)
    left, right = swap(head, tail, COL)
    inner = pl.pallas_call(
        inner_blocks_kernel,
        out_shape=jax.ShapeDtypeStruct((rows, cols - outer, cohorts), jnp.bfloat16),
        in_specs=[SMEM] + [VMEM] * 6,
        out_specs=VMEM,
        compiler_params=PARAMS,
        cost_estimate=work,
    )(slots, cells, seeds_in, seeds_out, fecundity, moves, ops)
    return pl.pallas_call(
        last_kernel,
        out_shape=state,
        in_specs=[SMEM] + [VMEM] * 10,
        out_specs=VMEM,
        scratch_shapes=[
            pltpu.VMEM((high, outer, cohorts), jnp.float32),
            pltpu.VMEM((RMAX, high, BY, cohorts), jnp.float32),
            pltpu.VMEM((rows, outer, cohorts), jnp.bfloat16),
        ],
        compiler_params=PARAMS,
        cost_estimate=pl.CostEstimate(flops=2**28, bytes_accessed=2**22, transcendentals=0),
    )(slots, cells, left, right, weights, fecundity, moves, ops, inner, partial_in, partial_out)


def solution(mesh):
    names = tuple(name for name, _ in SPLIT)
    sizes = tuple(size for _, size in SPLIT)
    fine = jax.sharding.Mesh(mesh.devices.reshape(sizes), names)
    placed = (
        P(ROW, COL, None),
        P(ROW, COL),
        P(ROW, COL, None),
        P(ROW, COL, None),
        P(COL, None, None),
        P(),
        P(),
        P(),
        P(),
    )
    return jax.shard_map(
        local, mesh=fine, in_specs=placed, out_specs=P(ROW, COL, None), check_vma=False
    )
```

```python
import functools
import math

import jax
import jax.numpy as jnp
from jax import lax
from jax.experimental import pallas as pl
from jax.experimental.pallas import tpu as pltpu
from jax.sharding import PartitionSpec as P

TB = 8
RMAX = 4
BX = 8
BY = 8
STEPS = 2

SPLIT = (("xl", 2), ("yh", 4), ("yl", 2), ("co", 2), ("zh", 4), ("zl", 2), ("xh", 2))
ROW = ("xl", "yh", "yl", "co")
COL = ("zh", "zl", "xh")
NEAR = ("xl", "yl", "co", "zl", "xh")
WIDE = ("xl", "yl", "co", "zh", "zl", "xh")

DIST_SQ = (0, 1, 2, 4, 5, 8, 9, 10, 13, 16)
OFFSETS = (1, 4, 4, 4, 8, 4, 4, 8, 8, 4)

VMEM = pl.BlockSpec(memory_space=pltpu.VMEM)
SMEM = pl.BlockSpec(memory_space=pltpu.SMEM)
ANY = pl.BlockSpec(memory_space=pl.ANY)
PARAMS = pltpu.CompilerParams(vmem_limit_bytes=32 * 1024 * 1024)
WHOLE = pltpu.CompilerParams(vmem_limit_bytes=60 * 1024 * 1024)

LEAD = 8


def shift_pairs(count):
    return [(i, i + 1) for i in range(count - 1)], [(i + 1, i) for i in range(count - 1)]


def swap(head, tail, axis):
    after, before = shift_pairs(math.prod(lax.axis_size(name) for name in axis))
    return lax.ppermute(tail, axis, after), lax.ppermute(head, axis, before)


def surround(near, far, head, tail):
    even = lax.axis_index("co") == 0
    count = math.prod(lax.axis_size(name) for name in ROW)
    pairs = [(i, i + 1) for i in range(1, count - 1, 2)]
    far = lax.ppermute(far, ROW, pairs + [(j, i) for i, j in pairs])
    near = lax.all_to_all(near, "co", 0, 0, tiled=True)
    near = jnp.where(even, near[1], near[0])
    top, bottom = jnp.where(even, far, near), jnp.where(even, near, far)
    head = jnp.concatenate([top[:, :RMAX], head, bottom[:, :RMAX]], axis=0)
    tail = jnp.concatenate([top[:, -RMAX:], tail, bottom[:, -RMAX:]], axis=0)
    return (top, bottom) + swap(head, tail, COL)


def class_weights(radius):
    dist = jnp.array(DIST_SQ, jnp.float32)[:, None]
    reach = (radius.astype(jnp.float32) ** 2)[None, :]
    values = jnp.exp(-dist / (2.0 * reach)) * (dist <= reach).astype(jnp.float32)
    total = jnp.sum(values * jnp.array(OFFSETS, jnp.float32)[:, None], axis=0, keepdims=True)
    return values / total


def sides_kernel(cells, token, head, tail):
    del token
    rows, cols, _ = cells.shape

    def one(x, carry):
        row = cells[x].astype(jnp.float32)
        head[x] = row[:RMAX].astype(jnp.bfloat16)
        tail[x] = row[cols - RMAX :].astype(jnp.bfloat16)
        return carry

    lax.fori_loop(0, rows, one, 0, unroll=4)


def rows_kernel(cells, left, right, first, last):
    rows = cells.shape[0]
    for out, start in ((first, 0), (last, rows - RMAX)):
        for i in range(RMAX):
            parts = [left[start + i], cells[start + i], right[start + i]]
            whole = jnp.concatenate([part.astype(jnp.float32) for part in parts], axis=0)
            out[i] = whole.astype(jnp.bfloat16)


def spread_kernel(tile_list, harvest_ops, spread, token, listed, held, sems):
    mine = (lax.axis_index("xl") * 2 + lax.axis_index("yl")) * 2 + lax.axis_index("co")
    list_copy = pltpu.make_async_copy(tile_list, listed, sems.at[0])
    held_copy = pltpu.make_async_copy(harvest_ops.at[mine // 2], held, sems.at[1])
    list_copy.start()
    held_copy.start()
    list_copy.wait()
    lane = lax.broadcasted_iota(jnp.int32, (16, 128), 1)
    names = jnp.zeros((16, 128), jnp.float32)
    for k in range(listed.shape[-1]):
        names = jnp.where(lax.rem(lane, 64) == k, listed[0, 0, k].astype(jnp.float32), names)
    sent = lane // 64 == lax.rem(mine, 2)
    token[...] = jnp.zeros_like(token)
    held_copy.wait()
    for group in range(8):
        for near in range(4):
            low, half = divmod(near, 2)
            piece = held[pl.ds(group * 32 + low * 16, 16), pl.ds(half * 128, 128)]
            message = jnp.where(sent, piece.astype(jnp.float32), names).astype(jnp.bfloat16)
            for far in range(4):
                spread[(group * 4 + far) * 4 + near] = message


def gather_kernel(places, arrived, left, right, weights, moves, wanted):
    del left, right, weights, moves
    members, count = wanted.shape[:2]
    lower = lax.broadcasted_iota(jnp.int32, (16, 128), 1) < 64

    def one(m, carry):
        found = []
        for k in range(count):
            at = places[m, k]
            found.append(jnp.where(lower, arrived[at], arrived[at + 16]))
        for k in range(count):
            wanted[m, k] = found[k]
        return carry

    lax.fori_loop(0, members, one, 0, unroll=2)


def fetch(tile_list, harvest_ops, cells, weights, moves):
    rows, cols, cohorts = cells.shape
    count = tile_list.shape[-1]
    col_part = jax.ShapeDtypeStruct((rows, RMAX, cohorts), jnp.bfloat16)
    row_part = jax.ShapeDtypeStruct((RMAX, cols + 2 * RMAX, cohorts), jnp.bfloat16)
    small = pl.CostEstimate(flops=0, bytes_accessed=2**20, transcendentals=0)
    spread, token = pl.pallas_call(
        spread_kernel,
        out_shape=(
            jax.ShapeDtypeStruct((128, 16, 128), jnp.bfloat16),
            jax.ShapeDtypeStruct((8, 128), jnp.float32),
        ),
        in_specs=[ANY, ANY],
        out_specs=(VMEM, VMEM),
        scratch_shapes=[
            pltpu.SMEM(tile_list.shape, jnp.int32),
            pltpu.VMEM((cohorts, cohorts), jnp.bfloat16),
            pltpu.SemaphoreType.DMA((2,)),
        ],
        compiler_params=WHOLE,
        cost_estimate=small,
    )(tile_list, harvest_ops)
    arrived = lax.all_to_all(spread, WIDE, 0, 0, tiled=True)
    head, tail = pl.pallas_call(
        sides_kernel,
        out_shape=(col_part, col_part),
        in_specs=[VMEM, ANY],
        out_specs=(VMEM,) * 2,
        compiler_params=PARAMS,
        cost_estimate=small,
    )(cells, token)
    left, right = swap(head, tail, COL)
    first, last = pl.pallas_call(
        rows_kernel,
        out_shape=(row_part, row_part),
        in_specs=[VMEM] * 3,
        out_specs=(VMEM,) * 2,
        compiler_params=PARAMS,
        cost_estimate=small,
    )(cells, left, right)
    top, bottom = swap(first, last, ROW)
    own = lax.dynamic_index_in_dim(
        arrived.reshape(8, 4, 4, 16, 128), lax.axis_index("zh"), axis=1, keepdims=False
    )[:, :, 0].astype(jnp.int32)
    even = jnp.arange(8)[:, None, None] % 2 == 0
    lists = jnp.where(even, own[:, :, 64 : 64 + count], own[:, :, :count])
    places = (lists % 4 * 32 + lists // 4).reshape(32, count)
    wanted = pl.pallas_call(
        gather_kernel,
        out_shape=jax.ShapeDtypeStruct((32, count, 16, 128), jnp.bfloat16),
        in_specs=[SMEM, VMEM] + [ANY] * 4,
        out_specs=VMEM,
        compiler_params=PARAMS,
        cost_estimate=small,
    )(places, arrived, left, right, weights, moves)
    parts = lax.all_to_all(wanted, NEAR, 0, 0, tiled=True)
    return parts, (top, bottom, left, right)


def fill_rows(cells, top, bottom, padded):
    rows, cols, _ = cells.shape
    wide = top.shape[1]
    for part, start in ((top, 0), (bottom, RMAX + rows)):
        for i in range(RMAX):
            at = pl.ds(LEAD - (wide - cols) // 2, wide)
            padded[start + i, at, :] = part[i].astype(jnp.float32)

    def fill(x, carry):
        padded[RMAX + x, pl.ds(LEAD, cols), :] = cells[x].astype(jnp.float32)
        return carry

    lax.fori_loop(0, rows, fill, 0, unroll=4)


def fill_sides(left, right, padded):
    def one(x, carry):
        at = RMAX + x
        cols = padded.shape[1] - 2 * LEAD
        padded[at, pl.ds(LEAD - RMAX, RMAX), :] = left[x].astype(jnp.float32)
        padded[at, pl.ds(LEAD + cols, RMAX), :] = right[x].astype(jnp.float32)
        return carry

    lax.fori_loop(0, left.shape[0], one, 0, unroll=4)


def clear_sides(padded):
    gap = jnp.zeros((RMAX, padded.shape[2]), jnp.float32)

    def one(x, carry):
        padded[x, pl.ds(LEAD - RMAX, RMAX), :] = gap
        padded[x, pl.ds(padded.shape[1] - LEAD, RMAX), :] = gap
        return carry

    lax.fori_loop(0, padded.shape[0], one, 0, unroll=4)


def add_pairs(padded, pairs):
    high, cols, _ = pairs.shape[1:]

    def one(x, carry):
        for b in range(1, RMAX + 1):
            pairs[b - 1, x] = (
                padded[x, pl.ds(LEAD - b, cols), :] + padded[x, pl.ds(LEAD + b, cols), :]
            )
        return carry

    lax.fori_loop(0, high, one, 0, unroll=2)


def weigh(x, row_sum, weights):
    at = x + RMAX

    def both(a, b):
        low, high = row_sum(at - a, b), row_sum(at + a, b)
        return None if low is None else low + high

    sums = (
        (row_sum(at, 0),),
        (row_sum(at, 1), both(1, 0)),
        (both(1, 1),),
        (row_sum(at, 2), both(2, 0)),
        (both(2, 1), both(1, 2)),
        (both(2, 2),),
        (row_sum(at, 3), both(3, 0)),
        (both(1, 3), both(3, 1)),
        (both(2, 3), both(3, 2)),
        (row_sum(at, 4), both(4, 0)),
    )
    total = None
    for k, terms in enumerate(sums):
        terms = [term for term in terms if term is not None]
        if terms:
            value = functools.reduce(lambda p, q: p + q, terms) * weights[k : k + 1, :]
            total = value if total is None else total + value
    return total


def establish(seeds, here, fecundity, moves):
    arrived = jnp.dot(seeds, fecundity[...], preferred_element_type=jnp.float32)
    middle = (here + arrived).astype(jnp.bfloat16)
    shifted = jnp.dot(middle, moves[...], preferred_element_type=jnp.float32)
    norm = lax.rsqrt(1.0 + jnp.mean(shifted * shifted, axis=-1, keepdims=True))
    return (shifted * norm).astype(jnp.bfloat16)


def remove(flat, slot, ops):
    count = ops.shape[0]
    product = jnp.dot(flat, ops[jnp.minimum(slot, count - 1)], preferred_element_type=jnp.float32)
    return jnp.where(slot == count, flat.astype(jnp.float32), product)


def remove_pair(flat, slots, ops):
    halves = []
    for h, slot in enumerate(slots):
        product = remove(flat, slot, ops).reshape(BX, 2 * BY, flat.shape[-1])
        halves.append(product[:, h * BY : (h + 1) * BY])
    return jnp.concatenate(halves, axis=1)


def assemble(parts, ops):
    count = ops.shape[0]

    def one(k, carry):
        for piece in range(parts.shape[0]):
            r, h = divmod(piece, 2)
            ops[k, r * 16 : (r + 1) * 16, h * 128 : (h + 1) * 128] = parts[piece, k]
        return carry

    lax.fori_loop(0, count, one, 0)


def first_kernel(cells, top, bottom, left, right, weights, fecundity, moves, grown, padded, pairs, seeds):
    rows, cols, cohorts = cells.shape
    fill_rows(cells, top, bottom, padded)
    fill_sides(left, right, padded)
    add_pairs(padded, pairs)

    def row_sum(x, b):
        return padded[x, pl.ds(LEAD, cols), :] if b == 0 else pairs[b - 1, x]

    def one(x, carry):
        seeds[x] = weigh(x, row_sum, weights).astype(jnp.bfloat16)
        return carry

    lax.fori_loop(0, rows, one, 0, unroll=2)
    for i in range(rows // BX):
        span = pl.ds(i * BX, BX)
        here = cells[span].reshape(BX * cols, cohorts).astype(jnp.float32)
        result = establish(seeds[span].reshape(BX * cols, cohorts), here, fecundity, moves)
        grown[span] = result.reshape(BX, cols, cohorts)


def harvest_kernel(slots, grown, parts, out, ops, near, far, head, tail):
    assemble(parts, ops)
    rows, cols, cohorts = grown.shape
    wide = 2 * BY
    for i in range(rows // BX):
        span = pl.ds(i * BX, BX)
        done = []
        for j in range(cols // wide):
            flat = grown[span, pl.ds(j * wide, wide), :].reshape(BX * wide, cohorts)
            done.append(remove_pair(flat, (slots[i, 2 * j], slots[i, 2 * j + 1]), ops))
        whole = jnp.concatenate(done, axis=1)
        out[span] = whole.astype(jnp.bfloat16)
        head[span] = whole[:, :RMAX].astype(jnp.bfloat16)
        tail[span] = whole[:, cols - RMAX :].astype(jnp.bfloat16)
    even = lax.axis_index("co") == 0
    at = jnp.where(even, rows - RMAX, 0)
    for i in range(RMAX):
        near[0, i] = out[at + i]
        near[1, i] = out[at + i]
        far[i] = out[rows - RMAX - at + i]


def middle_kernel(
    slots, cells, top, bottom, weights, fecundity, moves, ops, inner, partial, padded, pairs, seeds
):
    rows, cols, cohorts = cells.shape
    fill_rows(cells, top, bottom, padded)
    clear_sides(padded)
    add_pairs(padded, pairs)

    def row_sum(x, b):
        return padded[x, pl.ds(LEAD, cols), :] if b == 0 else pairs[b - 1, x]

    def one(x, carry):
        total = weigh(x, row_sum, weights)
        partial[x] = jnp.concatenate([total[:BY], total[cols - BY :]], axis=0)
        seeds[x] = total[BY : cols - BY].astype(jnp.bfloat16)
        return carry

    lax.fori_loop(0, rows, one, 0, unroll=2)
    for i in range(0, rows // BX, 2):
        span = pl.ds(i * BX, 2 * BX)
        here = cells[span].astype(jnp.float32)[:, BY : cols - BY].reshape(-1, cohorts)
        grown = establish(seeds[span].reshape(-1, cohorts), here, fecundity, moves)
        half = grown.shape[0] // 2
        for k in range(2):
            done = remove_pair(
                grown[k * half : (k + 1) * half], (slots[i + k, 1], slots[i + k, 2]), ops
            )
            inner[pl.ds((i + k) * BX, BX)] = done.astype(jnp.bfloat16)


def last_kernel(
    slots, cells, left, right, weights, fecundity, moves, ops, inner, partial,
    out, sides, pairs, seeds,
):
    rows, cols, cohorts = cells.shape
    near = lax.broadcasted_iota(jnp.int32, (BY, cohorts), 0) < RMAX
    gap = jnp.zeros((RMAX, cohorts), jnp.float32)

    def place(x, carry):
        sides[x, pl.ds(BY - RMAX, RMAX), :] = left[x].astype(jnp.float32)
        sides[x, pl.ds(BY, RMAX), :] = gap
        sides[x, pl.ds(BY + RMAX, RMAX), :] = right[x].astype(jnp.float32)
        for b in range(1, RMAX + 1):
            pairs[b - 1, x] = jnp.where(
                near, sides[x, pl.ds(BY - b, BY), :], sides[x, pl.ds(RMAX + b, BY), :]
            )
        return carry

    lax.fori_loop(0, rows + 2 * RMAX, place, 0, unroll=4)

    def row_sum(x, b):
        return None if b == 0 else pairs[b - 1, x]

    def one(x, carry):
        extra = weigh(x, row_sum, weights)
        both = jnp.concatenate([jnp.where(near, extra, 0.0), jnp.where(near, 0.0, extra)], axis=0)
        seeds[x] = (partial[x] + both).astype(jnp.bfloat16)
        return carry

    lax.fori_loop(0, rows, one, 0, unroll=4)
    for i in range(0, rows // BX, 2):
        span = pl.ds(i * BX, 2 * BX)
        here = cells[span].astype(jnp.float32)
        here = jnp.concatenate([here[:, :BY], here[:, cols - BY :]], axis=1).reshape(-1, cohorts)
        grown = establish(seeds[span].reshape(-1, cohorts), here, fecundity, moves)
        half = grown.shape[0] // 2
        for k in range(2):
            done = remove_pair(
                grown[k * half : (k + 1) * half], (slots[i + k, 0], slots[i + k, 3]), ops
            )
            at = pl.ds((i + k) * BX, BX)
            whole = jnp.concatenate(
                [done[:, :BY], inner[at].astype(jnp.float32), done[:, BY:]], axis=1
            )
            out[at] = whole.astype(jnp.bfloat16)


def scratch(rows, cols, cohorts, seeded=None):
    high = rows + 2 * RMAX
    return [
        pltpu.VMEM((high, cols + 2 * LEAD, cohorts), jnp.float32),
        pltpu.VMEM((RMAX, high, cols, cohorts), jnp.float32),
        pltpu.VMEM((rows, seeded or cols, cohorts), jnp.bfloat16),
    ]


def local(
    biomass, block_stand, stand_slot, tile_list, harvest_ops, transition, pattern, fecundity, radius
):
    shape = biomass.shape
    rows, cols, cohorts = shape
    count = tile_list.shape[-1]
    stands = stand_slot.shape[-1]
    state = jax.ShapeDtypeStruct(shape, jnp.bfloat16)
    operators = jax.ShapeDtypeStruct((count, cohorts, cohorts), jnp.bfloat16)

    weights = class_weights(radius)
    block_mask = jnp.repeat(jnp.repeat(pattern, TB, 0), TB, 1).astype(jnp.float32)
    moves = (transition.astype(jnp.float32) * block_mask).astype(jnp.bfloat16)
    stand_hit = block_stand[:, :, None] == jnp.arange(stands)[None, None, :]
    slots = jnp.sum(jnp.where(stand_hit, stand_slot[0, 0][None, None, :], 0), axis=-1)

    parts, around = fetch(tile_list, harvest_ops, biomass, weights, moves)
    grown = pl.pallas_call(
        first_kernel,
        out_shape=state,
        in_specs=[VMEM] * 8,
        out_specs=VMEM,
        scratch_shapes=scratch(*shape),
        compiler_params=PARAMS,
        cost_estimate=pl.CostEstimate(flops=2**28, bytes_accessed=2**24, transcendentals=0),
    )(biomass, *around, weights, fecundity, moves)
    row_part = jax.ShapeDtypeStruct((RMAX, cols, cohorts), jnp.bfloat16)
    row_pair = jax.ShapeDtypeStruct((2, RMAX, cols, cohorts), jnp.bfloat16)
    col_part = jax.ShapeDtypeStruct((rows, RMAX, cohorts), jnp.bfloat16)
    cells, ops, near, far, head, tail = pl.pallas_call(
        harvest_kernel,
        out_shape=(state, operators, row_pair, row_part, col_part, col_part),
        in_specs=[SMEM, VMEM, VMEM],
        out_specs=(VMEM,) * 6,
        compiler_params=PARAMS,
        cost_estimate=pl.CostEstimate(flops=2**28, bytes_accessed=2**22, transcendentals=0),
    )(slots, grown, parts)
    top, bottom, left, right = surround(near, far, head, tail)
    high = rows + 2 * RMAX
    outer = 2 * BY
    inner, partial = pl.pallas_call(
        middle_kernel,
        out_shape=(
            jax.ShapeDtypeStruct((rows, cols - outer, cohorts), jnp.bfloat16),
            jax.ShapeDtypeStruct((rows, outer, cohorts), jnp.float32),
        ),
        in_specs=[SMEM] + [VMEM] * 7,
        out_specs=(VMEM, VMEM),
        scratch_shapes=scratch(rows, cols, cohorts, cols - outer),
        compiler_params=PARAMS,
        cost_estimate=pl.CostEstimate(flops=2**28, bytes_accessed=2**24, transcendentals=0),
    )(slots, cells, top, bottom, weights, fecundity, moves, ops)
    return pl.pallas_call(
        last_kernel,
        out_shape=state,
        in_specs=[SMEM] + [VMEM] * 9,
        out_specs=VMEM,
        scratch_shapes=[
            pltpu.VMEM((high, outer, cohorts), jnp.float32),
            pltpu.VMEM((RMAX, high, BY, cohorts), jnp.float32),
            pltpu.VMEM((rows, outer, cohorts), jnp.bfloat16),
        ],
        compiler_params=PARAMS,
        cost_estimate=pl.CostEstimate(flops=2**28, bytes_accessed=2**22, transcendentals=0),
    )(slots, cells, left, right, weights, fecundity, moves, ops, inner, partial)


def solution(mesh):
    names = tuple(name for name, _ in SPLIT)
    sizes = tuple(size for _, size in SPLIT)
    fine = jax.sharding.Mesh(mesh.devices.reshape(sizes), names)
    placed = (
        P(ROW, COL, None),
        P(ROW, COL),
        P(ROW, COL, None),
        P(ROW, COL, None),
        P(COL, None, None),
        P(),
        P(),
        P(),
        P(),
    )
    return jax.shard_map(
        local, mesh=fine, in_specs=placed, out_specs=P(ROW, COL, None), check_vma=False
    )
```

```python
import functools
import math

import jax
import jax.numpy as jnp
from jax import lax
from jax.experimental import pallas as pl
from jax.experimental.pallas import tpu as pltpu
from jax.sharding import PartitionSpec as P

TB = 8
RMAX = 4
BX = 8
BY = 8
STEPS = 2

SPLIT = (("xl", 2), ("yh", 4), ("yl", 2), ("co", 2), ("zh", 4), ("zl", 2), ("xh", 2))
ROW = ("xl", "yh", "yl", "co")
COL = ("zh", "zl", "xh")
NEAR = ("xl", "yl", "co", "zl", "xh")
WIDE = ("xl", "yl", "co", "zh", "zl", "xh")

DIST_SQ = (0, 1, 2, 4, 5, 8, 9, 10, 13, 16)
OFFSETS = (1, 4, 4, 4, 8, 4, 4, 8, 8, 4)

VMEM = pl.BlockSpec(memory_space=pltpu.VMEM)
SMEM = pl.BlockSpec(memory_space=pltpu.SMEM)
ANY = pl.BlockSpec(memory_space=pl.ANY)
PARAMS = pltpu.CompilerParams(vmem_limit_bytes=32 * 1024 * 1024)
WHOLE = pltpu.CompilerParams(vmem_limit_bytes=60 * 1024 * 1024)

LEAD = 8


def shift_pairs(count):
    return [(i, i + 1) for i in range(count - 1)], [(i + 1, i) for i in range(count - 1)]


def swap(head, tail, axis):
    after, before = shift_pairs(math.prod(lax.axis_size(name) for name in axis))
    return lax.ppermute(tail, axis, after), lax.ppermute(head, axis, before)


def surround(near, far, head, tail):
    even = lax.axis_index("co") == 0
    count = math.prod(lax.axis_size(name) for name in ROW)
    pairs = [(i, i + 1) for i in range(1, count - 1, 2)]
    far = lax.ppermute(far, ROW, pairs + [(j, i) for i, j in pairs])
    near = lax.all_to_all(near, "co", 0, 0, tiled=True)
    near = jnp.where(even, near[1], near[0])
    top, bottom = jnp.where(even, far, near), jnp.where(even, near, far)
    head = jnp.concatenate([top[:, :RMAX], head, bottom[:, :RMAX]], axis=0)
    tail = jnp.concatenate([top[:, -RMAX:], tail, bottom[:, -RMAX:]], axis=0)
    return (top, bottom) + swap(head, tail, COL)


def class_weights(radius):
    dist = jnp.array(DIST_SQ, jnp.float32)[:, None]
    reach = (radius.astype(jnp.float32) ** 2)[None, :]
    values = jnp.exp(-dist / (2.0 * reach)) * (dist <= reach).astype(jnp.float32)
    total = jnp.sum(values * jnp.array(OFFSETS, jnp.float32)[:, None], axis=0, keepdims=True)
    return values / total


def sides_kernel(cells, token, head, tail):
    del token
    rows, cols, _ = cells.shape

    def one(x, carry):
        row = cells[x].astype(jnp.float32)
        head[x] = row[:RMAX].astype(jnp.bfloat16)
        tail[x] = row[cols - RMAX :].astype(jnp.bfloat16)
        return carry

    lax.fori_loop(0, rows, one, 0, unroll=4)


def rows_kernel(cells, left, right, first, last):
    rows = cells.shape[0]
    for out, start in ((first, 0), (last, rows - RMAX)):
        for i in range(RMAX):
            parts = [left[start + i], cells[start + i], right[start + i]]
            whole = jnp.concatenate([part.astype(jnp.float32) for part in parts], axis=0)
            out[i] = whole.astype(jnp.bfloat16)


def spread_kernel(tile_list, harvest_ops, spread, token, listed, held, sems):
    mine = (lax.axis_index("xl") * 2 + lax.axis_index("yl")) * 2 + lax.axis_index("co")
    list_copy = pltpu.make_async_copy(tile_list, listed, sems.at[0])
    held_copy = pltpu.make_async_copy(harvest_ops.at[mine // 2], held, sems.at[1])
    list_copy.start()
    held_copy.start()
    list_copy.wait()
    lane = lax.broadcasted_iota(jnp.int32, (16, 128), 1)
    names = jnp.zeros((16, 128), jnp.float32)
    for k in range(listed.shape[-1]):
        names = jnp.where(lax.rem(lane, 64) == k, listed[0, 0, k].astype(jnp.float32), names)
    sent = lane // 64 == lax.rem(mine, 2)
    token[...] = jnp.zeros_like(token)
    held_copy.wait()
    for group in range(8):
        for near in range(4):
            low, half = divmod(near, 2)
            piece = held[pl.ds(group * 32 + low * 16, 16), pl.ds(half * 128, 128)]
            message = jnp.where(sent, piece.astype(jnp.float32), names).astype(jnp.bfloat16)
            for far in range(4):
                spread[(group * 4 + far) * 4 + near] = message


def gather_kernel(places, arrived, left, right, weights, moves, wanted):
    del left, right, weights, moves
    members, count = wanted.shape[:2]
    lower = lax.broadcasted_iota(jnp.int32, (16, 128), 1) < 64

    def one(m, carry):
        found = []
        for k in range(count):
            at = places[m, k]
            found.append(jnp.where(lower, arrived[at], arrived[at + 16]))
        for k in range(count):
            wanted[m, k] = found[k]
        return carry

    lax.fori_loop(0, members, one, 0, unroll=2)


def fetch(tile_list, harvest_ops, cells, weights, moves):
    rows, cols, cohorts = cells.shape
    count = tile_list.shape[-1]
    col_part = jax.ShapeDtypeStruct((rows, RMAX, cohorts), jnp.bfloat16)
    row_part = jax.ShapeDtypeStruct((RMAX, cols + 2 * RMAX, cohorts), jnp.bfloat16)
    small = pl.CostEstimate(flops=0, bytes_accessed=2**20, transcendentals=0)
    spread, token = pl.pallas_call(
        spread_kernel,
        out_shape=(
            jax.ShapeDtypeStruct((128, 16, 128), jnp.bfloat16),
            jax.ShapeDtypeStruct((8, 128), jnp.float32),
        ),
        in_specs=[ANY, ANY],
        out_specs=(VMEM, VMEM),
        scratch_shapes=[
            pltpu.SMEM(tile_list.shape, jnp.int32),
            pltpu.VMEM((cohorts, cohorts), jnp.bfloat16),
            pltpu.SemaphoreType.DMA((2,)),
        ],
        compiler_params=WHOLE,
        cost_estimate=small,
    )(tile_list, harvest_ops)
    arrived = lax.all_to_all(spread, WIDE, 0, 0, tiled=True)
    head, tail = pl.pallas_call(
        sides_kernel,
        out_shape=(col_part, col_part),
        in_specs=[VMEM, ANY],
        out_specs=(VMEM,) * 2,
        compiler_params=PARAMS,
        cost_estimate=small,
    )(cells, token)
    left, right = swap(head, tail, COL)
    first, last = pl.pallas_call(
        rows_kernel,
        out_shape=(row_part, row_part),
        in_specs=[VMEM] * 3,
        out_specs=(VMEM,) * 2,
        compiler_params=PARAMS,
        cost_estimate=small,
    )(cells, left, right)
    top, bottom = swap(first, last, ROW)
    own = lax.dynamic_index_in_dim(
        arrived.reshape(8, 4, 4, 16, 128), lax.axis_index("zh"), axis=1, keepdims=False
    )[:, :, 0].astype(jnp.int32)
    even = jnp.arange(8)[:, None, None] % 2 == 0
    lists = jnp.where(even, own[:, :, 64 : 64 + count], own[:, :, :count])
    places = (lists % 4 * 32 + lists // 4).reshape(32, count)
    wanted = pl.pallas_call(
        gather_kernel,
        out_shape=jax.ShapeDtypeStruct((32, count, 16, 128), jnp.bfloat16),
        in_specs=[SMEM, VMEM] + [ANY] * 4,
        out_specs=VMEM,
        compiler_params=PARAMS,
        cost_estimate=small,
    )(places, arrived, left, right, weights, moves)
    parts = lax.all_to_all(wanted, NEAR, 0, 0, tiled=True)
    return parts, (top, bottom, left, right)


def fill_rows(cells, top, bottom, padded):
    rows, cols, _ = cells.shape
    wide = top.shape[1]
    for part, start in ((top, 0), (bottom, RMAX + rows)):
        for i in range(RMAX):
            at = pl.ds(LEAD - (wide - cols) // 2, wide)
            padded[start + i, at, :] = part[i].astype(jnp.float32)

    def fill(x, carry):
        padded[RMAX + x, pl.ds(LEAD, cols), :] = cells[x].astype(jnp.float32)
        return carry

    lax.fori_loop(0, rows, fill, 0, unroll=4)


def fill_sides(left, right, padded):
    def one(x, carry):
        at = RMAX + x
        cols = padded.shape[1] - 2 * LEAD
        padded[at, pl.ds(LEAD - RMAX, RMAX), :] = left[x].astype(jnp.float32)
        padded[at, pl.ds(LEAD + cols, RMAX), :] = right[x].astype(jnp.float32)
        return carry

    lax.fori_loop(0, left.shape[0], one, 0, unroll=4)


def clear_sides(padded):
    gap = jnp.zeros((RMAX, padded.shape[2]), jnp.float32)

    def one(x, carry):
        padded[x, pl.ds(LEAD - RMAX, RMAX), :] = gap
        padded[x, pl.ds(padded.shape[1] - LEAD, RMAX), :] = gap
        return carry

    lax.fori_loop(0, padded.shape[0], one, 0, unroll=4)


def add_pairs(padded, pairs):
    high, cols, _ = pairs.shape[1:]

    def one(x, carry):
        for b in range(1, RMAX + 1):
            pairs[b - 1, x] = (
                padded[x, pl.ds(LEAD - b, cols), :] + padded[x, pl.ds(LEAD + b, cols), :]
            )
        return carry

    lax.fori_loop(0, high, one, 0, unroll=2)


def weigh(x, row_sum, weights):
    at = x + RMAX

    def both(a, b):
        low, high = row_sum(at - a, b), row_sum(at + a, b)
        return None if low is None else low + high

    sums = (
        (row_sum(at, 0),),
        (row_sum(at, 1), both(1, 0)),
        (both(1, 1),),
        (row_sum(at, 2), both(2, 0)),
        (both(2, 1), both(1, 2)),
        (both(2, 2),),
        (row_sum(at, 3), both(3, 0)),
        (both(1, 3), both(3, 1)),
        (both(2, 3), both(3, 2)),
        (row_sum(at, 4), both(4, 0)),
    )
    total = None
    for k, terms in enumerate(sums):
        terms = [term for term in terms if term is not None]
        if terms:
            value = functools.reduce(lambda p, q: p + q, terms) * weights[k : k + 1, :]
            total = value if total is None else total + value
    return total


def establish(seeds, here, fecundity, moves):
    arrived = jnp.dot(seeds, fecundity[...], preferred_element_type=jnp.float32)
    middle = (here + arrived).astype(jnp.bfloat16)
    shifted = jnp.dot(middle, moves[...], preferred_element_type=jnp.float32)
    norm = lax.rsqrt(1.0 + jnp.mean(shifted * shifted, axis=-1, keepdims=True))
    return (shifted * norm).astype(jnp.bfloat16)


def remove(flat, slot, ops):
    count = ops.shape[0]
    product = jnp.dot(flat, ops[jnp.minimum(slot, count - 1)], preferred_element_type=jnp.float32)
    return jnp.where(slot == count, flat.astype(jnp.float32), product)


def remove_pair(flat, slots, ops):
    halves = []
    for h, slot in enumerate(slots):
        product = remove(flat, slot, ops).reshape(BX, 2 * BY, flat.shape[-1])
        halves.append(product[:, h * BY : (h + 1) * BY])
    return jnp.concatenate(halves, axis=1)


def assemble(parts, ops):
    count = ops.shape[0]

    def one(k, carry):
        for piece in range(parts.shape[0]):
            r, h = divmod(piece, 2)
            ops[k, r * 16 : (r + 1) * 16, h * 128 : (h + 1) * 128] = parts[piece, k]
        return carry

    lax.fori_loop(0, count, one, 0)


def first_kernel(cells, top, bottom, left, right, weights, fecundity, moves, grown, padded, pairs, seeds):
    rows, cols, cohorts = cells.shape
    fill_rows(cells, top, bottom, padded)
    fill_sides(left, right, padded)
    add_pairs(padded, pairs)

    def row_sum(x, b):
        return padded[x, pl.ds(LEAD, cols), :] if b == 0 else pairs[b - 1, x]

    def one(x, carry):
        seeds[x] = weigh(x, row_sum, weights).astype(jnp.bfloat16)
        return carry

    lax.fori_loop(0, rows, one, 0, unroll=2)
    for i in range(rows // BX):
        span = pl.ds(i * BX, BX)
        here = cells[span].reshape(BX * cols, cohorts).astype(jnp.float32)
        result = establish(seeds[span].reshape(BX * cols, cohorts), here, fecundity, moves)
        grown[span] = result.reshape(BX, cols, cohorts)


def harvest_kernel(slots, grown, parts, out, ops, near, far):
    assemble(parts, ops)
    rows, cols, cohorts = grown.shape
    wide = 2 * BY
    for i in range(rows // BX):
        span = pl.ds(i * BX, BX)
        done = []
        for j in range(cols // wide):
            flat = grown[span, pl.ds(j * wide, wide), :].reshape(BX * wide, cohorts)
            done.append(remove_pair(flat, (slots[i, 2 * j], slots[i, 2 * j + 1]), ops))
        whole = jnp.concatenate(done, axis=1)
        out[span] = whole.astype(jnp.bfloat16)
    even = lax.axis_index("co") == 0
    at = jnp.where(even, rows - RMAX, 0)
    for i in range(RMAX):
        near[0, i] = out[at + i]
        near[1, i] = out[at + i]
        far[i] = out[rows - RMAX - at + i]


def middle_kernel(
    slots, cells, top, bottom, weights, fecundity, moves, ops, inner, partial, padded, pairs, seeds
):
    rows, cols, cohorts = cells.shape
    fill_rows(cells, top, bottom, padded)
    clear_sides(padded)
    add_pairs(padded, pairs)

    def row_sum(x, b):
        return padded[x, pl.ds(LEAD, cols), :] if b == 0 else pairs[b - 1, x]

    def one(x, carry):
        total = weigh(x, row_sum, weights)
        partial[x] = jnp.concatenate([total[:BY], total[cols - BY :]], axis=0)
        seeds[x] = total[BY : cols - BY].astype(jnp.bfloat16)
        return carry

    lax.fori_loop(0, rows, one, 0, unroll=2)
    for i in range(0, rows // BX, 2):
        span = pl.ds(i * BX, 2 * BX)
        here = cells[span].astype(jnp.float32)[:, BY : cols - BY].reshape(-1, cohorts)
        grown = establish(seeds[span].reshape(-1, cohorts), here, fecundity, moves)
        half = grown.shape[0] // 2
        for k in range(2):
            done = remove_pair(
                grown[k * half : (k + 1) * half], (slots[i + k, 1], slots[i + k, 2]), ops
            )
            inner[pl.ds((i + k) * BX, BX)] = done.astype(jnp.bfloat16)


def last_kernel(
    slots, cells, left, right, weights, fecundity, moves, ops, inner, partial,
    out, sides, pairs, seeds,
):
    rows, cols, cohorts = cells.shape
    near = lax.broadcasted_iota(jnp.int32, (BY, cohorts), 0) < RMAX
    gap = jnp.zeros((RMAX, cohorts), jnp.float32)

    def place(x, carry):
        sides[x, pl.ds(BY - RMAX, RMAX), :] = left[x].astype(jnp.float32)
        sides[x, pl.ds(BY, RMAX), :] = gap
        sides[x, pl.ds(BY + RMAX, RMAX), :] = right[x].astype(jnp.float32)
        for b in range(1, RMAX + 1):
            pairs[b - 1, x] = jnp.where(
                near, sides[x, pl.ds(BY - b, BY), :], sides[x, pl.ds(RMAX + b, BY), :]
            )
        return carry

    lax.fori_loop(0, rows + 2 * RMAX, place, 0, unroll=4)

    def row_sum(x, b):
        return None if b == 0 else pairs[b - 1, x]

    def one(x, carry):
        extra = weigh(x, row_sum, weights)
        both = jnp.concatenate([jnp.where(near, extra, 0.0), jnp.where(near, 0.0, extra)], axis=0)
        seeds[x] = (partial[x] + both).astype(jnp.bfloat16)
        return carry

    lax.fori_loop(0, rows, one, 0, unroll=4)
    for i in range(0, rows // BX, 2):
        span = pl.ds(i * BX, 2 * BX)
        here = cells[span].astype(jnp.float32)
        here = jnp.concatenate([here[:, :BY], here[:, cols - BY :]], axis=1).reshape(-1, cohorts)
        grown = establish(seeds[span].reshape(-1, cohorts), here, fecundity, moves)
        half = grown.shape[0] // 2
        for k in range(2):
            done = remove_pair(
                grown[k * half : (k + 1) * half], (slots[i + k, 0], slots[i + k, 3]), ops
            )
            at = pl.ds((i + k) * BX, BX)
            whole = jnp.concatenate(
                [done[:, :BY], inner[at].astype(jnp.float32), done[:, BY:]], axis=1
            )
            out[at] = whole.astype(jnp.bfloat16)


def scratch(rows, cols, cohorts, seeded=None):
    high = rows + 2 * RMAX
    return [
        pltpu.VMEM((high, cols + 2 * LEAD, cohorts), jnp.float32),
        pltpu.VMEM((RMAX, high, cols, cohorts), jnp.float32),
        pltpu.VMEM((rows, seeded or cols, cohorts), jnp.bfloat16),
    ]


def local(
    biomass, block_stand, stand_slot, tile_list, harvest_ops, transition, pattern, fecundity, radius
):
    shape = biomass.shape
    rows, cols, cohorts = shape
    count = tile_list.shape[-1]
    stands = stand_slot.shape[-1]
    state = jax.ShapeDtypeStruct(shape, jnp.bfloat16)
    operators = jax.ShapeDtypeStruct((count, cohorts, cohorts), jnp.bfloat16)

    weights = class_weights(radius)
    block_mask = jnp.repeat(jnp.repeat(pattern, TB, 0), TB, 1).astype(jnp.float32)
    moves = (transition.astype(jnp.float32) * block_mask).astype(jnp.bfloat16)
    stand_hit = block_stand[:, :, None] == jnp.arange(stands)[None, None, :]
    slots = jnp.sum(jnp.where(stand_hit, stand_slot[0, 0][None, None, :], 0), axis=-1)

    parts, around = fetch(tile_list, harvest_ops, biomass, weights, moves)
    grown = pl.pallas_call(
        first_kernel,
        out_shape=state,
        in_specs=[VMEM] * 8,
        out_specs=VMEM,
        scratch_shapes=scratch(*shape),
        compiler_params=PARAMS,
        cost_estimate=pl.CostEstimate(flops=2**28, bytes_accessed=2**24, transcendentals=0),
    )(biomass, *around, weights, fecundity, moves)
    row_part = jax.ShapeDtypeStruct((RMAX, cols, cohorts), jnp.bfloat16)
    row_pair = jax.ShapeDtypeStruct((2, RMAX, cols, cohorts), jnp.bfloat16)
    cells, ops, near, far = pl.pallas_call(
        harvest_kernel,
        out_shape=(state, operators, row_pair, row_part),
        in_specs=[SMEM, VMEM, VMEM],
        out_specs=(VMEM,) * 4,
        compiler_params=PARAMS,
        cost_estimate=pl.CostEstimate(flops=2**28, bytes_accessed=2**22, transcendentals=0),
    )(slots, grown, parts)
    top, bottom, left, right = surround(near, far, cells[:, :RMAX], cells[:, -RMAX:])
    high = rows + 2 * RMAX
    outer = 2 * BY
    inner, partial = pl.pallas_call(
        middle_kernel,
        out_shape=(
            jax.ShapeDtypeStruct((rows, cols - outer, cohorts), jnp.bfloat16),
            jax.ShapeDtypeStruct((rows, outer, cohorts), jnp.float32),
        ),
        in_specs=[SMEM] + [VMEM] * 7,
        out_specs=(VMEM, VMEM),
        scratch_shapes=scratch(rows, cols, cohorts, cols - outer),
        compiler_params=PARAMS,
        cost_estimate=pl.CostEstimate(flops=2**28, bytes_accessed=2**24, transcendentals=0),
    )(slots, cells, top, bottom, weights, fecundity, moves, ops)
    return pl.pallas_call(
        last_kernel,
        out_shape=state,
        in_specs=[SMEM] + [VMEM] * 9,
        out_specs=VMEM,
        scratch_shapes=[
            pltpu.VMEM((high, outer, cohorts), jnp.float32),
            pltpu.VMEM((RMAX, high, BY, cohorts), jnp.float32),
            pltpu.VMEM((rows, outer, cohorts), jnp.bfloat16),
        ],
        compiler_params=PARAMS,
        cost_estimate=pl.CostEstimate(flops=2**28, bytes_accessed=2**22, transcendentals=0),
    )(slots, cells, left, right, weights, fecundity, moves, ops, inner, partial)


def solution(mesh):
    names = tuple(name for name, _ in SPLIT)
    sizes = tuple(size for _, size in SPLIT)
    fine = jax.sharding.Mesh(mesh.devices.reshape(sizes), names)
    placed = (
        P(ROW, COL, None),
        P(ROW, COL),
        P(ROW, COL, None),
        P(ROW, COL, None),
        P(COL, None, None),
        P(),
        P(),
        P(),
        P(),
    )
    return jax.shard_map(
        local, mesh=fine, in_specs=placed, out_specs=P(ROW, COL, None), check_vma=False
    )
```

```python
import functools
import math

import jax
import jax.numpy as jnp
from jax import lax
from jax.experimental import pallas as pl
from jax.experimental.pallas import tpu as pltpu
from jax.sharding import PartitionSpec as P

TB = 8
RMAX = 4
BX = 8
BY = 8
STEPS = 2

SPLIT = (("xl", 2), ("yh", 4), ("yl", 2), ("co", 2), ("zh", 4), ("zl", 2), ("xh", 2))
ROW = ("xl", "yh", "yl", "co")
COL = ("zh", "zl", "xh")
NEAR = ("xl", "yl", "co", "zl", "xh")
WIDE = ("xl", "yl", "co", "zh", "zl", "xh")

DIST_SQ = (0, 1, 2, 4, 5, 8, 9, 10, 13, 16)
OFFSETS = (1, 4, 4, 4, 8, 4, 4, 8, 8, 4)

VMEM = pl.BlockSpec(memory_space=pltpu.VMEM)
SMEM = pl.BlockSpec(memory_space=pltpu.SMEM)
ANY = pl.BlockSpec(memory_space=pl.ANY)
PARAMS = pltpu.CompilerParams(vmem_limit_bytes=32 * 1024 * 1024)
WHOLE = pltpu.CompilerParams(vmem_limit_bytes=60 * 1024 * 1024)

LEAD = 8


def shift_pairs(count):
    return [(i, i + 1) for i in range(count - 1)], [(i + 1, i) for i in range(count - 1)]


def swap(head, tail, axis):
    after, before = shift_pairs(math.prod(lax.axis_size(name) for name in axis))
    return lax.ppermute(tail, axis, after), lax.ppermute(head, axis, before)


def surround(first, last, head, tail):
    top, bottom = swap(first, last, ROW)
    head = jnp.concatenate([top[:, :RMAX], head, bottom[:, :RMAX]], axis=0)
    tail = jnp.concatenate([top[:, -RMAX:], tail, bottom[:, -RMAX:]], axis=0)
    return (top, bottom) + swap(head, tail, COL)


def class_weights(radius):
    dist = jnp.array(DIST_SQ, jnp.float32)[:, None]
    reach = (radius.astype(jnp.float32) ** 2)[None, :]
    values = jnp.exp(-dist / (2.0 * reach)) * (dist <= reach).astype(jnp.float32)
    total = jnp.sum(values * jnp.array(OFFSETS, jnp.float32)[:, None], axis=0, keepdims=True)
    return values / total


def sides_kernel(cells, token, head, tail):
    del token
    rows, cols, _ = cells.shape

    def one(x, carry):
        row = cells[x].astype(jnp.float32)
        head[x] = row[:RMAX].astype(jnp.bfloat16)
        tail[x] = row[cols - RMAX :].astype(jnp.bfloat16)
        return carry

    lax.fori_loop(0, rows, one, 0, unroll=4)


def rows_kernel(cells, left, right, first, last):
    rows = cells.shape[0]
    for out, start in ((first, 0), (last, rows - RMAX)):
        for i in range(RMAX):
            parts = [left[start + i], cells[start + i], right[start + i]]
            whole = jnp.concatenate([part.astype(jnp.float32) for part in parts], axis=0)
            out[i] = whole.astype(jnp.bfloat16)


def spread_kernel(tile_list, harvest_ops, spread, token, listed, held, sems):
    mine = (lax.axis_index("xl") * 2 + lax.axis_index("yl")) * 2 + lax.axis_index("co")
    list_copy = pltpu.make_async_copy(tile_list, listed, sems.at[0])
    held_copy = pltpu.make_async_copy(harvest_ops.at[mine // 2], held, sems.at[1])
    list_copy.start()
    held_copy.start()
    list_copy.wait()
    lane = lax.broadcasted_iota(jnp.int32, (16, 128), 1)
    names = jnp.zeros((16, 128), jnp.float32)
    for k in range(listed.shape[-1]):
        names = jnp.where(lax.rem(lane, 64) == k, listed[0, 0, k].astype(jnp.float32), names)
    sent = lane // 64 == lax.rem(mine, 2)
    token[...] = jnp.zeros_like(token)
    held_copy.wait()
    for group in range(8):
        for near in range(4):
            low, half = divmod(near, 2)
            piece = held[pl.ds(group * 32 + low * 16, 16), pl.ds(half * 128, 128)]
            message = jnp.where(sent, piece.astype(jnp.float32), names).astype(jnp.bfloat16)
            for far in range(4):
                spread[(group * 4 + far) * 4 + near] = message


def gather_kernel(places, arrived, left, right, weights, moves, wanted):
    del left, right, weights, moves
    members, count = wanted.shape[:2]
    lower = lax.broadcasted_iota(jnp.int32, (16, 128), 1) < 64

    def one(m, carry):
        found = []
        for k in range(count):
            at = places[m, k]
            found.append(jnp.where(lower, arrived[at], arrived[at + 16]))
        for k in range(count):
            wanted[m, k] = found[k]
        return carry

    lax.fori_loop(0, members, one, 0, unroll=2)


def fetch(tile_list, harvest_ops, cells, weights, moves):
    rows, cols, cohorts = cells.shape
    count = tile_list.shape[-1]
    col_part = jax.ShapeDtypeStruct((rows, RMAX, cohorts), jnp.bfloat16)
    row_part = jax.ShapeDtypeStruct((RMAX, cols + 2 * RMAX, cohorts), jnp.bfloat16)
    small = pl.CostEstimate(flops=0, bytes_accessed=2**20, transcendentals=0)
    spread, token = pl.pallas_call(
        spread_kernel,
        out_shape=(
            jax.ShapeDtypeStruct((128, 16, 128), jnp.bfloat16),
            jax.ShapeDtypeStruct((8, 128), jnp.float32),
        ),
        in_specs=[ANY, ANY],
        out_specs=(VMEM, VMEM),
        scratch_shapes=[
            pltpu.SMEM(tile_list.shape, jnp.int32),
            pltpu.VMEM((cohorts, cohorts), jnp.bfloat16),
            pltpu.SemaphoreType.DMA((2,)),
        ],
        compiler_params=WHOLE,
        cost_estimate=small,
    )(tile_list, harvest_ops)
    arrived = lax.all_to_all(spread, WIDE, 0, 0, tiled=True)
    head, tail = pl.pallas_call(
        sides_kernel,
        out_shape=(col_part, col_part),
        in_specs=[VMEM, ANY],
        out_specs=(VMEM,) * 2,
        compiler_params=PARAMS,
        cost_estimate=small,
    )(cells, token)
    left, right = swap(head, tail, COL)
    first, last = pl.pallas_call(
        rows_kernel,
        out_shape=(row_part, row_part),
        in_specs=[VMEM] * 3,
        out_specs=(VMEM,) * 2,
        compiler_params=PARAMS,
        cost_estimate=small,
    )(cells, left, right)
    top, bottom = swap(first, last, ROW)
    own = lax.dynamic_index_in_dim(
        arrived.reshape(8, 4, 4, 16, 128), lax.axis_index("zh"), axis=1, keepdims=False
    )[:, :, 0].astype(jnp.int32)
    even = jnp.arange(8)[:, None, None] % 2 == 0
    lists = jnp.where(even, own[:, :, 64 : 64 + count], own[:, :, :count])
    places = (lists % 4 * 32 + lists // 4).reshape(32, count)
    wanted = pl.pallas_call(
        gather_kernel,
        out_shape=jax.ShapeDtypeStruct((32, count, 16, 128), jnp.bfloat16),
        in_specs=[SMEM, VMEM] + [ANY] * 4,
        out_specs=VMEM,
        compiler_params=PARAMS,
        cost_estimate=small,
    )(places, arrived, left, right, weights, moves)
    parts = lax.all_to_all(wanted, NEAR, 0, 0, tiled=True)
    return parts, (top, bottom, left, right)


def fill_rows(cells, top, bottom, padded):
    rows, cols, _ = cells.shape
    wide = top.shape[1]
    for part, start in ((top, 0), (bottom, RMAX + rows)):
        for i in range(RMAX):
            at = pl.ds(LEAD - (wide - cols) // 2, wide)
            padded[start + i, at, :] = part[i].astype(jnp.float32)

    def fill(x, carry):
        padded[RMAX + x, pl.ds(LEAD, cols), :] = cells[x].astype(jnp.float32)
        return carry

    lax.fori_loop(0, rows, fill, 0, unroll=4)


def fill_sides(left, right, padded):
    def one(x, carry):
        at = RMAX + x
        cols = padded.shape[1] - 2 * LEAD
        padded[at, pl.ds(LEAD - RMAX, RMAX), :] = left[x].astype(jnp.float32)
        padded[at, pl.ds(LEAD + cols, RMAX), :] = right[x].astype(jnp.float32)
        return carry

    lax.fori_loop(0, left.shape[0], one, 0, unroll=4)


def clear_sides(padded):
    gap = jnp.zeros((RMAX, padded.shape[2]), jnp.float32)

    def one(x, carry):
        padded[x, pl.ds(LEAD - RMAX, RMAX), :] = gap
        padded[x, pl.ds(padded.shape[1] - LEAD, RMAX), :] = gap
        return carry

    lax.fori_loop(0, padded.shape[0], one, 0, unroll=4)


def add_pairs(padded, pairs):
    high, cols, _ = pairs.shape[1:]

    def one(x, carry):
        for b in range(1, RMAX + 1):
            pairs[b - 1, x] = (
                padded[x, pl.ds(LEAD - b, cols), :] + padded[x, pl.ds(LEAD + b, cols), :]
            )
        return carry

    lax.fori_loop(0, high, one, 0, unroll=2)


def weigh(x, row_sum, weights):
    at = x + RMAX

    def both(a, b):
        low, high = row_sum(at - a, b), row_sum(at + a, b)
        return None if low is None else low + high

    sums = (
        (row_sum(at, 0),),
        (row_sum(at, 1), both(1, 0)),
        (both(1, 1),),
        (row_sum(at, 2), both(2, 0)),
        (both(2, 1), both(1, 2)),
        (both(2, 2),),
        (row_sum(at, 3), both(3, 0)),
        (both(1, 3), both(3, 1)),
        (both(2, 3), both(3, 2)),
        (row_sum(at, 4), both(4, 0)),
    )
    total = None
    for k, terms in enumerate(sums):
        terms = [term for term in terms if term is not None]
        if terms:
            value = functools.reduce(lambda p, q: p + q, terms) * weights[k : k + 1, :]
            total = value if total is None else total + value
    return total


def establish(seeds, here, fecundity, moves):
    arrived = jnp.dot(seeds, fecundity[...], preferred_element_type=jnp.float32)
    middle = (here + arrived).astype(jnp.bfloat16)
    shifted = jnp.dot(middle, moves[...], preferred_element_type=jnp.float32)
    norm = lax.rsqrt(1.0 + jnp.mean(shifted * shifted, axis=-1, keepdims=True))
    return (shifted * norm).astype(jnp.bfloat16)


def remove(flat, slot, ops):
    count = ops.shape[0]
    product = jnp.dot(flat, ops[jnp.minimum(slot, count - 1)], preferred_element_type=jnp.float32)
    return jnp.where(slot == count, flat.astype(jnp.float32), product)


def remove_pair(flat, slots, ops):
    halves = []
    for h, slot in enumerate(slots):
        product = remove(flat, slot, ops).reshape(BX, 2 * BY, flat.shape[-1])
        halves.append(product[:, h * BY : (h + 1) * BY])
    return jnp.concatenate(halves, axis=1)


def assemble(parts, ops):
    count = ops.shape[0]

    def one(k, carry):
        for piece in range(parts.shape[0]):
            r, h = divmod(piece, 2)
            ops[k, r * 16 : (r + 1) * 16, h * 128 : (h + 1) * 128] = parts[piece, k]
        return carry

    lax.fori_loop(0, count, one, 0)


def first_kernel(cells, top, bottom, left, right, weights, fecundity, moves, grown, padded, pairs, seeds):
    rows, cols, cohorts = cells.shape
    fill_rows(cells, top, bottom, padded)
    fill_sides(left, right, padded)
    add_pairs(padded, pairs)

    def row_sum(x, b):
        return padded[x, pl.ds(LEAD, cols), :] if b == 0 else pairs[b - 1, x]

    def one(x, carry):
        seeds[x] = weigh(x, row_sum, weights).astype(jnp.bfloat16)
        return carry

    lax.fori_loop(0, rows, one, 0, unroll=2)
    for i in range(rows // BX):
        span = pl.ds(i * BX, BX)
        here = cells[span].reshape(BX * cols, cohorts).astype(jnp.float32)
        result = establish(seeds[span].reshape(BX * cols, cohorts), here, fecundity, moves)
        grown[span] = result.reshape(BX, cols, cohorts)


def harvest_kernel(slots, grown, parts, out, ops, first, last, head, tail):
    assemble(parts, ops)
    rows, cols, cohorts = grown.shape
    wide = 2 * BY
    for i in range(rows // BX):
        span = pl.ds(i * BX, BX)
        done = []
        for j in range(cols // wide):
            flat = grown[span, pl.ds(j * wide, wide), :].reshape(BX * wide, cohorts)
            done.append(remove_pair(flat, (slots[i, 2 * j], slots[i, 2 * j + 1]), ops))
        whole = jnp.concatenate(done, axis=1)
        out[span] = whole.astype(jnp.bfloat16)
        head[span] = whole[:, :RMAX].astype(jnp.bfloat16)
        tail[span] = whole[:, cols - RMAX :].astype(jnp.bfloat16)
        if i == 0:
            first[...] = whole[:RMAX].astype(jnp.bfloat16)
        if i == rows // BX - 1:
            last[...] = whole[BX - RMAX :].astype(jnp.bfloat16)


def middle_kernel(
    slots, cells, top, bottom, weights, fecundity, moves, ops, inner, partial, padded, pairs, seeds
):
    rows, cols, cohorts = cells.shape
    fill_rows(cells, top, bottom, padded)
    clear_sides(padded)
    add_pairs(padded, pairs)

    def row_sum(x, b):
        return padded[x, pl.ds(LEAD, cols), :] if b == 0 else pairs[b - 1, x]

    def one(x, carry):
        total = weigh(x, row_sum, weights)
        partial[x] = jnp.concatenate([total[:BY], total[cols - BY :]], axis=0)
        seeds[x] = total[BY : cols - BY].astype(jnp.bfloat16)
        return carry

    lax.fori_loop(0, rows, one, 0, unroll=2)
    for i in range(0, rows // BX, 2):
        span = pl.ds(i * BX, 2 * BX)
        here = cells[span].astype(jnp.float32)[:, BY : cols - BY].reshape(-1, cohorts)
        grown = establish(seeds[span].reshape(-1, cohorts), here, fecundity, moves)
        half = grown.shape[0] // 2
        for k in range(2):
            done = remove_pair(
                grown[k * half : (k + 1) * half], (slots[i + k, 1], slots[i + k, 2]), ops
            )
            inner[pl.ds((i + k) * BX, BX)] = done.astype(jnp.bfloat16)


def last_kernel(
    slots, cells, left, right, weights, fecundity, moves, ops, inner, partial,
    out, sides, pairs, seeds,
):
    rows, cols, cohorts = cells.shape
    near = lax.broadcasted_iota(jnp.int32, (BY, cohorts), 0) < RMAX
    gap = jnp.zeros((RMAX, cohorts), jnp.float32)

    def place(x, carry):
        sides[x, pl.ds(BY - RMAX, RMAX), :] = left[x].astype(jnp.float32)
        sides[x, pl.ds(BY, RMAX), :] = gap
        sides[x, pl.ds(BY + RMAX, RMAX), :] = right[x].astype(jnp.float32)
        for b in range(1, RMAX + 1):
            pairs[b - 1, x] = jnp.where(
                near, sides[x, pl.ds(BY - b, BY), :], sides[x, pl.ds(RMAX + b, BY), :]
            )
        return carry

    lax.fori_loop(0, rows + 2 * RMAX, place, 0, unroll=4)

    def row_sum(x, b):
        return None if b == 0 else pairs[b - 1, x]

    def one(x, carry):
        extra = weigh(x, row_sum, weights)
        both = jnp.concatenate([jnp.where(near, extra, 0.0), jnp.where(near, 0.0, extra)], axis=0)
        seeds[x] = (partial[x] + both).astype(jnp.bfloat16)
        return carry

    lax.fori_loop(0, rows, one, 0, unroll=4)
    for i in range(0, rows // BX, 2):
        span = pl.ds(i * BX, 2 * BX)
        here = cells[span].astype(jnp.float32)
        here = jnp.concatenate([here[:, :BY], here[:, cols - BY :]], axis=1).reshape(-1, cohorts)
        grown = establish(seeds[span].reshape(-1, cohorts), here, fecundity, moves)
        half = grown.shape[0] // 2
        for k in range(2):
            done = remove_pair(
                grown[k * half : (k + 1) * half], (slots[i + k, 0], slots[i + k, 3]), ops
            )
            at = pl.ds((i + k) * BX, BX)
            whole = jnp.concatenate(
                [done[:, :BY], inner[at].astype(jnp.float32), done[:, BY:]], axis=1
            )
            out[at] = whole.astype(jnp.bfloat16)


def scratch(rows, cols, cohorts, seeded=None):
    high = rows + 2 * RMAX
    return [
        pltpu.VMEM((high, cols + 2 * LEAD, cohorts), jnp.float32),
        pltpu.VMEM((RMAX, high, cols, cohorts), jnp.float32),
        pltpu.VMEM((rows, seeded or cols, cohorts), jnp.bfloat16),
    ]


def local(
    biomass, block_stand, stand_slot, tile_list, harvest_ops, transition, pattern, fecundity, radius
):
    shape = biomass.shape
    rows, cols, cohorts = shape
    count = tile_list.shape[-1]
    stands = stand_slot.shape[-1]
    state = jax.ShapeDtypeStruct(shape, jnp.bfloat16)
    operators = jax.ShapeDtypeStruct((count, cohorts, cohorts), jnp.bfloat16)

    weights = class_weights(radius)
    block_mask = jnp.repeat(jnp.repeat(pattern, TB, 0), TB, 1).astype(jnp.float32)
    moves = (transition.astype(jnp.float32) * block_mask).astype(jnp.bfloat16)
    stand_hit = block_stand[:, :, None] == jnp.arange(stands)[None, None, :]
    slots = jnp.sum(jnp.where(stand_hit, stand_slot[0, 0][None, None, :], 0), axis=-1)

    parts, around = fetch(tile_list, harvest_ops, biomass, weights, moves)
    grown = pl.pallas_call(
        first_kernel,
        out_shape=state,
        in_specs=[VMEM] * 8,
        out_specs=VMEM,
        scratch_shapes=scratch(*shape),
        compiler_params=PARAMS,
        cost_estimate=pl.CostEstimate(flops=2**28, bytes_accessed=2**24, transcendentals=0),
    )(biomass, *around, weights, fecundity, moves)
    row_part = jax.ShapeDtypeStruct((RMAX, cols, cohorts), jnp.bfloat16)
    col_part = jax.ShapeDtypeStruct((rows, RMAX, cohorts), jnp.bfloat16)
    cells, ops, first, last, head, tail = pl.pallas_call(
        harvest_kernel,
        out_shape=(state, operators, row_part, row_part, col_part, col_part),
        in_specs=[SMEM, VMEM, VMEM],
        out_specs=(VMEM,) * 6,
        compiler_params=PARAMS,
        cost_estimate=pl.CostEstimate(flops=2**28, bytes_accessed=2**22, transcendentals=0),
    )(slots, grown, parts)
    top, bottom, left, right = surround(first, last, head, tail)
    high = rows + 2 * RMAX
    outer = 2 * BY
    inner, partial = pl.pallas_call(
        middle_kernel,
        out_shape=(
            jax.ShapeDtypeStruct((rows, cols - outer, cohorts), jnp.bfloat16),
            jax.ShapeDtypeStruct((rows, outer, cohorts), jnp.float32),
        ),
        in_specs=[SMEM] + [VMEM] * 7,
        out_specs=(VMEM, VMEM),
        scratch_shapes=scratch(rows, cols, cohorts, cols - outer),
        compiler_params=PARAMS,
        cost_estimate=pl.CostEstimate(flops=2**28, bytes_accessed=2**24, transcendentals=0),
    )(slots, cells, top, bottom, weights, fecundity, moves, ops)
    return pl.pallas_call(
        last_kernel,
        out_shape=state,
        in_specs=[SMEM] + [VMEM] * 9,
        out_specs=VMEM,
        scratch_shapes=[
            pltpu.VMEM((high, outer, cohorts), jnp.float32),
            pltpu.VMEM((RMAX, high, BY, cohorts), jnp.float32),
            pltpu.VMEM((rows, outer, cohorts), jnp.bfloat16),
        ],
        compiler_params=PARAMS,
        cost_estimate=pl.CostEstimate(flops=2**28, bytes_accessed=2**22, transcendentals=0),
    )(slots, cells, left, right, weights, fecundity, moves, ops, inner, partial)


def solution(mesh):
    names = tuple(name for name, _ in SPLIT)
    sizes = tuple(size for _, size in SPLIT)
    fine = jax.sharding.Mesh(mesh.devices.reshape(sizes), names)
    placed = (
        P(ROW, COL, None),
        P(ROW, COL),
        P(ROW, COL, None),
        P(ROW, COL, None),
        P(COL, None, None),
        P(),
        P(),
        P(),
        P(),
    )
    return jax.shard_map(
        local, mesh=fine, in_specs=placed, out_specs=P(ROW, COL, None), check_vma=False
    )
```

```python
import functools
import math

import jax
import jax.numpy as jnp
from jax import lax
from jax.experimental import pallas as pl
from jax.experimental.pallas import tpu as pltpu
from jax.sharding import PartitionSpec as P

TB = 8
RMAX = 4
BX = 8
BY = 8
STEPS = 2

SPLIT = (("xl", 2), ("yh", 4), ("yl", 2), ("co", 2), ("zh", 4), ("zl", 2), ("xh", 2))
ROW = ("xl", "yh", "yl", "co")
COL = ("zh", "zl", "xh")
NEAR = ("xl", "yl", "co", "zl", "xh")
WIDE = ("xl", "yl", "co", "zh", "zl", "xh")

DIST_SQ = (0, 1, 2, 4, 5, 8, 9, 10, 13, 16)
OFFSETS = (1, 4, 4, 4, 8, 4, 4, 8, 8, 4)

VMEM = pl.BlockSpec(memory_space=pltpu.VMEM)
SMEM = pl.BlockSpec(memory_space=pltpu.SMEM)
ANY = pl.BlockSpec(memory_space=pl.ANY)
PARAMS = pltpu.CompilerParams(vmem_limit_bytes=32 * 1024 * 1024)
WHOLE = pltpu.CompilerParams(vmem_limit_bytes=60 * 1024 * 1024)

LEAD = 8


def shift_pairs(count):
    return [(i, i + 1) for i in range(count - 1)], [(i + 1, i) for i in range(count - 1)]


def swap(head, tail, axis):
    after, before = shift_pairs(math.prod(lax.axis_size(name) for name in axis))
    return lax.ppermute(tail, axis, after), lax.ppermute(head, axis, before)


def surround(first, last, head, tail):
    top, bottom = swap(first, last, ROW)
    head = jnp.concatenate([top[:, :RMAX], head, bottom[:, :RMAX]], axis=0)
    tail = jnp.concatenate([top[:, -RMAX:], tail, bottom[:, -RMAX:]], axis=0)
    return (top, bottom) + swap(head, tail, COL)


def class_weights(radius):
    dist = jnp.array(DIST_SQ, jnp.float32)[:, None]
    reach = (radius.astype(jnp.float32) ** 2)[None, :]
    values = jnp.exp(-dist / (2.0 * reach)) * (dist <= reach).astype(jnp.float32)
    total = jnp.sum(values * jnp.array(OFFSETS, jnp.float32)[:, None], axis=0, keepdims=True)
    return values / total


def sides_kernel(cells, token, head, tail):
    del token
    rows, cols, _ = cells.shape

    def one(x, carry):
        row = cells[x].astype(jnp.float32)
        head[x] = row[:RMAX].astype(jnp.bfloat16)
        tail[x] = row[cols - RMAX :].astype(jnp.bfloat16)
        return carry

    lax.fori_loop(0, rows, one, 0, unroll=4)


def rows_kernel(cells, left, right, first, last):
    rows = cells.shape[0]
    for out, start in ((first, 0), (last, rows - RMAX)):
        for i in range(RMAX):
            parts = [left[start + i], cells[start + i], right[start + i]]
            whole = jnp.concatenate([part.astype(jnp.float32) for part in parts], axis=0)
            out[i] = whole.astype(jnp.bfloat16)


def spread_kernel(tile_list, harvest_ops, spread, token, listed, held, stage, sems):
    mine = (lax.axis_index("xl") * 2 + lax.axis_index("yl")) * 2 + lax.axis_index("co")
    list_copy = pltpu.make_async_copy(tile_list, listed, sems.at[0])
    held_copy = pltpu.make_async_copy(harvest_ops.at[mine // 2], held, sems.at[1])
    list_copy.start()
    held_copy.start()
    list_copy.wait()
    lane = lax.broadcasted_iota(jnp.int32, (16, 128), 1)
    names = jnp.zeros((16, 128), jnp.float32)
    for k in range(listed.shape[-1]):
        names = jnp.where(lax.rem(lane, 64) == k, listed[0, 0, k].astype(jnp.float32), names)
    sent = lane // 64 == lax.rem(mine, 2)
    token[...] = jnp.zeros_like(token)
    held_copy.wait()
    for group in range(8):
        for near in range(4):
            low, half = divmod(near, 2)
            piece = held[pl.ds(group * 32 + low * 16, 16), pl.ds(half * 128, 128)]
            message = jnp.where(sent, piece.astype(jnp.float32), names).astype(jnp.bfloat16)
            for far in range(4):
                stage[(group * 4 + far) * 4 + near] = message
        span = pl.ds(group * 16, 16)
        pltpu.make_async_copy(stage.at[span], spread.at[span], sems.at[2 + group]).start()
    for group in range(8):
        span = pl.ds(group * 16, 16)
        pltpu.make_async_copy(stage.at[span], spread.at[span], sems.at[2 + group]).wait()


def gather_kernel(places, arrived, left, right, weights, moves, wanted, stage, sems):
    del left, right, weights, moves
    members, count = wanted.shape[:2]
    lower = lax.broadcasted_iota(jnp.int32, (16, 128), 1) < 64
    size = members // 4

    def one(m, carry):
        found = []
        for k in range(count):
            at = places[m, k]
            found.append(jnp.where(lower, arrived[at], arrived[at + 16]))
        for k in range(count):
            stage[m, k] = found[k]
        return carry

    for part in range(4):
        lax.fori_loop(part * size, (part + 1) * size, one, 0, unroll=2)
        span = pl.ds(part * size, size)
        pltpu.make_async_copy(stage.at[span], wanted.at[span], sems.at[part]).start()
    for part in range(4):
        span = pl.ds(part * size, size)
        pltpu.make_async_copy(stage.at[span], wanted.at[span], sems.at[part]).wait()


def fetch(tile_list, harvest_ops, cells, weights, moves):
    rows, cols, cohorts = cells.shape
    count = tile_list.shape[-1]
    col_part = jax.ShapeDtypeStruct((rows, RMAX, cohorts), jnp.bfloat16)
    row_part = jax.ShapeDtypeStruct((RMAX, cols + 2 * RMAX, cohorts), jnp.bfloat16)
    small = pl.CostEstimate(flops=0, bytes_accessed=2**20, transcendentals=0)
    spread, token = pl.pallas_call(
        spread_kernel,
        out_shape=(
            jax.ShapeDtypeStruct((128, 16, 128), jnp.bfloat16),
            jax.ShapeDtypeStruct((8, 128), jnp.float32),
        ),
        in_specs=[ANY, ANY],
        out_specs=(ANY, VMEM),
        scratch_shapes=[
            pltpu.SMEM(tile_list.shape, jnp.int32),
            pltpu.VMEM((cohorts, cohorts), jnp.bfloat16),
            pltpu.VMEM((128, 16, 128), jnp.bfloat16),
            pltpu.SemaphoreType.DMA((10,)),
        ],
        compiler_params=WHOLE,
        cost_estimate=small,
    )(tile_list, harvest_ops)
    arrived = lax.all_to_all(spread, WIDE, 0, 0, tiled=True)
    head, tail = pl.pallas_call(
        sides_kernel,
        out_shape=(col_part, col_part),
        in_specs=[VMEM, ANY],
        out_specs=(VMEM,) * 2,
        compiler_params=PARAMS,
        cost_estimate=small,
    )(cells, token)
    left, right = swap(head, tail, COL)
    first, last = pl.pallas_call(
        rows_kernel,
        out_shape=(row_part, row_part),
        in_specs=[VMEM] * 3,
        out_specs=(VMEM,) * 2,
        compiler_params=PARAMS,
        cost_estimate=small,
    )(cells, left, right)
    top, bottom = swap(first, last, ROW)
    own = lax.dynamic_index_in_dim(
        arrived.reshape(8, 4, 4, 16, 128), lax.axis_index("zh"), axis=1, keepdims=False
    )[:, :, 0].astype(jnp.int32)
    even = jnp.arange(8)[:, None, None] % 2 == 0
    lists = jnp.where(even, own[:, :, 64 : 64 + count], own[:, :, :count])
    places = (lists % 4 * 32 + lists // 4).reshape(32, count)
    wanted = pl.pallas_call(
        gather_kernel,
        out_shape=jax.ShapeDtypeStruct((32, count, 16, 128), jnp.bfloat16),
        in_specs=[SMEM, VMEM] + [ANY] * 4,
        out_specs=ANY,
        scratch_shapes=[
            pltpu.VMEM((32, count, 16, 128), jnp.bfloat16), pltpu.SemaphoreType.DMA((4,))
        ],
        compiler_params=PARAMS,
        cost_estimate=small,
    )(places, arrived, left, right, weights, moves)
    parts = lax.all_to_all(wanted, NEAR, 0, 0, tiled=True)
    return parts, (top, bottom, left, right)


def fill_rows(cells, top, bottom, padded):
    rows, cols, _ = cells.shape
    wide = top.shape[1]
    for part, start in ((top, 0), (bottom, RMAX + rows)):
        for i in range(RMAX):
            at = pl.ds(LEAD - (wide - cols) // 2, wide)
            padded[start + i, at, :] = part[i].astype(jnp.float32)

    def fill(x, carry):
        padded[RMAX + x, pl.ds(LEAD, cols), :] = cells[x].astype(jnp.float32)
        return carry

    lax.fori_loop(0, rows, fill, 0, unroll=4)


def fill_sides(left, right, padded):
    def one(x, carry):
        at = RMAX + x
        cols = padded.shape[1] - 2 * LEAD
        padded[at, pl.ds(LEAD - RMAX, RMAX), :] = left[x].astype(jnp.float32)
        padded[at, pl.ds(LEAD + cols, RMAX), :] = right[x].astype(jnp.float32)
        return carry

    lax.fori_loop(0, left.shape[0], one, 0, unroll=4)


def clear_sides(padded):
    gap = jnp.zeros((RMAX, padded.shape[2]), jnp.float32)

    def one(x, carry):
        padded[x, pl.ds(LEAD - RMAX, RMAX), :] = gap
        padded[x, pl.ds(padded.shape[1] - LEAD, RMAX), :] = gap
        return carry

    lax.fori_loop(0, padded.shape[0], one, 0, unroll=4)


def add_pairs(padded, pairs):
    high, cols, _ = pairs.shape[1:]

    def one(x, carry):
        for b in range(1, RMAX + 1):
            pairs[b - 1, x] = (
                padded[x, pl.ds(LEAD - b, cols), :] + padded[x, pl.ds(LEAD + b, cols), :]
            )
        return carry

    lax.fori_loop(0, high, one, 0, unroll=2)


def weigh(x, row_sum, weights):
    at = x + RMAX

    def both(a, b):
        low, high = row_sum(at - a, b), row_sum(at + a, b)
        return None if low is None else low + high

    sums = (
        (row_sum(at, 0),),
        (row_sum(at, 1), both(1, 0)),
        (both(1, 1),),
        (row_sum(at, 2), both(2, 0)),
        (both(2, 1), both(1, 2)),
        (both(2, 2),),
        (row_sum(at, 3), both(3, 0)),
        (both(1, 3), both(3, 1)),
        (both(2, 3), both(3, 2)),
        (row_sum(at, 4), both(4, 0)),
    )
    total = None
    for k, terms in enumerate(sums):
        terms = [term for term in terms if term is not None]
        if terms:
            value = functools.reduce(lambda p, q: p + q, terms) * weights[k : k + 1, :]
            total = value if total is None else total + value
    return total


def establish(seeds, here, fecundity, moves):
    arrived = jnp.dot(seeds, fecundity[...], preferred_element_type=jnp.float32)
    middle = (here + arrived).astype(jnp.bfloat16)
    shifted = jnp.dot(middle, moves[...], preferred_element_type=jnp.float32)
    norm = lax.rsqrt(1.0 + jnp.mean(shifted * shifted, axis=-1, keepdims=True))
    return (shifted * norm).astype(jnp.bfloat16)


def remove(flat, slot, ops):
    count = ops.shape[0]
    product = jnp.dot(flat, ops[jnp.minimum(slot, count - 1)], preferred_element_type=jnp.float32)
    return jnp.where(slot == count, flat.astype(jnp.float32), product)


def remove_pair(flat, slots, ops):
    halves = []
    for h, slot in enumerate(slots):
        product = remove(flat, slot, ops).reshape(BX, 2 * BY, flat.shape[-1])
        halves.append(product[:, h * BY : (h + 1) * BY])
    return jnp.concatenate(halves, axis=1)


def assemble(parts, ops):
    count = ops.shape[0]

    def one(k, carry):
        for piece in range(parts.shape[0]):
            r, h = divmod(piece, 2)
            ops[k, r * 16 : (r + 1) * 16, h * 128 : (h + 1) * 128] = parts[piece, k]
        return carry

    lax.fori_loop(0, count, one, 0)


def first_kernel(cells, top, bottom, left, right, weights, fecundity, moves, grown, padded, pairs, seeds):
    rows, cols, cohorts = cells.shape
    fill_rows(cells, top, bottom, padded)
    fill_sides(left, right, padded)
    add_pairs(padded, pairs)

    def row_sum(x, b):
        return padded[x, pl.ds(LEAD, cols), :] if b == 0 else pairs[b - 1, x]

    def one(x, carry):
        seeds[x] = weigh(x, row_sum, weights).astype(jnp.bfloat16)
        return carry

    lax.fori_loop(0, rows, one, 0, unroll=2)
    for i in range(rows // BX):
        span = pl.ds(i * BX, BX)
        here = cells[span].reshape(BX * cols, cohorts).astype(jnp.float32)
        result = establish(seeds[span].reshape(BX * cols, cohorts), here, fecundity, moves)
        grown[span] = result.reshape(BX, cols, cohorts)


def harvest_kernel(slot_table, grown, parts, out, ops, first, last, head, tail, slots, sem):
    slot_copy = pltpu.make_async_copy(slot_table, slots, sem)
    slot_copy.start()
    assemble(parts, ops)
    slot_copy.wait()
    rows, cols, cohorts = grown.shape
    wide = 2 * BY
    for i in range(rows // BX):
        span = pl.ds(i * BX, BX)
        done = []
        for j in range(cols // wide):
            flat = grown[span, pl.ds(j * wide, wide), :].reshape(BX * wide, cohorts)
            done.append(remove_pair(flat, (slots[i, 2 * j], slots[i, 2 * j + 1]), ops))
        whole = jnp.concatenate(done, axis=1)
        out[span] = whole.astype(jnp.bfloat16)
        head[span] = whole[:, :RMAX].astype(jnp.bfloat16)
        tail[span] = whole[:, cols - RMAX :].astype(jnp.bfloat16)
        if i == 0:
            first[...] = whole[:RMAX].astype(jnp.bfloat16)
        if i == rows // BX - 1:
            last[...] = whole[BX - RMAX :].astype(jnp.bfloat16)


def middle_kernel(
    slot_table, cells, top, bottom, weights, fecundity, moves, ops,
    inner, partial, padded, pairs, seeds, slots, sem,
):
    slot_copy = pltpu.make_async_copy(slot_table, slots, sem)
    slot_copy.start()
    rows, cols, cohorts = cells.shape
    fill_rows(cells, top, bottom, padded)
    clear_sides(padded)
    add_pairs(padded, pairs)

    def row_sum(x, b):
        return padded[x, pl.ds(LEAD, cols), :] if b == 0 else pairs[b - 1, x]

    def one(x, carry):
        total = weigh(x, row_sum, weights)
        partial[x] = jnp.concatenate([total[:BY], total[cols - BY :]], axis=0)
        seeds[x] = total[BY : cols - BY].astype(jnp.bfloat16)
        return carry

    lax.fori_loop(0, rows, one, 0, unroll=2)
    slot_copy.wait()
    for i in range(0, rows // BX, 2):
        span = pl.ds(i * BX, 2 * BX)
        here = cells[span].astype(jnp.float32)[:, BY : cols - BY].reshape(-1, cohorts)
        grown = establish(seeds[span].reshape(-1, cohorts), here, fecundity, moves)
        half = grown.shape[0] // 2
        for k in range(2):
            done = remove_pair(
                grown[k * half : (k + 1) * half], (slots[i + k, 1], slots[i + k, 2]), ops
            )
            inner[pl.ds((i + k) * BX, BX)] = done.astype(jnp.bfloat16)


def last_kernel(
    slot_table, cells, left, right, weights, fecundity, moves, ops, inner, partial,
    out, sides, pairs, seeds, stage, slots, sem, sems,
):
    slot_copy = pltpu.make_async_copy(slot_table, slots, sem)
    slot_copy.start()
    rows, cols, cohorts = cells.shape
    near = lax.broadcasted_iota(jnp.int32, (BY, cohorts), 0) < RMAX
    gap = jnp.zeros((RMAX, cohorts), jnp.float32)

    def place(x, carry):
        sides[x, pl.ds(BY - RMAX, RMAX), :] = left[x].astype(jnp.float32)
        sides[x, pl.ds(BY, RMAX), :] = gap
        sides[x, pl.ds(BY + RMAX, RMAX), :] = right[x].astype(jnp.float32)
        for b in range(1, RMAX + 1):
            pairs[b - 1, x] = jnp.where(
                near, sides[x, pl.ds(BY - b, BY), :], sides[x, pl.ds(RMAX + b, BY), :]
            )
        return carry

    lax.fori_loop(0, rows + 2 * RMAX, place, 0, unroll=4)

    def row_sum(x, b):
        return None if b == 0 else pairs[b - 1, x]

    def one(x, carry):
        extra = weigh(x, row_sum, weights)
        both = jnp.concatenate([jnp.where(near, extra, 0.0), jnp.where(near, 0.0, extra)], axis=0)
        seeds[x] = (partial[x] + both).astype(jnp.bfloat16)
        return carry

    lax.fori_loop(0, rows, one, 0, unroll=4)
    slot_copy.wait()
    for i in range(0, rows // BX, 2):
        span = pl.ds(i * BX, 2 * BX)
        here = cells[span].astype(jnp.float32)
        here = jnp.concatenate([here[:, :BY], here[:, cols - BY :]], axis=1).reshape(-1, cohorts)
        grown = establish(seeds[span].reshape(-1, cohorts), here, fecundity, moves)
        half = grown.shape[0] // 2
        for k in range(2):
            done = remove_pair(
                grown[k * half : (k + 1) * half], (slots[i + k, 0], slots[i + k, 3]), ops
            )
            at = pl.ds((i + k) * BX, BX)
            whole = jnp.concatenate(
                [done[:, :BY], inner[at].astype(jnp.float32), done[:, BY:]], axis=1
            )
            stage[at] = whole.astype(jnp.bfloat16)
            pltpu.make_async_copy(stage.at[at], out.at[at], sems.at[i + k]).start()
    for i in range(rows // BX):
        at = pl.ds(i * BX, BX)
        pltpu.make_async_copy(stage.at[at], out.at[at], sems.at[i]).wait()


def scratch(rows, cols, cohorts, seeded=None):
    high = rows + 2 * RMAX
    return [
        pltpu.VMEM((high, cols + 2 * LEAD, cohorts), jnp.float32),
        pltpu.VMEM((RMAX, high, cols, cohorts), jnp.float32),
        pltpu.VMEM((rows, seeded or cols, cohorts), jnp.bfloat16),
    ]


def local(
    biomass, block_stand, stand_slot, tile_list, harvest_ops, transition, pattern, fecundity, radius
):
    shape = biomass.shape
    rows, cols, cohorts = shape
    count = tile_list.shape[-1]
    stands = stand_slot.shape[-1]
    state = jax.ShapeDtypeStruct(shape, jnp.bfloat16)
    operators = jax.ShapeDtypeStruct((count, cohorts, cohorts), jnp.bfloat16)

    weights = class_weights(radius)
    block_mask = jnp.repeat(jnp.repeat(pattern, TB, 0), TB, 1).astype(jnp.float32)
    moves = (transition.astype(jnp.float32) * block_mask).astype(jnp.bfloat16)
    stand_hit = block_stand[:, :, None] == jnp.arange(stands)[None, None, :]
    slots = jnp.sum(jnp.where(stand_hit, stand_slot[0, 0][None, None, :], 0), axis=-1)

    parts, around = fetch(tile_list, harvest_ops, biomass, weights, moves)
    grown = pl.pallas_call(
        first_kernel,
        out_shape=state,
        in_specs=[VMEM] * 8,
        out_specs=VMEM,
        scratch_shapes=scratch(*shape),
        compiler_params=PARAMS,
        cost_estimate=pl.CostEstimate(flops=2**28, bytes_accessed=2**24, transcendentals=0),
    )(biomass, *around, weights, fecundity, moves)
    slot_room = [pltpu.SMEM(slots.shape, jnp.int32), pltpu.SemaphoreType.DMA]
    row_part = jax.ShapeDtypeStruct((RMAX, cols, cohorts), jnp.bfloat16)
    col_part = jax.ShapeDtypeStruct((rows, RMAX, cohorts), jnp.bfloat16)
    cells, ops, first, last, head, tail = pl.pallas_call(
        harvest_kernel,
        out_shape=(state, operators, row_part, row_part, col_part, col_part),
        in_specs=[ANY, VMEM, VMEM],
        out_specs=(VMEM,) * 6,
        scratch_shapes=slot_room,
        compiler_params=PARAMS,
        cost_estimate=pl.CostEstimate(flops=2**28, bytes_accessed=2**22, transcendentals=0),
    )(slots, grown, parts)
    top, bottom, left, right = surround(first, last, head, tail)
    high = rows + 2 * RMAX
    outer = 2 * BY
    inner, partial = pl.pallas_call(
        middle_kernel,
        out_shape=(
            jax.ShapeDtypeStruct((rows, cols - outer, cohorts), jnp.bfloat16),
            jax.ShapeDtypeStruct((rows, outer, cohorts), jnp.float32),
        ),
        in_specs=[ANY] + [VMEM] * 7,
        out_specs=(VMEM, VMEM),
        scratch_shapes=scratch(rows, cols, cohorts, cols - outer) + slot_room,
        compiler_params=PARAMS,
        cost_estimate=pl.CostEstimate(flops=2**28, bytes_accessed=2**24, transcendentals=0),
    )(slots, cells, top, bottom, weights, fecundity, moves, ops)
    return pl.pallas_call(
        last_kernel,
        out_shape=state,
        in_specs=[ANY] + [VMEM] * 9,
        out_specs=ANY,
        scratch_shapes=[
            pltpu.VMEM((high, outer, cohorts), jnp.float32),
            pltpu.VMEM((RMAX, high, BY, cohorts), jnp.float32),
            pltpu.VMEM((rows, outer, cohorts), jnp.bfloat16),
            pltpu.VMEM(shape, jnp.bfloat16),
        ]
        + slot_room
        + [pltpu.SemaphoreType.DMA((rows // BX,))],
        compiler_params=PARAMS,
        cost_estimate=pl.CostEstimate(flops=2**28, bytes_accessed=2**22, transcendentals=0),
    )(slots, cells, left, right, weights, fecundity, moves, ops, inner, partial)


def solution(mesh):
    names = tuple(name for name, _ in SPLIT)
    sizes = tuple(size for _, size in SPLIT)
    fine = jax.sharding.Mesh(mesh.devices.reshape(sizes), names)
    placed = (
        P(ROW, COL, None),
        P(ROW, COL),
        P(ROW, COL, None),
        P(ROW, COL, None),
        P(COL, None, None),
        P(),
        P(),
        P(),
        P(),
    )
    return jax.shard_map(
        local, mesh=fine, in_specs=placed, out_specs=P(ROW, COL, None), check_vma=False
    )
```

```python
import functools
import math

import jax
import jax.numpy as jnp
from jax import lax
from jax.experimental import pallas as pl
from jax.experimental.pallas import tpu as pltpu
from jax.sharding import PartitionSpec as P

TB = 8
RMAX = 4
BX = 8
BY = 8
STEPS = 2

SPLIT = (("xl", 2), ("yh", 4), ("yl", 2), ("co", 2), ("zh", 4), ("zl", 2), ("xh", 2))
ROW = ("xl", "yh", "yl", "co")
COL = ("zh", "zl", "xh")
NEAR = ("xl", "yl", "co", "zl", "xh")
WIDE = ("xl", "yl", "co", "zh", "zl", "xh")

DIST_SQ = (0, 1, 2, 4, 5, 8, 9, 10, 13, 16)
OFFSETS = (1, 4, 4, 4, 8, 4, 4, 8, 8, 4)

VMEM = pl.BlockSpec(memory_space=pltpu.VMEM)
SMEM = pl.BlockSpec(memory_space=pltpu.SMEM)
ANY = pl.BlockSpec(memory_space=pl.ANY)
PARAMS = pltpu.CompilerParams(vmem_limit_bytes=32 * 1024 * 1024)
WHOLE = pltpu.CompilerParams(vmem_limit_bytes=60 * 1024 * 1024)

LEAD = 8


def shift_pairs(count):
    return [(i, i + 1) for i in range(count - 1)], [(i + 1, i) for i in range(count - 1)]


def swap(head, tail, axis):
    after, before = shift_pairs(math.prod(lax.axis_size(name) for name in axis))
    return lax.ppermute(tail, axis, after), lax.ppermute(head, axis, before)


def surround(first, last, head, tail):
    top, bottom = swap(first, last, ROW)
    head = jnp.concatenate([top[:, :RMAX], head, bottom[:, :RMAX]], axis=0)
    tail = jnp.concatenate([top[:, -RMAX:], tail, bottom[:, -RMAX:]], axis=0)
    return (top, bottom) + swap(head, tail, COL)


def class_weights(radius):
    dist = jnp.array(DIST_SQ, jnp.float32)[:, None]
    reach = (radius.astype(jnp.float32) ** 2)[None, :]
    values = jnp.exp(-dist / (2.0 * reach)) * (dist <= reach).astype(jnp.float32)
    total = jnp.sum(values * jnp.array(OFFSETS, jnp.float32)[:, None], axis=0, keepdims=True)
    return values / total


def sides_kernel(cells, token, head, tail):
    del token
    rows, cols, _ = cells.shape

    def one(x, carry):
        row = cells[x].astype(jnp.float32)
        head[x] = row[:RMAX].astype(jnp.bfloat16)
        tail[x] = row[cols - RMAX :].astype(jnp.bfloat16)
        return carry

    lax.fori_loop(0, rows, one, 0, unroll=4)


def rows_kernel(cells, left, right, first, last):
    rows = cells.shape[0]
    for out, start in ((first, 0), (last, rows - RMAX)):
        for i in range(RMAX):
            parts = [left[start + i], cells[start + i], right[start + i]]
            whole = jnp.concatenate([part.astype(jnp.float32) for part in parts], axis=0)
            out[i] = whole.astype(jnp.bfloat16)


def spread_kernel(tile_list, harvest_ops, spread, token, listed, held, sems):
    mine = (lax.axis_index("xl") * 2 + lax.axis_index("yl")) * 2 + lax.axis_index("co")
    list_copy = pltpu.make_async_copy(tile_list, listed, sems.at[0])
    held_copy = pltpu.make_async_copy(harvest_ops.at[mine // 2], held, sems.at[1])
    list_copy.start()
    held_copy.start()
    list_copy.wait()
    lane = lax.broadcasted_iota(jnp.int32, (16, 128), 1)
    names = jnp.zeros((16, 128), jnp.float32)
    for k in range(listed.shape[-1]):
        names = jnp.where(lax.rem(lane, 64) == k, listed[0, 0, k].astype(jnp.float32), names)
    sent = lane // 64 == lax.rem(mine, 2)
    token[...] = jnp.zeros_like(token)
    held_copy.wait()
    for group in range(8):
        for near in range(4):
            low, half = divmod(near, 2)
            piece = held[pl.ds(group * 32 + low * 16, 16), pl.ds(half * 128, 128)]
            message = jnp.where(sent, piece.astype(jnp.float32), names).astype(jnp.bfloat16)
            for far in range(4):
                spread[(group * 4 + far) * 4 + near] = message


def gather_kernel(places, arrived, left, right, weights, moves, wanted, stage, sems):
    del left, right, weights, moves
    members, count = wanted.shape[:2]
    lower = lax.broadcasted_iota(jnp.int32, (16, 128), 1) < 64
    size = members // 4

    def one(m, carry):
        found = []
        for k in range(count):
            at = places[m, k]
            found.append(jnp.where(lower, arrived[at], arrived[at + 16]))
        for k in range(count):
            stage[m, k] = found[k]
        return carry

    for part in range(4):
        lax.fori_loop(part * size, (part + 1) * size, one, 0, unroll=2)
        span = pl.ds(part * size, size)
        pltpu.make_async_copy(stage.at[span], wanted.at[span], sems.at[part]).start()
    for part in range(4):
        span = pl.ds(part * size, size)
        pltpu.make_async_copy(stage.at[span], wanted.at[span], sems.at[part]).wait()


def fetch(tile_list, harvest_ops, cells, weights, moves):
    rows, cols, cohorts = cells.shape
    count = tile_list.shape[-1]
    col_part = jax.ShapeDtypeStruct((rows, RMAX, cohorts), jnp.bfloat16)
    row_part = jax.ShapeDtypeStruct((RMAX, cols + 2 * RMAX, cohorts), jnp.bfloat16)
    small = pl.CostEstimate(flops=0, bytes_accessed=2**20, transcendentals=0)
    spread, token = pl.pallas_call(
        spread_kernel,
        out_shape=(
            jax.ShapeDtypeStruct((128, 16, 128), jnp.bfloat16),
            jax.ShapeDtypeStruct((8, 128), jnp.float32),
        ),
        in_specs=[ANY, ANY],
        out_specs=(VMEM, VMEM),
        scratch_shapes=[
            pltpu.SMEM(tile_list.shape, jnp.int32),
            pltpu.VMEM((cohorts, cohorts), jnp.bfloat16),
            pltpu.SemaphoreType.DMA((2,)),
        ],
        compiler_params=WHOLE,
        cost_estimate=small,
    )(tile_list, harvest_ops)
    arrived = lax.all_to_all(spread, WIDE, 0, 0, tiled=True)
    head, tail = pl.pallas_call(
        sides_kernel,
        out_shape=(col_part, col_part),
        in_specs=[VMEM, ANY],
        out_specs=(VMEM,) * 2,
        compiler_params=PARAMS,
        cost_estimate=small,
    )(cells, token)
    left, right = swap(head, tail, COL)
    first, last = pl.pallas_call(
        rows_kernel,
        out_shape=(row_part, row_part),
        in_specs=[VMEM] * 3,
        out_specs=(VMEM,) * 2,
        compiler_params=PARAMS,
        cost_estimate=small,
    )(cells, left, right)
    top, bottom = swap(first, last, ROW)
    own = lax.dynamic_index_in_dim(
        arrived.reshape(8, 4, 4, 16, 128), lax.axis_index("zh"), axis=1, keepdims=False
    )[:, :, 0].astype(jnp.int32)
    even = jnp.arange(8)[:, None, None] % 2 == 0
    lists = jnp.where(even, own[:, :, 64 : 64 + count], own[:, :, :count])
    places = (lists % 4 * 32 + lists // 4).reshape(32, count)
    wanted = pl.pallas_call(
        gather_kernel,
        out_shape=jax.ShapeDtypeStruct((32, count, 16, 128), jnp.bfloat16),
        in_specs=[SMEM, VMEM] + [ANY] * 4,
        out_specs=ANY,
        scratch_shapes=[
            pltpu.VMEM((32, count, 16, 128), jnp.bfloat16), pltpu.SemaphoreType.DMA((4,))
        ],
        compiler_params=PARAMS,
        cost_estimate=small,
    )(places, arrived, left, right, weights, moves)
    parts = lax.all_to_all(wanted, NEAR, 0, 0, tiled=True)
    return parts, (top, bottom, left, right)


def fill_rows(cells, top, bottom, padded):
    rows, cols, _ = cells.shape
    wide = top.shape[1]
    for part, start in ((top, 0), (bottom, RMAX + rows)):
        for i in range(RMAX):
            at = pl.ds(LEAD - (wide - cols) // 2, wide)
            padded[start + i, at, :] = part[i].astype(jnp.float32)

    def fill(x, carry):
        padded[RMAX + x, pl.ds(LEAD, cols), :] = cells[x].astype(jnp.float32)
        return carry

    lax.fori_loop(0, rows, fill, 0, unroll=4)


def fill_sides(left, right, padded):
    def one(x, carry):
        at = RMAX + x
        cols = padded.shape[1] - 2 * LEAD
        padded[at, pl.ds(LEAD - RMAX, RMAX), :] = left[x].astype(jnp.float32)
        padded[at, pl.ds(LEAD + cols, RMAX), :] = right[x].astype(jnp.float32)
        return carry

    lax.fori_loop(0, left.shape[0], one, 0, unroll=4)


def clear_sides(padded):
    gap = jnp.zeros((RMAX, padded.shape[2]), jnp.float32)

    def one(x, carry):
        padded[x, pl.ds(LEAD - RMAX, RMAX), :] = gap
        padded[x, pl.ds(padded.shape[1] - LEAD, RMAX), :] = gap
        return carry

    lax.fori_loop(0, padded.shape[0], one, 0, unroll=4)


def add_pairs(padded, pairs):
    high, cols, _ = pairs.shape[1:]

    def one(x, carry):
        for b in range(1, RMAX + 1):
            pairs[b - 1, x] = (
                padded[x, pl.ds(LEAD - b, cols), :] + padded[x, pl.ds(LEAD + b, cols), :]
            )
        return carry

    lax.fori_loop(0, high, one, 0, unroll=2)


def weigh(x, row_sum, weights):
    at = x + RMAX

    def both(a, b):
        low, high = row_sum(at - a, b), row_sum(at + a, b)
        return None if low is None else low + high

    sums = (
        (row_sum(at, 0),),
        (row_sum(at, 1), both(1, 0)),
        (both(1, 1),),
        (row_sum(at, 2), both(2, 0)),
        (both(2, 1), both(1, 2)),
        (both(2, 2),),
        (row_sum(at, 3), both(3, 0)),
        (both(1, 3), both(3, 1)),
        (both(2, 3), both(3, 2)),
        (row_sum(at, 4), both(4, 0)),
    )
    total = None
    for k, terms in enumerate(sums):
        terms = [term for term in terms if term is not None]
        if terms:
            value = functools.reduce(lambda p, q: p + q, terms) * weights[k : k + 1, :]
            total = value if total is None else total + value
    return total


def establish(seeds, here, fecundity, moves):
    arrived = jnp.dot(seeds, fecundity[...], preferred_element_type=jnp.float32)
    middle = (here + arrived).astype(jnp.bfloat16)
    shifted = jnp.dot(middle, moves[...], preferred_element_type=jnp.float32)
    norm = lax.rsqrt(1.0 + jnp.mean(shifted * shifted, axis=-1, keepdims=True))
    return (shifted * norm).astype(jnp.bfloat16)


def remove(flat, slot, ops):
    count = ops.shape[0]
    product = jnp.dot(flat, ops[jnp.minimum(slot, count - 1)], preferred_element_type=jnp.float32)
    return jnp.where(slot == count, flat.astype(jnp.float32), product)


def remove_pair(flat, slots, ops):
    halves = []
    for h, slot in enumerate(slots):
        product = remove(flat, slot, ops).reshape(BX, 2 * BY, flat.shape[-1])
        halves.append(product[:, h * BY : (h + 1) * BY])
    return jnp.concatenate(halves, axis=1)


def assemble(parts, ops):
    count = ops.shape[0]

    def one(k, carry):
        for piece in range(parts.shape[0]):
            r, h = divmod(piece, 2)
            ops[k, r * 16 : (r + 1) * 16, h * 128 : (h + 1) * 128] = parts[piece, k]
        return carry

    lax.fori_loop(0, count, one, 0)


def first_kernel(cells, top, bottom, left, right, weights, fecundity, moves, grown, padded, pairs, seeds):
    rows, cols, cohorts = cells.shape
    fill_rows(cells, top, bottom, padded)
    fill_sides(left, right, padded)
    add_pairs(padded, pairs)

    def row_sum(x, b):
        return padded[x, pl.ds(LEAD, cols), :] if b == 0 else pairs[b - 1, x]

    def one(x, carry):
        seeds[x] = weigh(x, row_sum, weights).astype(jnp.bfloat16)
        return carry

    lax.fori_loop(0, rows, one, 0, unroll=2)
    for i in range(rows // BX):
        span = pl.ds(i * BX, BX)
        here = cells[span].reshape(BX * cols, cohorts).astype(jnp.float32)
        result = establish(seeds[span].reshape(BX * cols, cohorts), here, fecundity, moves)
        grown[span] = result.reshape(BX, cols, cohorts)


def harvest_kernel(slot_table, grown, parts, out, ops, first, last, head, tail, slots, sem):
    slot_copy = pltpu.make_async_copy(slot_table, slots, sem)
    slot_copy.start()
    assemble(parts, ops)
    slot_copy.wait()
    rows, cols, cohorts = grown.shape
    wide = 2 * BY
    for i in range(rows // BX):
        span = pl.ds(i * BX, BX)
        done = []
        for j in range(cols // wide):
            flat = grown[span, pl.ds(j * wide, wide), :].reshape(BX * wide, cohorts)
            done.append(remove_pair(flat, (slots[i, 2 * j], slots[i, 2 * j + 1]), ops))
        whole = jnp.concatenate(done, axis=1)
        out[span] = whole.astype(jnp.bfloat16)
        head[span] = whole[:, :RMAX].astype(jnp.bfloat16)
        tail[span] = whole[:, cols - RMAX :].astype(jnp.bfloat16)
        if i == 0:
            first[...] = whole[:RMAX].astype(jnp.bfloat16)
        if i == rows // BX - 1:
            last[...] = whole[BX - RMAX :].astype(jnp.bfloat16)


def middle_kernel(
    slot_table, cells, top, bottom, weights, fecundity, moves, ops,
    inner, partial, padded, pairs, seeds, slots, sem,
):
    slot_copy = pltpu.make_async_copy(slot_table, slots, sem)
    slot_copy.start()
    rows, cols, cohorts = cells.shape
    fill_rows(cells, top, bottom, padded)
    clear_sides(padded)
    add_pairs(padded, pairs)

    def row_sum(x, b):
        return padded[x, pl.ds(LEAD, cols), :] if b == 0 else pairs[b - 1, x]

    def one(x, carry):
        total = weigh(x, row_sum, weights)
        partial[x] = jnp.concatenate([total[:BY], total[cols - BY :]], axis=0)
        seeds[x] = total[BY : cols - BY].astype(jnp.bfloat16)
        return carry

    lax.fori_loop(0, rows, one, 0, unroll=2)
    slot_copy.wait()
    for i in range(0, rows // BX, 2):
        span = pl.ds(i * BX, 2 * BX)
        here = cells[span].astype(jnp.float32)[:, BY : cols - BY].reshape(-1, cohorts)
        grown = establish(seeds[span].reshape(-1, cohorts), here, fecundity, moves)
        half = grown.shape[0] // 2
        for k in range(2):
            done = remove_pair(
                grown[k * half : (k + 1) * half], (slots[i + k, 1], slots[i + k, 2]), ops
            )
            inner[pl.ds((i + k) * BX, BX)] = done.astype(jnp.bfloat16)


def finish_side(
    lead, block, cells, side, weights, fecundity, moves, ops, partial, write, sides, pairs, seeds,
    slots, slot_copy,
):
    rows, cols, cohorts = cells.shape
    gap = jnp.zeros((BY, cohorts), jnp.float32)
    at = BY - RMAX if lead < 0 else BY

    def place(x, carry):
        sides[x, pl.ds(BY if lead < 0 else 0, BY), :] = gap
        sides[x, pl.ds(at, RMAX), :] = side[x].astype(jnp.float32)
        for b in range(1, RMAX + 1):
            pairs[b - 1, x] = sides[x, pl.ds(BY - b if lead < 0 else b, BY), :]
        return carry

    lax.fori_loop(0, rows + 2 * RMAX, place, 0, unroll=4)

    def row_sum(x, b):
        return None if b == 0 else pairs[b - 1, x]

    first = 0 if lead < 0 else BY

    def one(x, carry):
        seeds[x] = partial[x, pl.ds(first, BY), :] + weigh(x, row_sum, weights)
        return carry

    lax.fori_loop(0, rows, one, 0, unroll=4)
    start = block * BY
    here = cells[...].astype(jnp.float32)[:, start : start + BY].reshape(-1, cohorts)
    arrived = seeds[...].reshape(-1, cohorts).astype(jnp.bfloat16)
    grown = establish(arrived, here, fecundity, moves)
    slot_copy.wait()
    size = BX * BY
    for i in range(rows // BX):
        done = remove(grown[i * size : (i + 1) * size], slots[i, block], ops)
        write(i, done.reshape(BX, BY, cohorts))


def left_kernel(
    slot_table, cells, left, weights, fecundity, moves, ops, partial,
    result, sides, pairs, seeds, slots, sem,
):
    slot_copy = pltpu.make_async_copy(slot_table, slots, sem)
    slot_copy.start()

    def write(i, done):
        result[pl.ds(i * BX, BX)] = done

    finish_side(
        -1, 0, cells, left, weights, fecundity, moves, ops, partial, write, sides, pairs, seeds,
        slots, slot_copy,
    )


def last_kernel(
    slot_table, cells, right, weights, fecundity, moves, ops, partial, before, inner,
    out, sides, pairs, seeds, slots, sem, stage, sems,
):
    rows, cols, _ = cells.shape
    slot_copy = pltpu.make_async_copy(slot_table, slots, sem)
    slot_copy.start()

    def write(i, done):
        at = pl.ds(i * BX, BX)
        whole = jnp.concatenate([before[at], inner[at].astype(jnp.float32), done], axis=1)
        stage[at] = whole.astype(jnp.bfloat16)
        pltpu.make_async_copy(stage.at[at], out.at[at], sems.at[i]).start()

    finish_side(
        1, cols // BY - 1, cells, right, weights, fecundity, moves, ops, partial, write, sides,
        pairs, seeds, slots, slot_copy,
    )
    for i in range(rows // BX):
        at = pl.ds(i * BX, BX)
        pltpu.make_async_copy(stage.at[at], out.at[at], sems.at[i]).wait()


def scratch(rows, cols, cohorts, seeded=None):
    high = rows + 2 * RMAX
    return [
        pltpu.VMEM((high, cols + 2 * LEAD, cohorts), jnp.float32),
        pltpu.VMEM((RMAX, high, cols, cohorts), jnp.float32),
        pltpu.VMEM((rows, seeded or cols, cohorts), jnp.bfloat16),
    ]


def local(
    biomass, block_stand, stand_slot, tile_list, harvest_ops, transition, pattern, fecundity, radius
):
    shape = biomass.shape
    rows, cols, cohorts = shape
    count = tile_list.shape[-1]
    stands = stand_slot.shape[-1]
    state = jax.ShapeDtypeStruct(shape, jnp.bfloat16)
    operators = jax.ShapeDtypeStruct((count, cohorts, cohorts), jnp.bfloat16)

    weights = class_weights(radius)
    block_mask = jnp.repeat(jnp.repeat(pattern, TB, 0), TB, 1).astype(jnp.float32)
    moves = (transition.astype(jnp.float32) * block_mask).astype(jnp.bfloat16)
    stand_hit = block_stand[:, :, None] == jnp.arange(stands)[None, None, :]
    slots = jnp.sum(jnp.where(stand_hit, stand_slot[0, 0][None, None, :], 0), axis=-1)

    parts, around = fetch(tile_list, harvest_ops, biomass, weights, moves)
    grown = pl.pallas_call(
        first_kernel,
        out_shape=state,
        in_specs=[VMEM] * 8,
        out_specs=VMEM,
        scratch_shapes=scratch(*shape),
        compiler_params=PARAMS,
        cost_estimate=pl.CostEstimate(flops=2**28, bytes_accessed=2**24, transcendentals=0),
    )(biomass, *around, weights, fecundity, moves)
    slot_room = [pltpu.SMEM(slots.shape, jnp.int32), pltpu.SemaphoreType.DMA]
    row_part = jax.ShapeDtypeStruct((RMAX, cols, cohorts), jnp.bfloat16)
    col_part = jax.ShapeDtypeStruct((rows, RMAX, cohorts), jnp.bfloat16)
    cells, ops, first, last, head, tail = pl.pallas_call(
        harvest_kernel,
        out_shape=(state, operators, row_part, row_part, col_part, col_part),
        in_specs=[ANY, VMEM, VMEM],
        out_specs=(VMEM,) * 6,
        scratch_shapes=slot_room,
        compiler_params=PARAMS,
        cost_estimate=pl.CostEstimate(flops=2**28, bytes_accessed=2**22, transcendentals=0),
    )(slots, grown, parts)
    top, bottom, left, right = surround(first, last, head, tail)
    high = rows + 2 * RMAX
    outer = 2 * BY
    inner, partial = pl.pallas_call(
        middle_kernel,
        out_shape=(
            jax.ShapeDtypeStruct((rows, cols - outer, cohorts), jnp.bfloat16),
            jax.ShapeDtypeStruct((rows, outer, cohorts), jnp.float32),
        ),
        in_specs=[ANY] + [VMEM] * 7,
        out_specs=(VMEM, VMEM),
        scratch_shapes=scratch(rows, cols, cohorts, cols - outer) + slot_room,
        compiler_params=PARAMS,
        cost_estimate=pl.CostEstimate(flops=2**28, bytes_accessed=2**24, transcendentals=0),
    )(slots, cells, top, bottom, weights, fecundity, moves, ops)
    side_room = [
        pltpu.VMEM((high, outer, cohorts), jnp.float32),
        pltpu.VMEM((RMAX, high, BY, cohorts), jnp.float32),
        pltpu.VMEM((rows, BY, cohorts), jnp.float32),
    ] + slot_room
    before = pl.pallas_call(
        left_kernel,
        out_shape=jax.ShapeDtypeStruct((rows, BY, cohorts), jnp.float32),
        in_specs=[ANY] + [VMEM] * 7,
        out_specs=VMEM,
        scratch_shapes=side_room,
        compiler_params=PARAMS,
        cost_estimate=pl.CostEstimate(flops=2**27, bytes_accessed=2**22, transcendentals=0),
    )(slots, cells, left, weights, fecundity, moves, ops, partial)
    return pl.pallas_call(
        last_kernel,
        out_shape=state,
        in_specs=[ANY] + [VMEM] * 9,
        out_specs=ANY,
        scratch_shapes=side_room
        + [pltpu.VMEM(shape, jnp.bfloat16), pltpu.SemaphoreType.DMA((rows // BX,))],
        compiler_params=PARAMS,
        cost_estimate=pl.CostEstimate(flops=2**28, bytes_accessed=2**22, transcendentals=0),
    )(slots, cells, right, weights, fecundity, moves, ops, partial, before, inner)


def solution(mesh):
    names = tuple(name for name, _ in SPLIT)
    sizes = tuple(size for _, size in SPLIT)
    fine = jax.sharding.Mesh(mesh.devices.reshape(sizes), names)
    placed = (
        P(ROW, COL, None),
        P(ROW, COL),
        P(ROW, COL, None),
        P(ROW, COL, None),
        P(COL, None, None),
        P(),
        P(),
        P(),
        P(),
    )
    return jax.shard_map(
        local, mesh=fine, in_specs=placed, out_specs=P(ROW, COL, None), check_vma=False
    )
```

```python
import functools
import math

import jax
import jax.numpy as jnp
from jax import lax
from jax.experimental import pallas as pl
from jax.experimental.pallas import tpu as pltpu
from jax.sharding import PartitionSpec as P

TB = 8
RMAX = 4
BX = 8
BY = 8
STEPS = 2

SPLIT = (("xl", 2), ("yh", 4), ("yl", 2), ("co", 2), ("zh", 4), ("zl", 2), ("xh", 2))
ROW = ("xl", "yh", "yl", "co")
COL = ("zh", "zl", "xh")
NEAR = ("xl", "yl", "co", "zl", "xh")
WIDE = ("xl", "yl", "co", "zh", "zl", "xh")

DIST_SQ = (0, 1, 2, 4, 5, 8, 9, 10, 13, 16)
OFFSETS = (1, 4, 4, 4, 8, 4, 4, 8, 8, 4)

VMEM = pl.BlockSpec(memory_space=pltpu.VMEM)
SMEM = pl.BlockSpec(memory_space=pltpu.SMEM)
ANY = pl.BlockSpec(memory_space=pl.ANY)
PARAMS = pltpu.CompilerParams(vmem_limit_bytes=32 * 1024 * 1024)
WHOLE = pltpu.CompilerParams(vmem_limit_bytes=60 * 1024 * 1024)

LEAD = 8


def shift_pairs(count):
    return [(i, i + 1) for i in range(count - 1)], [(i + 1, i) for i in range(count - 1)]


def swap(head, tail, axis):
    after, before = shift_pairs(math.prod(lax.axis_size(name) for name in axis))
    return lax.ppermute(tail, axis, after), lax.ppermute(head, axis, before)


def surround(first, last, head, tail):
    top, bottom = swap(first, last, ROW)
    head = jnp.concatenate([top[:, :RMAX], head, bottom[:, :RMAX]], axis=0)
    tail = jnp.concatenate([top[:, -RMAX:], tail, bottom[:, -RMAX:]], axis=0)
    return (top, bottom) + swap(head, tail, COL)


def class_weights(radius):
    dist = jnp.array(DIST_SQ, jnp.float32)[:, None]
    reach = (radius.astype(jnp.float32) ** 2)[None, :]
    values = jnp.exp(-dist / (2.0 * reach)) * (dist <= reach).astype(jnp.float32)
    total = jnp.sum(values * jnp.array(OFFSETS, jnp.float32)[:, None], axis=0, keepdims=True)
    return values / total


def sides_kernel(cells, token, head, tail):
    del token
    rows, cols, _ = cells.shape

    def one(x, carry):
        row = cells[x].astype(jnp.float32)
        head[x] = row[:RMAX].astype(jnp.bfloat16)
        tail[x] = row[cols - RMAX :].astype(jnp.bfloat16)
        return carry

    lax.fori_loop(0, rows, one, 0, unroll=4)


def rows_kernel(cells, left, right, first, last):
    rows = cells.shape[0]
    for out, start in ((first, 0), (last, rows - RMAX)):
        for i in range(RMAX):
            parts = [left[start + i], cells[start + i], right[start + i]]
            whole = jnp.concatenate([part.astype(jnp.float32) for part in parts], axis=0)
            out[i] = whole.astype(jnp.bfloat16)


def spread_kernel(tile_list, harvest_ops, spread, token, listed, held, sems):
    mine = (lax.axis_index("xl") * 2 + lax.axis_index("yl")) * 2 + lax.axis_index("co")
    list_copy = pltpu.make_async_copy(tile_list, listed, sems.at[0])
    held_copy = pltpu.make_async_copy(harvest_ops.at[mine // 2], held, sems.at[1])
    list_copy.start()
    held_copy.start()
    list_copy.wait()
    lane = lax.broadcasted_iota(jnp.int32, (16, 128), 1)
    names = jnp.zeros((16, 128), jnp.float32)
    for k in range(listed.shape[-1]):
        names = jnp.where(lax.rem(lane, 64) == k, listed[0, 0, k].astype(jnp.float32), names)
    sent = lane // 64 == lax.rem(mine, 2)
    token[...] = jnp.zeros_like(token)
    held_copy.wait()
    for group in range(8):
        for near in range(4):
            low, half = divmod(near, 2)
            piece = held[pl.ds(group * 32 + low * 16, 16), pl.ds(half * 128, 128)]
            message = jnp.where(sent, piece.astype(jnp.float32), names).astype(jnp.bfloat16)
            for far in range(4):
                spread[(group * 4 + far) * 4 + near] = message


def gather_kernel(places, arrived, left, right, weights, moves, wanted, stage, sems):
    del left, right, weights, moves
    members, count = wanted.shape[:2]
    lower = lax.broadcasted_iota(jnp.int32, (16, 128), 1) < 64
    size = members // 4

    def one(m, carry):
        found = []
        for k in range(count):
            at = places[m, k]
            found.append(jnp.where(lower, arrived[at], arrived[at + 16]))
        for k in range(count):
            stage[m, k] = found[k]
        return carry

    for part in range(4):
        lax.fori_loop(part * size, (part + 1) * size, one, 0, unroll=2)
        span = pl.ds(part * size, size)
        pltpu.make_async_copy(stage.at[span], wanted.at[span], sems.at[part]).start()
    for part in range(4):
        span = pl.ds(part * size, size)
        pltpu.make_async_copy(stage.at[span], wanted.at[span], sems.at[part]).wait()


def fetch(tile_list, harvest_ops, cells, weights, moves):
    rows, cols, cohorts = cells.shape
    count = tile_list.shape[-1]
    col_part = jax.ShapeDtypeStruct((rows, RMAX, cohorts), jnp.bfloat16)
    row_part = jax.ShapeDtypeStruct((RMAX, cols + 2 * RMAX, cohorts), jnp.bfloat16)
    small = pl.CostEstimate(flops=0, bytes_accessed=2**20, transcendentals=0)
    spread, token = pl.pallas_call(
        spread_kernel,
        out_shape=(
            jax.ShapeDtypeStruct((128, 16, 128), jnp.bfloat16),
            jax.ShapeDtypeStruct((8, 128), jnp.float32),
        ),
        in_specs=[ANY, ANY],
        out_specs=(VMEM, VMEM),
        scratch_shapes=[
            pltpu.SMEM(tile_list.shape, jnp.int32),
            pltpu.VMEM((cohorts, cohorts), jnp.bfloat16),
            pltpu.SemaphoreType.DMA((2,)),
        ],
        compiler_params=WHOLE,
        cost_estimate=small,
    )(tile_list, harvest_ops)
    arrived = lax.all_to_all(spread, WIDE, 0, 0, tiled=True)
    head, tail = pl.pallas_call(
        sides_kernel,
        out_shape=(col_part, col_part),
        in_specs=[VMEM, ANY],
        out_specs=(VMEM,) * 2,
        compiler_params=PARAMS,
        cost_estimate=small,
    )(cells, token)
    left, right = swap(head, tail, COL)
    first, last = pl.pallas_call(
        rows_kernel,
        out_shape=(row_part, row_part),
        in_specs=[VMEM] * 3,
        out_specs=(VMEM,) * 2,
        compiler_params=PARAMS,
        cost_estimate=small,
    )(cells, left, right)
    top, bottom = swap(first, last, ROW)
    own = lax.dynamic_index_in_dim(
        arrived.reshape(8, 4, 4, 16, 128), lax.axis_index("zh"), axis=1, keepdims=False
    )[:, :, 0].astype(jnp.int32)
    even = jnp.arange(8)[:, None, None] % 2 == 0
    lists = jnp.where(even, own[:, :, 64 : 64 + count], own[:, :, :count])
    places = (lists % 4 * 32 + lists // 4).reshape(32, count)
    wanted = pl.pallas_call(
        gather_kernel,
        out_shape=jax.ShapeDtypeStruct((32, count, 16, 128), jnp.bfloat16),
        in_specs=[SMEM, VMEM] + [ANY] * 4,
        out_specs=ANY,
        scratch_shapes=[
            pltpu.VMEM((32, count, 16, 128), jnp.bfloat16), pltpu.SemaphoreType.DMA((4,))
        ],
        compiler_params=PARAMS,
        cost_estimate=small,
    )(places, arrived, left, right, weights, moves)
    parts = lax.all_to_all(wanted, NEAR, 0, 0, tiled=True)
    return parts, (top, bottom, left, right)


def fill_rows(cells, top, bottom, padded):
    rows, cols, _ = cells.shape
    wide = top.shape[1]
    for part, start in ((top, 0), (bottom, RMAX + rows)):
        for i in range(RMAX):
            at = pl.ds(LEAD - (wide - cols) // 2, wide)
            padded[start + i, at, :] = part[i].astype(jnp.float32)

    def fill(x, carry):
        padded[RMAX + x, pl.ds(LEAD, cols), :] = cells[x].astype(jnp.float32)
        return carry

    lax.fori_loop(0, rows, fill, 0, unroll=4)


def fill_sides(left, right, padded):
    def one(x, carry):
        at = RMAX + x
        cols = padded.shape[1] - 2 * LEAD
        padded[at, pl.ds(LEAD - RMAX, RMAX), :] = left[x].astype(jnp.float32)
        padded[at, pl.ds(LEAD + cols, RMAX), :] = right[x].astype(jnp.float32)
        return carry

    lax.fori_loop(0, left.shape[0], one, 0, unroll=4)


def clear_sides(padded):
    gap = jnp.zeros((RMAX, padded.shape[2]), jnp.float32)

    def one(x, carry):
        padded[x, pl.ds(LEAD - RMAX, RMAX), :] = gap
        padded[x, pl.ds(padded.shape[1] - LEAD, RMAX), :] = gap
        return carry

    lax.fori_loop(0, padded.shape[0], one, 0, unroll=4)


def add_pairs(padded, pairs):
    high, cols, _ = pairs.shape[1:]

    def one(x, carry):
        for b in range(1, RMAX + 1):
            pairs[b - 1, x] = (
                padded[x, pl.ds(LEAD - b, cols), :] + padded[x, pl.ds(LEAD + b, cols), :]
            )
        return carry

    lax.fori_loop(0, high, one, 0, unroll=2)


def weigh(x, row_sum, weights):
    at = x + RMAX

    def both(a, b):
        low, high = row_sum(at - a, b), row_sum(at + a, b)
        return None if low is None else low + high

    sums = (
        (row_sum(at, 0),),
        (row_sum(at, 1), both(1, 0)),
        (both(1, 1),),
        (row_sum(at, 2), both(2, 0)),
        (both(2, 1), both(1, 2)),
        (both(2, 2),),
        (row_sum(at, 3), both(3, 0)),
        (both(1, 3), both(3, 1)),
        (both(2, 3), both(3, 2)),
        (row_sum(at, 4), both(4, 0)),
    )
    total = None
    for k, terms in enumerate(sums):
        terms = [term for term in terms if term is not None]
        if terms:
            value = functools.reduce(lambda p, q: p + q, terms) * weights[k : k + 1, :]
            total = value if total is None else total + value
    return total


def establish(seeds, here, fecundity, moves):
    arrived = jnp.dot(seeds, fecundity[...], preferred_element_type=jnp.float32)
    middle = (here + arrived).astype(jnp.bfloat16)
    shifted = jnp.dot(middle, moves[...], preferred_element_type=jnp.float32)
    norm = lax.rsqrt(1.0 + jnp.mean(shifted * shifted, axis=-1, keepdims=True))
    return (shifted * norm).astype(jnp.bfloat16)


def remove(flat, slot, ops):
    count = ops.shape[0]
    product = jnp.dot(flat, ops[jnp.minimum(slot, count - 1)], preferred_element_type=jnp.float32)
    return jnp.where(slot == count, flat.astype(jnp.float32), product)


def remove_pair(flat, slots, ops):
    halves = []
    for h, slot in enumerate(slots):
        product = remove(flat, slot, ops).reshape(BX, 2 * BY, flat.shape[-1])
        halves.append(product[:, h * BY : (h + 1) * BY])
    return jnp.concatenate(halves, axis=1)


def assemble(parts, ops):
    count = ops.shape[0]

    def one(k, carry):
        for piece in range(parts.shape[0]):
            r, h = divmod(piece, 2)
            ops[k, r * 16 : (r + 1) * 16, h * 128 : (h + 1) * 128] = parts[piece, k]
        return carry

    lax.fori_loop(0, count, one, 0)


def first_kernel(cells, top, bottom, left, right, weights, fecundity, moves, grown, padded, pairs, seeds):
    rows, cols, cohorts = cells.shape
    fill_rows(cells, top, bottom, padded)
    fill_sides(left, right, padded)
    add_pairs(padded, pairs)

    def row_sum(x, b):
        return padded[x, pl.ds(LEAD, cols), :] if b == 0 else pairs[b - 1, x]

    def one(x, carry):
        seeds[x] = weigh(x, row_sum, weights).astype(jnp.bfloat16)
        return carry

    lax.fori_loop(0, rows, one, 0, unroll=2)
    for i in range(rows // BX):
        span = pl.ds(i * BX, BX)
        here = cells[span].reshape(BX * cols, cohorts).astype(jnp.float32)
        result = establish(seeds[span].reshape(BX * cols, cohorts), here, fecundity, moves)
        grown[span] = result.reshape(BX, cols, cohorts)


def harvest_kernel(slot_table, grown, parts, out, ops, first, last, head, tail, slots, sem):
    slot_copy = pltpu.make_async_copy(slot_table, slots, sem)
    slot_copy.start()
    assemble(parts, ops)
    slot_copy.wait()
    rows, cols, cohorts = grown.shape
    wide = 2 * BY
    for i in range(rows // BX):
        span = pl.ds(i * BX, BX)
        done = []
        for j in range(cols // wide):
            flat = grown[span, pl.ds(j * wide, wide), :].reshape(BX * wide, cohorts)
            done.append(remove_pair(flat, (slots[i, 2 * j], slots[i, 2 * j + 1]), ops))
        whole = jnp.concatenate(done, axis=1)
        out[span] = whole.astype(jnp.bfloat16)
        head[span] = whole[:, :RMAX].astype(jnp.bfloat16)
        tail[span] = whole[:, cols - RMAX :].astype(jnp.bfloat16)
        if i == 0:
            first[...] = whole[:RMAX].astype(jnp.bfloat16)
        if i == rows // BX - 1:
            last[...] = whole[BX - RMAX :].astype(jnp.bfloat16)


def middle_kernel(
    slot_table, cells, top, bottom, weights, fecundity, moves, ops,
    inner, partial, padded, pairs, seeds, slots, sem,
):
    slot_copy = pltpu.make_async_copy(slot_table, slots, sem)
    slot_copy.start()
    rows, cols, cohorts = cells.shape
    fill_rows(cells, top, bottom, padded)
    clear_sides(padded)
    add_pairs(padded, pairs)

    def row_sum(x, b):
        return padded[x, pl.ds(LEAD, cols), :] if b == 0 else pairs[b - 1, x]

    def one(x, carry):
        total = weigh(x, row_sum, weights)
        partial[x] = jnp.concatenate([total[:BY], total[cols - BY :]], axis=0)
        seeds[x] = total[BY : cols - BY].astype(jnp.bfloat16)
        return carry

    lax.fori_loop(0, rows, one, 0, unroll=2)
    slot_copy.wait()
    for i in range(0, rows // BX, 2):
        span = pl.ds(i * BX, 2 * BX)
        here = cells[span].astype(jnp.float32)[:, BY : cols - BY].reshape(-1, cohorts)
        grown = establish(seeds[span].reshape(-1, cohorts), here, fecundity, moves)
        half = grown.shape[0] // 2
        for k in range(2):
            done = remove_pair(
                grown[k * half : (k + 1) * half], (slots[i + k, 1], slots[i + k, 2]), ops
            )
            inner[pl.ds((i + k) * BX, BX)] = done.astype(jnp.bfloat16)


def finish_side(
    lead, block, cells, side, weights, fecundity, moves, ops, partial, write, sides, pairs, seeds,
    slots, slot_copy,
):
    rows, cols, cohorts = cells.shape
    gap = jnp.zeros((BY, cohorts), jnp.float32)
    at = BY - RMAX if lead < 0 else BY

    def place(x, carry):
        sides[x, pl.ds(BY if lead < 0 else 0, BY), :] = gap
        sides[x, pl.ds(at, RMAX), :] = side[x].astype(jnp.float32)
        for b in range(1, RMAX + 1):
            pairs[b - 1, x] = sides[x, pl.ds(BY - b if lead < 0 else b, BY), :]
        return carry

    lax.fori_loop(0, rows + 2 * RMAX, place, 0, unroll=4)

    def row_sum(x, b):
        return None if b == 0 else pairs[b - 1, x]

    first = 0 if lead < 0 else BY

    def one(x, carry):
        seeds[x] = partial[x, pl.ds(first, BY), :] + weigh(x, row_sum, weights)
        return carry

    lax.fori_loop(0, rows, one, 0, unroll=4)
    start = block * BY
    here = cells[...].astype(jnp.float32)[:, start : start + BY].reshape(-1, cohorts)
    arrived = seeds[...].reshape(-1, cohorts).astype(jnp.bfloat16)
    grown = establish(arrived, here, fecundity, moves)
    slot_copy.wait()
    size = BX * BY
    for i in range(rows // BX):
        done = remove(grown[i * size : (i + 1) * size], slots[i, block], ops)
        write(i, done.reshape(BX, BY, cohorts))


def write_half(low, out, inner, stage, sems):
    wide = 2 * BY

    def copy(i):
        at = pl.ds(i * BX, BX)
        half = out.at[at, pl.ds(0 if low else wide, wide), :]
        return pltpu.make_async_copy(stage.at[at], half, sems.at[i])

    def write(i, done):
        at = pl.ds(i * BX, BX)
        kept = inner[at].astype(jnp.float32)
        parts = [done, kept[:, :BY]] if low else [kept[:, BY:], done]
        stage[at] = jnp.concatenate(parts, axis=1).astype(jnp.bfloat16)
        copy(i).start()

    def wait():
        for i in range(stage.shape[0] // BX):
            copy(i).wait()

    return write, wait


def left_kernel(
    slot_table, cells, left, weights, fecundity, moves, ops, partial, inner,
    out, sides, pairs, seeds, slots, sem, stage, sems,
):
    slot_copy = pltpu.make_async_copy(slot_table, slots, sem)
    slot_copy.start()
    write, wait = write_half(True, out, inner, stage, sems)
    finish_side(
        -1, 0, cells, left, weights, fecundity, moves, ops, partial, write, sides, pairs, seeds,
        slots, slot_copy,
    )
    wait()


def last_kernel(
    slot_table, cells, right, weights, fecundity, moves, ops, partial, inner, begun,
    out, sides, pairs, seeds, slots, sem, stage, sems,
):
    del begun
    slot_copy = pltpu.make_async_copy(slot_table, slots, sem)
    slot_copy.start()
    write, wait = write_half(False, out, inner, stage, sems)
    finish_side(
        1, cells.shape[1] // BY - 1, cells, right, weights, fecundity, moves, ops, partial, write,
        sides, pairs, seeds, slots, slot_copy,
    )
    wait()


def scratch(rows, cols, cohorts, seeded=None):
    high = rows + 2 * RMAX
    return [
        pltpu.VMEM((high, cols + 2 * LEAD, cohorts), jnp.float32),
        pltpu.VMEM((RMAX, high, cols, cohorts), jnp.float32),
        pltpu.VMEM((rows, seeded or cols, cohorts), jnp.bfloat16),
    ]


def local(
    biomass, block_stand, stand_slot, tile_list, harvest_ops, transition, pattern, fecundity, radius
):
    shape = biomass.shape
    rows, cols, cohorts = shape
    count = tile_list.shape[-1]
    stands = stand_slot.shape[-1]
    state = jax.ShapeDtypeStruct(shape, jnp.bfloat16)
    operators = jax.ShapeDtypeStruct((count, cohorts, cohorts), jnp.bfloat16)

    weights = class_weights(radius)
    block_mask = jnp.repeat(jnp.repeat(pattern, TB, 0), TB, 1).astype(jnp.float32)
    moves = (transition.astype(jnp.float32) * block_mask).astype(jnp.bfloat16)
    stand_hit = block_stand[:, :, None] == jnp.arange(stands)[None, None, :]
    slots = jnp.sum(jnp.where(stand_hit, stand_slot[0, 0][None, None, :], 0), axis=-1)

    parts, around = fetch(tile_list, harvest_ops, biomass, weights, moves)
    grown = pl.pallas_call(
        first_kernel,
        out_shape=state,
        in_specs=[VMEM] * 8,
        out_specs=VMEM,
        scratch_shapes=scratch(*shape),
        compiler_params=PARAMS,
        cost_estimate=pl.CostEstimate(flops=2**28, bytes_accessed=2**24, transcendentals=0),
    )(biomass, *around, weights, fecundity, moves)
    slot_room = [pltpu.SMEM(slots.shape, jnp.int32), pltpu.SemaphoreType.DMA]
    row_part = jax.ShapeDtypeStruct((RMAX, cols, cohorts), jnp.bfloat16)
    col_part = jax.ShapeDtypeStruct((rows, RMAX, cohorts), jnp.bfloat16)
    cells, ops, first, last, head, tail = pl.pallas_call(
        harvest_kernel,
        out_shape=(state, operators, row_part, row_part, col_part, col_part),
        in_specs=[ANY, VMEM, VMEM],
        out_specs=(VMEM,) * 6,
        scratch_shapes=slot_room,
        compiler_params=PARAMS,
        cost_estimate=pl.CostEstimate(flops=2**28, bytes_accessed=2**22, transcendentals=0),
    )(slots, grown, parts)
    top, bottom, left, right = surround(first, last, head, tail)
    high = rows + 2 * RMAX
    outer = 2 * BY
    inner, partial = pl.pallas_call(
        middle_kernel,
        out_shape=(
            jax.ShapeDtypeStruct((rows, cols - outer, cohorts), jnp.bfloat16),
            jax.ShapeDtypeStruct((rows, outer, cohorts), jnp.float32),
        ),
        in_specs=[ANY] + [VMEM] * 7,
        out_specs=(VMEM, VMEM),
        scratch_shapes=scratch(rows, cols, cohorts, cols - outer) + slot_room,
        compiler_params=PARAMS,
        cost_estimate=pl.CostEstimate(flops=2**28, bytes_accessed=2**24, transcendentals=0),
    )(slots, cells, top, bottom, weights, fecundity, moves, ops)
    side_room = [
        pltpu.VMEM((high, outer, cohorts), jnp.float32),
        pltpu.VMEM((RMAX, high, BY, cohorts), jnp.float32),
        pltpu.VMEM((rows, BY, cohorts), jnp.float32),
    ] + slot_room
    half_room = [
        pltpu.VMEM((rows, outer, cohorts), jnp.bfloat16),
        pltpu.SemaphoreType.DMA((rows // BX,)),
    ]
    begun = pl.pallas_call(
        left_kernel,
        out_shape=state,
        in_specs=[ANY] + [VMEM] * 8,
        out_specs=ANY,
        scratch_shapes=side_room + half_room,
        compiler_params=PARAMS,
        cost_estimate=pl.CostEstimate(flops=2**27, bytes_accessed=2**22, transcendentals=0),
    )(slots, cells, left, weights, fecundity, moves, ops, partial, inner)
    return pl.pallas_call(
        last_kernel,
        out_shape=state,
        in_specs=[ANY] + [VMEM] * 8 + [ANY],
        out_specs=ANY,
        scratch_shapes=side_room + half_room,
        input_output_aliases={9: 0},
        compiler_params=PARAMS,
        cost_estimate=pl.CostEstimate(flops=2**28, bytes_accessed=2**22, transcendentals=0),
    )(slots, cells, right, weights, fecundity, moves, ops, partial, inner, begun)


def solution(mesh):
    names = tuple(name for name, _ in SPLIT)
    sizes = tuple(size for _, size in SPLIT)
    fine = jax.sharding.Mesh(mesh.devices.reshape(sizes), names)
    placed = (
        P(ROW, COL, None),
        P(ROW, COL),
        P(ROW, COL, None),
        P(ROW, COL, None),
        P(COL, None, None),
        P(),
        P(),
        P(),
        P(),
    )
    return jax.shard_map(
        local, mesh=fine, in_specs=placed, out_specs=P(ROW, COL, None), check_vma=False
    )
```

```python
import functools
import math

import jax
import jax.numpy as jnp
from jax import lax
from jax.experimental import pallas as pl
from jax.experimental.pallas import tpu as pltpu
from jax.sharding import PartitionSpec as P

TB = 8
RMAX = 4
BX = 8
BY = 8
STEPS = 2

SPLIT = (("xl", 2), ("yh", 4), ("yl", 2), ("co", 2), ("zh", 4), ("zl", 2), ("xh", 2))
ROW = ("xl", "yh", "yl", "co")
COL = ("zh", "zl", "xh")
NEAR = ("xl", "yl", "co", "zl", "xh")
WIDE = ("xl", "yl", "co", "zh", "zl", "xh")

DIST_SQ = (0, 1, 2, 4, 5, 8, 9, 10, 13, 16)
OFFSETS = (1, 4, 4, 4, 8, 4, 4, 8, 8, 4)

VMEM = pl.BlockSpec(memory_space=pltpu.VMEM)
SMEM = pl.BlockSpec(memory_space=pltpu.SMEM)
ANY = pl.BlockSpec(memory_space=pl.ANY)
PARAMS = pltpu.CompilerParams(vmem_limit_bytes=32 * 1024 * 1024)
WHOLE = pltpu.CompilerParams(vmem_limit_bytes=60 * 1024 * 1024)

LEAD = 8


def shift_pairs(count):
    return [(i, i + 1) for i in range(count - 1)], [(i + 1, i) for i in range(count - 1)]


def swap(head, tail, axis):
    after, before = shift_pairs(math.prod(lax.axis_size(name) for name in axis))
    return lax.ppermute(tail, axis, after), lax.ppermute(head, axis, before)


def surround(first, last, head, tail):
    top, bottom = swap(first, last, ROW)
    head = jnp.concatenate([top[:, :RMAX], head, bottom[:, :RMAX]], axis=0)
    tail = jnp.concatenate([top[:, -RMAX:], tail, bottom[:, -RMAX:]], axis=0)
    return (top, bottom) + swap(head, tail, COL)


def class_weights(radius):
    dist = jnp.array(DIST_SQ, jnp.float32)[:, None]
    reach = (radius.astype(jnp.float32) ** 2)[None, :]
    values = jnp.exp(-dist / (2.0 * reach)) * (dist <= reach).astype(jnp.float32)
    total = jnp.sum(values * jnp.array(OFFSETS, jnp.float32)[:, None], axis=0, keepdims=True)
    return values / total


def sides_kernel(cells, token, head, tail):
    del token
    rows, cols, _ = cells.shape

    def one(x, carry):
        row = cells[x].astype(jnp.float32)
        head[x] = row[:RMAX].astype(jnp.bfloat16)
        tail[x] = row[cols - RMAX :].astype(jnp.bfloat16)
        return carry

    lax.fori_loop(0, rows, one, 0, unroll=4)


def rows_kernel(cells, left, right, first, last):
    rows = cells.shape[0]
    for out, start in ((first, 0), (last, rows - RMAX)):
        for i in range(RMAX):
            parts = [left[start + i], cells[start + i], right[start + i]]
            whole = jnp.concatenate([part.astype(jnp.float32) for part in parts], axis=0)
            out[i] = whole.astype(jnp.bfloat16)


def spread_kernel(tile_list, harvest_ops, spread, token, listed, held, stage, sems):
    mine = (lax.axis_index("xl") * 2 + lax.axis_index("yl")) * 2 + lax.axis_index("co")
    list_copy = pltpu.make_async_copy(tile_list, listed, sems.at[0])
    held_copy = pltpu.make_async_copy(harvest_ops.at[mine // 2], held, sems.at[1])
    list_copy.start()
    held_copy.start()
    list_copy.wait()
    lane = lax.broadcasted_iota(jnp.int32, (16, 128), 1)
    names = jnp.zeros((16, 128), jnp.float32)
    for k in range(listed.shape[-1]):
        names = jnp.where(lax.rem(lane, 64) == k, listed[0, 0, k].astype(jnp.float32), names)
    sent = lane // 64 == lax.rem(mine, 2)
    token[...] = jnp.zeros_like(token)
    held_copy.wait()
    for group in range(8):
        for near in range(4):
            low, half = divmod(near, 2)
            piece = held[pl.ds(group * 32 + low * 16, 16), pl.ds(half * 128, 128)]
            message = jnp.where(sent, piece.astype(jnp.float32), names).astype(jnp.bfloat16)
            for far in range(4):
                stage[(group * 4 + far) * 4 + near] = message
        if group % 4 == 3:
            span = pl.ds((group - 3) * 16, 64)
            pltpu.make_async_copy(stage.at[span], spread.at[span], sems.at[2 + group // 4]).start()
    for part in range(2):
        span = pl.ds(part * 64, 64)
        pltpu.make_async_copy(stage.at[span], spread.at[span], sems.at[2 + part]).wait()


def gather_kernel(places, arrived, left, right, weights, moves, wanted, stage, sems):
    del left, right, weights, moves
    members, count = wanted.shape[:2]
    lower = lax.broadcasted_iota(jnp.int32, (16, 128), 1) < 64
    size = members // 4

    def one(m, carry):
        found = []
        for k in range(count):
            at = places[m, k]
            found.append(jnp.where(lower, arrived[at], arrived[at + 16]))
        for k in range(count):
            stage[m, k] = found[k]
        return carry

    for part in range(4):
        lax.fori_loop(part * size, (part + 1) * size, one, 0, unroll=2)
        span = pl.ds(part * size, size)
        pltpu.make_async_copy(stage.at[span], wanted.at[span], sems.at[part]).start()
    for part in range(4):
        span = pl.ds(part * size, size)
        pltpu.make_async_copy(stage.at[span], wanted.at[span], sems.at[part]).wait()


def fetch(tile_list, harvest_ops, cells, weights, moves):
    rows, cols, cohorts = cells.shape
    count = tile_list.shape[-1]
    col_part = jax.ShapeDtypeStruct((rows, RMAX, cohorts), jnp.bfloat16)
    row_part = jax.ShapeDtypeStruct((RMAX, cols + 2 * RMAX, cohorts), jnp.bfloat16)
    small = pl.CostEstimate(flops=0, bytes_accessed=2**20, transcendentals=0)
    spread, token = pl.pallas_call(
        spread_kernel,
        out_shape=(
            jax.ShapeDtypeStruct((128, 16, 128), jnp.bfloat16),
            jax.ShapeDtypeStruct((8, 128), jnp.float32),
        ),
        in_specs=[ANY, ANY],
        out_specs=(ANY, VMEM),
        scratch_shapes=[
            pltpu.SMEM(tile_list.shape, jnp.int32),
            pltpu.VMEM((cohorts, cohorts), jnp.bfloat16),
            pltpu.VMEM((128, 16, 128), jnp.bfloat16),
            pltpu.SemaphoreType.DMA((4,)),
        ],
        compiler_params=WHOLE,
        cost_estimate=small,
    )(tile_list, harvest_ops)
    arrived = lax.all_to_all(spread, WIDE, 0, 0, tiled=True)
    head, tail = pl.pallas_call(
        sides_kernel,
        out_shape=(col_part, col_part),
        in_specs=[VMEM, ANY],
        out_specs=(VMEM,) * 2,
        compiler_params=PARAMS,
        cost_estimate=small,
    )(cells, token)
    left, right = swap(head, tail, COL)
    first, last = pl.pallas_call(
        rows_kernel,
        out_shape=(row_part, row_part),
        in_specs=[VMEM] * 3,
        out_specs=(VMEM,) * 2,
        compiler_params=PARAMS,
        cost_estimate=small,
    )(cells, left, right)
    top, bottom = swap(first, last, ROW)
    own = lax.dynamic_index_in_dim(
        arrived.reshape(8, 4, 4, 16, 128), lax.axis_index("zh"), axis=1, keepdims=False
    )[:, :, 0].astype(jnp.int32)
    even = jnp.arange(8)[:, None, None] % 2 == 0
    lists = jnp.where(even, own[:, :, 64 : 64 + count], own[:, :, :count])
    places = (lists % 4 * 32 + lists // 4).reshape(32, count)
    wanted = pl.pallas_call(
        gather_kernel,
        out_shape=jax.ShapeDtypeStruct((32, count, 16, 128), jnp.bfloat16),
        in_specs=[SMEM, VMEM] + [ANY] * 4,
        out_specs=ANY,
        scratch_shapes=[
            pltpu.VMEM((32, count, 16, 128), jnp.bfloat16), pltpu.SemaphoreType.DMA((4,))
        ],
        compiler_params=PARAMS,
        cost_estimate=small,
    )(places, arrived, left, right, weights, moves)
    parts = lax.all_to_all(wanted, NEAR, 0, 0, tiled=True)
    return parts, (top, bottom, left, right)


def fill_rows(cells, top, bottom, padded):
    rows, cols, _ = cells.shape
    wide = top.shape[1]
    for part, start in ((top, 0), (bottom, RMAX + rows)):
        for i in range(RMAX):
            at = pl.ds(LEAD - (wide - cols) // 2, wide)
            padded[start + i, at, :] = part[i].astype(jnp.float32)

    def fill(x, carry):
        padded[RMAX + x, pl.ds(LEAD, cols), :] = cells[x].astype(jnp.float32)
        return carry

    lax.fori_loop(0, rows, fill, 0, unroll=4)


def fill_sides(left, right, padded):
    def one(x, carry):
        at = RMAX + x
        cols = padded.shape[1] - 2 * LEAD
        padded[at, pl.ds(LEAD - RMAX, RMAX), :] = left[x].astype(jnp.float32)
        padded[at, pl.ds(LEAD + cols, RMAX), :] = right[x].astype(jnp.float32)
        return carry

    lax.fori_loop(0, left.shape[0], one, 0, unroll=4)


def clear_sides(padded):
    gap = jnp.zeros((RMAX, padded.shape[2]), jnp.float32)

    def one(x, carry):
        padded[x, pl.ds(LEAD - RMAX, RMAX), :] = gap
        padded[x, pl.ds(padded.shape[1] - LEAD, RMAX), :] = gap
        return carry

    lax.fori_loop(0, padded.shape[0], one, 0, unroll=4)


def add_pairs(padded, pairs):
    high, cols, _ = pairs.shape[1:]

    def one(x, carry):
        for b in range(1, RMAX + 1):
            pairs[b - 1, x] = (
                padded[x, pl.ds(LEAD - b, cols), :] + padded[x, pl.ds(LEAD + b, cols), :]
            )
        return carry

    lax.fori_loop(0, high, one, 0, unroll=2)


def weigh(x, row_sum, weights):
    at = x + RMAX

    def both(a, b):
        low, high = row_sum(at - a, b), row_sum(at + a, b)
        return None if low is None else low + high

    sums = (
        (row_sum(at, 0),),
        (row_sum(at, 1), both(1, 0)),
        (both(1, 1),),
        (row_sum(at, 2), both(2, 0)),
        (both(2, 1), both(1, 2)),
        (both(2, 2),),
        (row_sum(at, 3), both(3, 0)),
        (both(1, 3), both(3, 1)),
        (both(2, 3), both(3, 2)),
        (row_sum(at, 4), both(4, 0)),
    )
    total = None
    for k, terms in enumerate(sums):
        terms = [term for term in terms if term is not None]
        if terms:
            value = functools.reduce(lambda p, q: p + q, terms) * weights[k : k + 1, :]
            total = value if total is None else total + value
    return total


def establish(seeds, here, fecundity, moves):
    arrived = jnp.dot(seeds, fecundity[...], preferred_element_type=jnp.float32)
    middle = (here + arrived).astype(jnp.bfloat16)
    shifted = jnp.dot(middle, moves[...], preferred_element_type=jnp.float32)
    norm = lax.rsqrt(1.0 + jnp.mean(shifted * shifted, axis=-1, keepdims=True))
    return (shifted * norm).astype(jnp.bfloat16)


def remove(flat, slot, ops):
    count = ops.shape[0]
    product = jnp.dot(flat, ops[jnp.minimum(slot, count - 1)], preferred_element_type=jnp.float32)
    return jnp.where(slot == count, flat.astype(jnp.float32), product)


def remove_pair(flat, slots, ops):
    halves = []
    for h, slot in enumerate(slots):
        product = remove(flat, slot, ops).reshape(BX, 2 * BY, flat.shape[-1])
        halves.append(product[:, h * BY : (h + 1) * BY])
    return jnp.concatenate(halves, axis=1)


def assemble(parts, ops):
    count = ops.shape[0]

    def one(k, carry):
        for piece in range(parts.shape[0]):
            r, h = divmod(piece, 2)
            ops[k, r * 16 : (r + 1) * 16, h * 128 : (h + 1) * 128] = parts[piece, k]
        return carry

    lax.fori_loop(0, count, one, 0)


def first_kernel(cells, top, bottom, left, right, weights, fecundity, moves, grown, padded, pairs, seeds):
    rows, cols, cohorts = cells.shape
    fill_rows(cells, top, bottom, padded)
    fill_sides(left, right, padded)
    add_pairs(padded, pairs)

    def row_sum(x, b):
        return padded[x, pl.ds(LEAD, cols), :] if b == 0 else pairs[b - 1, x]

    def one(x, carry):
        seeds[x] = weigh(x, row_sum, weights).astype(jnp.bfloat16)
        return carry

    lax.fori_loop(0, rows, one, 0, unroll=2)
    for i in range(rows // BX):
        span = pl.ds(i * BX, BX)
        here = cells[span].reshape(BX * cols, cohorts).astype(jnp.float32)
        result = establish(seeds[span].reshape(BX * cols, cohorts), here, fecundity, moves)
        grown[span] = result.reshape(BX, cols, cohorts)


def harvest_kernel(slot_table, grown, parts, out, ops, first, last, head, tail, slots, sem):
    slot_copy = pltpu.make_async_copy(slot_table, slots, sem)
    slot_copy.start()
    assemble(parts, ops)
    slot_copy.wait()
    rows, cols, cohorts = grown.shape
    wide = 2 * BY
    for i in range(rows // BX):
        span = pl.ds(i * BX, BX)
        done = []
        for j in range(cols // wide):
            flat = grown[span, pl.ds(j * wide, wide), :].reshape(BX * wide, cohorts)
            done.append(remove_pair(flat, (slots[i, 2 * j], slots[i, 2 * j + 1]), ops))
        whole = jnp.concatenate(done, axis=1)
        out[span] = whole.astype(jnp.bfloat16)
        head[span] = whole[:, :RMAX].astype(jnp.bfloat16)
        tail[span] = whole[:, cols - RMAX :].astype(jnp.bfloat16)
        if i == 0:
            first[...] = whole[:RMAX].astype(jnp.bfloat16)
        if i == rows // BX - 1:
            last[...] = whole[BX - RMAX :].astype(jnp.bfloat16)


def middle_kernel(
    slot_table, cells, top, bottom, weights, fecundity, moves, ops,
    inner, partial, padded, pairs, seeds, slots, sem,
):
    slot_copy = pltpu.make_async_copy(slot_table, slots, sem)
    slot_copy.start()
    rows, cols, cohorts = cells.shape
    fill_rows(cells, top, bottom, padded)
    clear_sides(padded)
    add_pairs(padded, pairs)

    def row_sum(x, b):
        return padded[x, pl.ds(LEAD, cols), :] if b == 0 else pairs[b - 1, x]

    def one(x, carry):
        total = weigh(x, row_sum, weights)
        partial[x] = jnp.concatenate([total[:BY], total[cols - BY :]], axis=0)
        seeds[x] = total[BY : cols - BY].astype(jnp.bfloat16)
        return carry

    lax.fori_loop(0, rows, one, 0, unroll=2)
    slot_copy.wait()
    for i in range(0, rows // BX, 2):
        span = pl.ds(i * BX, 2 * BX)
        here = cells[span].astype(jnp.float32)[:, BY : cols - BY].reshape(-1, cohorts)
        grown = establish(seeds[span].reshape(-1, cohorts), here, fecundity, moves)
        half = grown.shape[0] // 2
        for k in range(2):
            done = remove_pair(
                grown[k * half : (k + 1) * half], (slots[i + k, 1], slots[i + k, 2]), ops
            )
            inner[pl.ds((i + k) * BX, BX)] = done.astype(jnp.bfloat16)


def finish_side(
    lead, block, cells, side, weights, fecundity, moves, ops, partial, write, sides, pairs, seeds,
    slots, slot_copy,
):
    rows, cols, cohorts = cells.shape
    gap = jnp.zeros((BY, cohorts), jnp.float32)
    at = BY - RMAX if lead < 0 else BY

    def place(x, carry):
        sides[x, pl.ds(BY if lead < 0 else 0, BY), :] = gap
        sides[x, pl.ds(at, RMAX), :] = side[x].astype(jnp.float32)
        for b in range(1, RMAX + 1):
            pairs[b - 1, x] = sides[x, pl.ds(BY - b if lead < 0 else b, BY), :]
        return carry

    lax.fori_loop(0, rows + 2 * RMAX, place, 0, unroll=4)

    def row_sum(x, b):
        return None if b == 0 else pairs[b - 1, x]

    first = 0 if lead < 0 else BY

    def one(x, carry):
        seeds[x] = partial[x, pl.ds(first, BY), :] + weigh(x, row_sum, weights)
        return carry

    lax.fori_loop(0, rows, one, 0, unroll=4)
    start = block * BY
    here = cells[...].astype(jnp.float32)[:, start : start + BY].reshape(-1, cohorts)
    arrived = seeds[...].reshape(-1, cohorts).astype(jnp.bfloat16)
    grown = establish(arrived, here, fecundity, moves)
    slot_copy.wait()
    size = BX * BY
    for i in range(rows // BX):
        done = remove(grown[i * size : (i + 1) * size], slots[i, block], ops)
        write(i, done.reshape(BX, BY, cohorts))


def left_kernel(
    slot_table, cells, left, weights, fecundity, moves, ops, partial,
    result, sides, pairs, seeds, slots, sem,
):
    slot_copy = pltpu.make_async_copy(slot_table, slots, sem)
    slot_copy.start()

    def write(i, done):
        result[pl.ds(i * BX, BX)] = done

    finish_side(
        -1, 0, cells, left, weights, fecundity, moves, ops, partial, write, sides, pairs, seeds,
        slots, slot_copy,
    )


def last_kernel(
    slot_table, cells, right, weights, fecundity, moves, ops, partial, before, inner,
    out, sides, pairs, seeds, slots, sem, stage, sems,
):
    rows, cols, _ = cells.shape
    slot_copy = pltpu.make_async_copy(slot_table, slots, sem)
    slot_copy.start()

    def write(i, done):
        at = pl.ds(i * BX, BX)
        whole = jnp.concatenate([before[at], inner[at].astype(jnp.float32), done], axis=1)
        stage[at] = whole.astype(jnp.bfloat16)
        pltpu.make_async_copy(stage.at[at], out.at[at], sems.at[i]).start()

    finish_side(
        1, cols // BY - 1, cells, right, weights, fecundity, moves, ops, partial, write, sides,
        pairs, seeds, slots, slot_copy,
    )
    for i in range(rows // BX):
        at = pl.ds(i * BX, BX)
        pltpu.make_async_copy(stage.at[at], out.at[at], sems.at[i]).wait()


def scratch(rows, cols, cohorts, seeded=None):
    high = rows + 2 * RMAX
    return [
        pltpu.VMEM((high, cols + 2 * LEAD, cohorts), jnp.float32),
        pltpu.VMEM((RMAX, high, cols, cohorts), jnp.float32),
        pltpu.VMEM((rows, seeded or cols, cohorts), jnp.bfloat16),
    ]


def local(
    biomass, block_stand, stand_slot, tile_list, harvest_ops, transition, pattern, fecundity, radius
):
    shape = biomass.shape
    rows, cols, cohorts = shape
    count = tile_list.shape[-1]
    stands = stand_slot.shape[-1]
    state = jax.ShapeDtypeStruct(shape, jnp.bfloat16)
    operators = jax.ShapeDtypeStruct((count, cohorts, cohorts), jnp.bfloat16)

    weights = class_weights(radius)
    block_mask = jnp.repeat(jnp.repeat(pattern, TB, 0), TB, 1).astype(jnp.float32)
    moves = (transition.astype(jnp.float32) * block_mask).astype(jnp.bfloat16)
    stand_hit = block_stand[:, :, None] == jnp.arange(stands)[None, None, :]
    slots = jnp.sum(jnp.where(stand_hit, stand_slot[0, 0][None, None, :], 0), axis=-1)

    parts, around = fetch(tile_list, harvest_ops, biomass, weights, moves)
    grown = pl.pallas_call(
        first_kernel,
        out_shape=state,
        in_specs=[VMEM] * 8,
        out_specs=VMEM,
        scratch_shapes=scratch(*shape),
        compiler_params=PARAMS,
        cost_estimate=pl.CostEstimate(flops=2**28, bytes_accessed=2**24, transcendentals=0),
    )(biomass, *around, weights, fecundity, moves)
    slot_room = [pltpu.SMEM(slots.shape, jnp.int32), pltpu.SemaphoreType.DMA]
    row_part = jax.ShapeDtypeStruct((RMAX, cols, cohorts), jnp.bfloat16)
    col_part = jax.ShapeDtypeStruct((rows, RMAX, cohorts), jnp.bfloat16)
    cells, ops, first, last, head, tail = pl.pallas_call(
        harvest_kernel,
        out_shape=(state, operators, row_part, row_part, col_part, col_part),
        in_specs=[ANY, VMEM, VMEM],
        out_specs=(VMEM,) * 6,
        scratch_shapes=slot_room,
        compiler_params=PARAMS,
        cost_estimate=pl.CostEstimate(flops=2**28, bytes_accessed=2**22, transcendentals=0),
    )(slots, grown, parts)
    top, bottom, left, right = surround(first, last, head, tail)
    high = rows + 2 * RMAX
    outer = 2 * BY
    inner, partial = pl.pallas_call(
        middle_kernel,
        out_shape=(
            jax.ShapeDtypeStruct((rows, cols - outer, cohorts), jnp.bfloat16),
            jax.ShapeDtypeStruct((rows, outer, cohorts), jnp.float32),
        ),
        in_specs=[ANY] + [VMEM] * 7,
        out_specs=(VMEM, VMEM),
        scratch_shapes=scratch(rows, cols, cohorts, cols - outer) + slot_room,
        compiler_params=PARAMS,
        cost_estimate=pl.CostEstimate(flops=2**28, bytes_accessed=2**24, transcendentals=0),
    )(slots, cells, top, bottom, weights, fecundity, moves, ops)
    side_room = [
        pltpu.VMEM((high, outer, cohorts), jnp.float32),
        pltpu.VMEM((RMAX, high, BY, cohorts), jnp.float32),
        pltpu.VMEM((rows, BY, cohorts), jnp.float32),
    ] + slot_room
    before = pl.pallas_call(
        left_kernel,
        out_shape=jax.ShapeDtypeStruct((rows, BY, cohorts), jnp.float32),
        in_specs=[ANY] + [VMEM] * 7,
        out_specs=VMEM,
        scratch_shapes=side_room,
        compiler_params=PARAMS,
        cost_estimate=pl.CostEstimate(flops=2**27, bytes_accessed=2**22, transcendentals=0),
    )(slots, cells, left, weights, fecundity, moves, ops, partial)
    return pl.pallas_call(
        last_kernel,
        out_shape=state,
        in_specs=[ANY] + [VMEM] * 9,
        out_specs=ANY,
        scratch_shapes=side_room
        + [pltpu.VMEM(shape, jnp.bfloat16), pltpu.SemaphoreType.DMA((rows // BX,))],
        compiler_params=PARAMS,
        cost_estimate=pl.CostEstimate(flops=2**28, bytes_accessed=2**22, transcendentals=0),
    )(slots, cells, right, weights, fecundity, moves, ops, partial, before, inner)


def solution(mesh):
    names = tuple(name for name, _ in SPLIT)
    sizes = tuple(size for _, size in SPLIT)
    fine = jax.sharding.Mesh(mesh.devices.reshape(sizes), names)
    placed = (
        P(ROW, COL, None),
        P(ROW, COL),
        P(ROW, COL, None),
        P(ROW, COL, None),
        P(COL, None, None),
        P(),
        P(),
        P(),
        P(),
    )
    return jax.shard_map(
        local, mesh=fine, in_specs=placed, out_specs=P(ROW, COL, None), check_vma=False
    )
```
